256 devices in a mesh: dp: 4 (over y_hi, core), ctx: 64 (over x, z, y_lo).
Axes of the slice: x: 4, y: 4 (y_hi: 2, y_lo: 2; y = y_hi * 2 + y_lo), z: 8, core: 2. Of those that a mesh axis runs over, the one named last changes fastest.
Arguments:
- q_mid: bfloat16 [4, 8192, 1024], P('dp', 'ctx'), may hold values from -160 to 160
- k_mid: bfloat16 [4, 8192, 1024], P('dp', 'ctx'), may hold values from -8 to 8
- v_mid: bfloat16 [4, 8192, 1024], P('dp', 'ctx'), may hold values from -6 to 6
- doc_ids: int32 [4, 8192], P('dp', 'ctx'), may hold values from 0 to 63, never falling along the last dimension, each value on 1 to 512 neighbouring positions
- q_full: bfloat16 [4, 24576, 1024], P('dp', 'ctx'), may hold values from -160 to 160
- k_full: bfloat16 [4, 24576, 1024], P('dp', 'ctx'), may hold values from -8 to 8
- v_base: bfloat16 [4, 24576, 1024], P('dp', 'ctx'), may hold values from -6 to 6
- w_link: bfloat16 [1024, 1024], replicated, may hold values from -0.1875 to 0.1875
- cotangent: bfloat16 [4, 24576, 1024], P('dp', 'ctx'), may hold values from -6 to 6
Outputs:
- grad_q_mid: bfloat16 [4, 8192, 1024], P('dp', 'ctx')
- grad_k_mid: bfloat16 [4, 8192, 1024], P('dp', 'ctx')
- grad_v_mid: bfloat16 [4, 8192, 1024], P('dp', 'ctx')
- grad_q_full: bfloat16 [4, 24576, 1024], P('dp', 'ctx')
- grad_k_full: bfloat16 [4, 24576, 1024], P('dp', 'ctx')
- grad_v_full: bfloat16 [4, 24576, 1024], P('dp', 'ctx')
- grad_link: float32 [1024, 1024], P('ctx')
The draws below stay inside these ranges and needn't reach their ends.
Inputs may be any that keep to these rules, and one draw needn't show every extreme that they name: `doc_ids`: ids never fall along a sequence; every document holds 1 to 512 positions, and one holds exactly 512.
All inputs are finite; a program needn't handle non-finite values.
Results may differ from the reference program's by a relative error of at most 0.012.
Values may be sent and summed in bfloat16 or wider, within the bound.
No kernel may reach another device: no remote copies, remote signals or barrier semaphores. Data moves between devices by JAX's collectives and lax.ppermute only.
A program may use at most 192 MiB of HBM per device.

```python
import math
import jax
import jax.numpy as jnp
import numpy as np
from jax import lax

H = 8
E = 128
HE = 1024
S_DEV = 128
F_DEV = 384
SPAN = 4
FULL_REACH = 2
WIN = 768
MOST = 512
DOCS = 64
NS = 8192
NF = 24576
BATCH = 4
N_CTX = 64


def aligned_pair(key, tag, rows):
    shape = (BATCH, rows, H * E)
    keys_arr = jnp.clip(jax.random.normal(jax.random.fold_in(key, tag), shape, jnp.float32), -6.0, 6.0)
    queries = jnp.clip(jax.random.normal(jax.random.fold_in(key, tag + 1), shape, jnp.float32), -6.0, 6.0)
    position = jnp.arange(rows) % 61
    marked = (position == 37)[None, :, None]
    before = (position == 36)[None, :, None]
    keys_arr = jnp.where(before, keys_arr, keys_arr)
    queries = jnp.where(marked, queries, queries)
    return (queries, keys_arr)


def draw_q_mid(key, part):
    return aligned_pair(key, 11, NS)[0].astype(jnp.bfloat16)


def draw_k_mid(key, part):
    return aligned_pair(key, 11, NS)[1].astype(jnp.bfloat16)


def draw_q_full(key, part):
    return aligned_pair(key, 21, NF)[0].astype(jnp.bfloat16)


def draw_k_full(key, part):
    return aligned_pair(key, 21, NF)[1].astype(jnp.bfloat16)


def steps_of(stream_key, dims, pieces, smallest, top_value):
    level = 1.0
    for dim, shards_of in pieces:
        draws = jax.random.uniform(jax.random.fold_in(jax.random.fold_in(stream_key, 6), dim), (shards_of,), jnp.float32, smallest / len(pieces), top_value / len(pieces))
        level = level * jnp.repeat(jnp.exp(draws), dims[dim] // shards_of).reshape((-1,) + (1,) * (len(dims) - 1 - dim))
    return level


def length_profile(count, total, most, skew):
    loads = [(1 << 20) // math.isqrt(grade ** skew) + 1 for grade in range(2, count + 1)]
    surplus, holding = total - most - (count - 1), [1] * (count - 1)
    while surplus > 0:
        free = [i for i in range(count - 1) if holding[i] < most]
        mass, remaining = sum([loads[i] for i in free]), surplus
        for i in free:
            extra = min(most - holding[i], max(1, remaining * loads[i] // mass), surplus)
            holding[i] = holding[i] + extra
            surplus = surplus - extra
    return np.array([most] + holding)


def uneven_parts(rng, number_of, total, most, skew):
    if number_of == 2:
        one = jax.random.randint(rng, (), max(1, total - most), min(most, total - 1) + 1)
        return jnp.stack([one, total - one])
    sizes = jnp.asarray(length_profile(number_of, total, most, skew), jnp.int32)
    couples = (number_of - 1) // 2
    donor, sink = sizes[1:1 + 2 * couples:2], sizes[2:2 + 2 * couples:2]
    slack = jnp.minimum(donor - 1, most - sink)
    moved = jax.random.randint(jax.random.fold_in(rng, 1), (couples,), 0, 1 << 20) % (slack + 1)
    sizes = sizes.at[1:1 + 2 * couples:2].set(donor - moved).at[2:2 + 2 * couples:2].set(sink + moved)
    return sizes[jax.random.permutation(jax.random.fold_in(rng, 2), number_of)]


def gaussian(rng, shape, scale, bound, split=(), held_as=jnp.bfloat16):
    level = steps_of(rng, shape, split, -0.22, 0.18) if split else 1.0
    result = jax.random.normal(rng, shape, jnp.float32) * scale * level
    return jnp.minimum(jnp.maximum(result, -bound), bound).astype(held_as)


def setup_inputs(seed: int = 0) -> dict:
    key_list = jax.random.split(jax.random.key(seed), 10)
    q_mid = draw_q_mid(jax.random.fold_in(key_list[9], 71), 0)
    k_mid = draw_k_mid(jax.random.fold_in(key_list[9], 71), 0)
    v_mid = gaussian(key_list[2], (BATCH, NS, HE), 1.0, 6.0, ((0, 4), (1, 64)))
    doc_ids = jax.vmap(lambda own: jnp.searchsorted(jnp.cumsum(uneven_parts(own, DOCS, NS, MOST, 2)), jnp.arange(NS), side="right"))(jax.random.split(key_list[3], BATCH)).reshape((BATCH, NS)).astype(jnp.int32)
    q_full = draw_q_full(jax.random.fold_in(key_list[9], 71), 0)
    k_full = draw_k_full(jax.random.fold_in(key_list[9], 71), 0)
    v_base = gaussian(key_list[6], (BATCH, NF, HE), 1.0, 6.0, ((0, 4), (1, 64)))
    w_link = gaussian(key_list[7], (HE, HE), HE ** -0.5, 0.1875)
    cotangent = gaussian(key_list[8], (BATCH, NF, HE), 1.0, 6.0, ((0, 4), (1, 64)))
    return {"q_mid": q_mid, "k_mid": k_mid, "v_mid": v_mid, "doc_ids": doc_ids, "q_full": q_full, "k_full": k_full, "v_base": v_base, "w_link": w_link, "cotangent": cotangent}


def split_heads(rows):
    return rows.reshape(rows.shape[0], H, E).astype(jnp.float32)


def rounded(values):
    return lax.optimization_barrier(values.astype(jnp.bfloat16)).astype(jnp.float32)


def attend(queries, keys, values, allowed):
    scores = jnp.einsum("qhe,khe->hqk", split_heads(queries), split_heads(keys)) * (E ** -0.5)
    scores = jnp.where(allowed[None], scores, -jnp.inf)
    peak = jnp.max(scores, axis=2, keepdims=True)
    expo = jnp.exp(scores - peak)
    probs = expo / jnp.sum(expo, axis=2, keepdims=True)
    weights = rounded(probs)
    attended = jnp.einsum("hqk,khe->qhe", weights, split_heads(values))
    return attended.reshape(queries.shape[0], H * E), probs, weights


def attend_back(probs, weights, cot, attended, queries, keys, values):
    cot_heads = split_heads(cot)
    dots = jnp.einsum("qhe,khe->hqk", cot_heads, split_heads(values))
    delta = jnp.transpose(jnp.sum(cot_heads * attended.reshape(attended.shape[0], H, E), axis=2))[:, :, None]
    grads = rounded(probs * (dots - delta))
    grad_q = jnp.einsum("hqk,khe->qhe", grads, split_heads(keys)) * (E ** -0.5)
    grad_k = jnp.einsum("hqk,qhe->khe", grads, split_heads(queries)) * (E ** -0.5)
    grad_v = jnp.einsum("hqk,qhe->khe", weights, cot_heads)
    width = H * E
    return grad_q.reshape(-1, width), grad_k.reshape(-1, width), grad_v.reshape(-1, width)


def pad_front(array, count, fill):
    lead = jnp.full((count,) + array.shape[1:], fill, array.dtype)
    return jnp.concatenate([lead, array], axis=0)


def round_remote(grad_rows, lead):
    return jnp.concatenate([rounded(grad_rows[:lead]), grad_rows[lead:]], axis=0)


def window_inputs(first, rows, reach, queries, keys_pad, values_pad, docs, docs_pad, limit):
    span = (reach + 1) * rows
    q_rows = lax.dynamic_slice_in_dim(queries, first, rows, 0)
    k_rows = lax.dynamic_slice_in_dim(keys_pad, first, span, 0)
    v_rows = lax.dynamic_slice_in_dim(values_pad, first, span, 0)
    q_docs = lax.dynamic_slice_in_dim(docs, first, rows, 0)
    k_docs = lax.dynamic_slice_in_dim(docs_pad, first, span, 0)
    q_pos = first + jnp.arange(rows, dtype=jnp.int32)
    k_pos = first - reach * rows + jnp.arange(span, dtype=jnp.int32)
    gap = q_pos[:, None] - k_pos[None, :]
    allowed = (k_pos[None, :] >= 0) & (gap >= 0) & (gap < limit) & (k_docs[None, :] == q_docs[:, None])
    return q_rows, k_rows, v_rows, allowed


def one_sequence(q_mid, k_mid, v_mid, docs, q_full, k_full, v_base, w_link, cotangent):
    width = H * E
    blocks = jnp.arange(N_CTX, dtype=jnp.int32)
    mid_lead = SPAN * S_DEV
    mid_span = (SPAN + 1) * S_DEV
    k_mid_pad = pad_front(k_mid, mid_lead, 0)
    v_mid_pad = pad_front(v_mid, mid_lead, 0)
    docs_pad = pad_front(docs, mid_lead, -1)

    def mid_inputs(block):
        first = (block * S_DEV).astype(jnp.int32)
        return window_inputs(first, S_DEV, SPAN, q_mid, k_mid_pad, v_mid_pad, docs, docs_pad, mid_span)

    mid_attended = lax.map(lambda block: attend(*mid_inputs(block))[0], blocks).reshape(NS, width)
    mid_out = mid_attended.astype(jnp.bfloat16)
    upsampled = jnp.concatenate([jnp.zeros((2, width), jnp.bfloat16), jnp.repeat(mid_out, 3, axis=0)[:NF - 2]], axis=0)
    values_full = (v_base.astype(jnp.float32) + jnp.dot(upsampled, w_link, preferred_element_type=jnp.float32)).astype(jnp.bfloat16)

    full_lead = FULL_REACH * F_DEV
    full_span = (FULL_REACH + 1) * F_DEV
    k_full_pad = pad_front(k_full, full_lead, 0)
    v_full_pad = pad_front(values_full, full_lead, 0)
    docs_full = jnp.repeat(docs, 3)
    docs_full_pad = pad_front(docs_full, full_lead, -1)

    def full_step(carry, block):
        acc_k, acc_v = carry
        first = (block * F_DEV).astype(jnp.int32)
        q_rows, k_rows, v_rows, allowed = window_inputs(first, F_DEV, FULL_REACH, q_full, k_full_pad, v_full_pad, docs_full, docs_full_pad, WIN)
        cot_rows = lax.dynamic_slice_in_dim(cotangent, first, F_DEV, 0)
        attended, probs, weights = attend(q_rows, k_rows, v_rows, allowed)
        grad_q, grad_k, grad_v = attend_back(probs, weights, cot_rows, attended, q_rows, k_rows, v_rows)
        grad_k = round_remote(grad_k, full_lead)
        grad_v = round_remote(grad_v, full_lead)
        acc_k = lax.dynamic_update_slice_in_dim(acc_k, lax.dynamic_slice_in_dim(acc_k, first, full_span, 0) + grad_k, first, 0)
        acc_v = lax.dynamic_update_slice_in_dim(acc_v, lax.dynamic_slice_in_dim(acc_v, first, full_span, 0) + grad_v, first, 0)
        return (acc_k, acc_v), grad_q.astype(jnp.bfloat16)

    full_zero = jnp.zeros((NF + full_lead, width), jnp.float32)
    (acc_k, acc_v), grad_q_full = lax.scan(full_step, (full_zero, full_zero), blocks)
    grad_q_full = grad_q_full.reshape(NF, width)
    grad_k_full = acc_k[full_lead:].astype(jnp.bfloat16)
    grad_v_full = acc_v[full_lead:].astype(jnp.bfloat16)
    link_term = jnp.dot(upsampled.T, grad_v_full, preferred_element_type=jnp.float32)
    up_grads = jnp.dot(grad_v_full, w_link.T, preferred_element_type=jnp.float32)
    stacked = jnp.concatenate([up_grads[2:], jnp.zeros((2, width), jnp.float32)], axis=0)
    mid_out_grads = jnp.sum(stacked.reshape(NS, 3, width), axis=1).astype(jnp.bfloat16)

    def mid_step(carry, block):
        acc_k, acc_v = carry
        first = (block * S_DEV).astype(jnp.int32)
        q_rows, k_rows, v_rows, allowed = mid_inputs(block)
        cot_rows = lax.dynamic_slice_in_dim(mid_out_grads, first, S_DEV, 0)
        attended, probs, weights = attend(q_rows, k_rows, v_rows, allowed)
        grad_q, grad_k, grad_v = attend_back(probs, weights, cot_rows, attended, q_rows, k_rows, v_rows)
        grad_k = round_remote(grad_k, mid_lead)
        grad_v = round_remote(grad_v, mid_lead)
        acc_k = lax.dynamic_update_slice_in_dim(acc_k, lax.dynamic_slice_in_dim(acc_k, first, mid_span, 0) + grad_k, first, 0)
        acc_v = lax.dynamic_update_slice_in_dim(acc_v, lax.dynamic_slice_in_dim(acc_v, first, mid_span, 0) + grad_v, first, 0)
        return (acc_k, acc_v), grad_q.astype(jnp.bfloat16)

    mid_zero = jnp.zeros((NS + mid_lead, width), jnp.float32)
    (mid_k, mid_v), grad_q_mid = lax.scan(mid_step, (mid_zero, mid_zero), blocks)
    grad_q_mid = grad_q_mid.reshape(NS, width)
    grad_k_mid = mid_k[mid_lead:].astype(jnp.bfloat16)
    grad_v_mid = mid_v[mid_lead:].astype(jnp.bfloat16)
    return grad_q_mid, grad_k_mid, grad_v_mid, grad_q_full, grad_k_full, grad_v_full, link_term


def reference(q_mid, k_mid, v_mid, doc_ids, q_full, k_full, v_base, w_link, cotangent):
    results = []
    for index in range(BATCH):
        results.append(one_sequence(q_mid[index], k_mid[index], v_mid[index], doc_ids[index], q_full[index], k_full[index], v_base[index], w_link, cotangent[index]))
    link_total = results[0][6]
    for index in range(1, BATCH):
        link_total = link_total + results[index][6]
    grad_link = link_total * ((BATCH * NF) ** -0.5)
    return (jnp.stack([item[0] for item in results]), jnp.stack([item[1] for item in results]), jnp.stack([item[2] for item in results]), jnp.stack([item[3] for item in results]), jnp.stack([item[4] for item in results]), jnp.stack([item[5] for item in results]), grad_link)
```

```python
import math

import jax
import jax.numpy as jnp
from jax import lax
from jax.experimental import pallas as pl
from jax.experimental.pallas import tpu as pltpu
from jax.sharding import PartitionSpec as P

H = 8
E = 128
S = 128
F = 384
REACH = 4
FREACH = 2
WIDTH = H * E
SPAN_M = (REACH + 1) * S
SPAN_F = (FREACH + 1) * F
WIN = FREACH * F
TILES = F // S
TILE_W = WIN + S
SCALE = E ** (-0.5)
LOG2 = SCALE * math.log2(math.e)
NEG = -1e30
F32 = jnp.float32
BF16 = jnp.bfloat16
PARAMS = pltpu.CompilerParams(vmem_limit_bytes=48 * 1024 * 1024)


def dot_nn(a, b):
    return lax.dot_general(a, b, (((1,), (0,)), ((), ())), preferred_element_type=F32)


def dot_nt(a, b):
    return lax.dot_general(a, b, (((1,), (1,)), ((), ())), preferred_element_type=F32)


def dot_tn(a, b):
    return lax.dot_general(a, b, (((0,), (0,)), ((), ())), preferred_element_type=F32)


def iota(shape, axis):
    return lax.broadcasted_iota(jnp.int32, shape, axis)


def to_column(row, size):
    return jnp.transpose(jnp.broadcast_to(row, (size, size)))


def split3(x):
    hi = x.astype(BF16)
    rest = x - hi.astype(F32)
    mid = rest.astype(BF16)
    return hi, mid, (rest - mid.astype(F32)).astype(BF16)


def head_spec(rows):
    return pl.BlockSpec((rows, E), lambda h: (0, h))


def whole_spec(shape):
    return pl.BlockSpec(shape, lambda h: (0,) * len(shape))


def mid_fwd_body(q, p4, p3, p2, p1, p0, out, att, stat, bias):
    pays = (p4, p3, p2, p1, p0)

    @pl.when(pl.program_id(0) == 0)
    def _():
        mine = to_column(p0[2 * S : 2 * S + 16, :].astype(F32)[0:1], S)
        for n, pay in enumerate(pays):
            ok = mine == pay[2 * S : 2 * S + 16, :].astype(F32)[0:1]
            if n == REACH:
                ok = ok & (iota((S, S), 0) >= iota((S, S), 1))
            bias[:, n * S : (n + 1) * S] = jnp.where(ok, 0.0, NEG)

    keys = jnp.concatenate([pay[0:S, :] for pay in pays], axis=0)
    values = jnp.concatenate([pay[S : 2 * S, :] for pay in pays], axis=0)
    scores = dot_nt(q[...], keys) * LOG2 + bias[...]
    peak = jnp.max(scores, axis=1, keepdims=True)
    expo = jnp.exp2(scores - peak)
    inv = 1.0 / jnp.sum(expo, axis=1, keepdims=True)
    attended = dot_nn((expo * inv).astype(BF16), values)
    att[...] = attended
    out[...] = attended.astype(BF16)
    stat[0:1, :] = jnp.transpose(jnp.broadcast_to(peak, (S, S)))[0:1]
    stat[1:2, :] = jnp.transpose(jnp.broadcast_to(inv, (S, S)))[0:1]
    stat[2:8, :] = jnp.zeros((6, S), F32)


def mid_forward(q, pays):
    return pl.pallas_call(
        mid_fwd_body,
        grid=(H,),
        in_specs=[head_spec(S)] + [head_spec(2 * S + 16)] * 5,
        out_specs=[head_spec(S), head_spec(S), head_spec(8)],
        out_shape=[
            jax.ShapeDtypeStruct((S, WIDTH), BF16),
            jax.ShapeDtypeStruct((S, WIDTH), F32),
            jax.ShapeDtypeStruct((8, WIDTH), F32),
        ],
        scratch_shapes=[pltpu.VMEM((S, SPAN_M), F32)],
        compiler_params=PARAMS,
        cost_estimate=pl.CostEstimate(flops=700_000_000, bytes_accessed=4_000_000, transcendentals=0),
        name="mid_forward",
    )(q, *pays)


def full_mask(bias, docs, own_rows):
    spread = (iota((S, F), 1) // 3 == iota((S, F), 0)).astype(BF16)
    spread_t = (iota((F, S), 0) // 3 == iota((F, S), 1)).astype(BF16)
    rows = jnp.concatenate(
        [dot_nn(jnp.broadcast_to(d, (16, S)), spread)[0:1] for d in docs], axis=1
    )
    column = dot_nn(spread_t, to_column(own_rows.astype(F32), S).astype(BF16))
    for t in range(TILES):
        lo = t * S
        mine = jnp.concatenate([column[lo : lo + S]] * (TILE_W // S), axis=1)
        gap = iota((S, TILE_W), 1) - iota((S, TILE_W), 0)
        ok = (mine == rows[:, lo : lo + TILE_W]) & (gap >= 0) & (gap < WIN)
        bias[t] = jnp.where(ok, 0.0, NEG)


def doc_row(ref):
    return ref[S : S + 16, :][0:1]


def stats_body(k, base, mid, edge, w, q0, q1, q2, c0, c1, c2, m0, m1, m2, values, s0, s1, s2, bias, ext, part):
    head = pl.program_id(0)

    @pl.when(head == 0)
    def _():
        docs = [doc_row(ref) for ref in (m0, m1, m2)]
        full_mask(bias, docs, docs[0])
        for t in range(TILES):
            part[t, 0:H, :] = jnp.full((H, SPAN_F), NEG, F32)
            part[t, H : 3 * H, :] = jnp.zeros((2 * H, SPAN_F), F32)

    linked = dot_nn(mid[...], w[...])
    for n in range(2, 5):
        ext[pl.ds(n, S, stride=3), :] = linked
    ext[0:2, :] = jnp.broadcast_to(dot_nn(edge[...], w[...])[15:16], (2, E))
    v = (base[...].astype(F32) + ext[0:F, :]).astype(BF16)
    values[...] = v
    queries = jnp.concatenate([q0[...], q1[...], q2[...]], axis=0)
    cots = jnp.concatenate([c0[...], c1[...], c2[...]], axis=0)
    for t in range(TILES):
        lo = t * S
        scores = dot_nt(k[lo : lo + S, :], queries[lo : lo + TILE_W]) * LOG2 + bias[t]
        peak = jnp.max(scores, axis=0, keepdims=True)
        expo = jnp.exp2(scores - peak)
        dots = dot_nt(v[lo : lo + S], cots[lo : lo + TILE_W])
        part[t, pl.ds(head, 1), lo : lo + TILE_W] = peak
        part[t, pl.ds(H + head, 1), lo : lo + TILE_W] = jnp.sum(expo, axis=0, keepdims=True)
        part[t, pl.ds(2 * H + head, 1), lo : lo + TILE_W] = jnp.sum(expo * dots, axis=0, keepdims=True)

    @pl.when(head == H - 1)
    def _():
        for n, out in enumerate((s0, s1, s2)):
            cols = slice(n * F, (n + 1) * F)
            merged = merge([(part[t, 0:H, cols], part[t, H : 2 * H, cols], part[t, 2 * H : 3 * H, cols]) for t in range(TILES)])
            for j in range(3):
                out[j * H : (j + 1) * H, :] = merged[j]


def merge(parts):
    peak = parts[0][0]
    for part in parts[1:]:
        peak = jnp.maximum(peak, part[0])
    total, dots = 0.0, 0.0
    for part in parts:
        factor = jnp.exp2(part[0] - peak)
        total = total + part[1] * factor
        dots = dots + part[2] * factor
    return peak, total, dots


def full_stats(k, base, mid, edge, w, qs, cs, ms):
    stat = jax.ShapeDtypeStruct((3 * H, F), F32)
    return pl.pallas_call(
        stats_body,
        grid=(H,),
        in_specs=[head_spec(F), head_spec(F), whole_spec((S, WIDTH)), whole_spec((16, WIDTH)), head_spec(WIDTH)]
        + [head_spec(F)] * 6
        + [pl.BlockSpec((S + 16, E), lambda h: (0, 0))] * 3,
        out_specs=[head_spec(F)] + [whole_spec((3 * H, F))] * 3,
        out_shape=[jax.ShapeDtypeStruct((F, WIDTH), BF16), stat, stat, stat],
        scratch_shapes=[
            pltpu.VMEM((TILES, S, TILE_W), F32),
            pltpu.VMEM((400, E), F32),
            pltpu.VMEM((TILES, 3 * H, SPAN_F), F32),
        ],
        compiler_params=PARAMS,
        cost_estimate=pl.CostEstimate(flops=3_000_000_000, bytes_accessed=10_000_000, transcendentals=0),
        name="full_stats",
    )(k, base, mid, edge, w, *qs, *cs, *ms)


def grads_body(
    k, v, q0, q1, q2, c0, c1, c2, m0, m1, m2, s0, s1, s2, up1, up2, down1, down2,
    dk, dv, dq0, dq1, dq2, sums, link, tail, bias, ext, glob, kept,
):
    head = pl.program_id(0)

    @pl.when(head == 0)
    def _():
        docs = [doc_row(ref) for ref in (m0, m1, m2)]
        full_mask(bias, docs, docs[0])

        def triple(ref, base):
            peak, total, dots = (ref[base + j * H : base + (j + 1) * H, :] for j in range(3))
            return jnp.where(total > 0.0, peak, NEG), total, dots

        groups = (
            [triple(s0, 0), triple(up1, 0), triple(up2, 0)],
            [triple(s1, 0), triple(up1, 3 * H), triple(down1, 0)],
            [triple(s2, 0), triple(down1, 3 * H), triple(down2, 0)],
        )
        for n, group in enumerate(groups):
            cols = slice(n * F, (n + 1) * F)
            peak, total, dots = merge(group)
            inv = jnp.where(total > 0.0, 1.0 / total, 0.0)
            glob[0:H, cols] = peak
            glob[H : 2 * H, cols] = inv
            glob[2 * H : 3 * H, cols] = dots * inv
        kept[...] = jnp.zeros((F, SPAN_F), BF16)
        ext[F:400, :] = jnp.zeros((400 - F, E), F32)

    queries = jnp.concatenate([q0[...], q1[...], q2[...]], axis=0)
    cots = jnp.concatenate([c0[...], c1[...], c2[...]], axis=0)
    for t in range(TILES):
        lo = t * S
        cols = slice(lo, lo + TILE_W)
        scores = dot_nt(k[lo : lo + S, :], queries[cols]) * LOG2 + bias[t]
        probs = jnp.exp2(scores - glob[pl.ds(head, 1), cols]) * glob[pl.ds(H + head, 1), cols]
        dots = dot_nt(v[lo : lo + S, :], cots[cols])
        grads = (probs * (dots - glob[pl.ds(2 * H + head, 1), cols])).astype(BF16)
        kept[lo : lo + S, cols] = grads
        dk[lo : lo + S, :] = (dot_nn(grads, queries[cols]) * SCALE).astype(BF16)
        grad_v = dot_nn(probs.astype(BF16), cots[cols]).astype(BF16)
        dv[lo : lo + S, :] = grad_v
        ext[lo : lo + S, :] = grad_v.astype(F32)
    for n, out in enumerate((dq0, dq1, dq2)):
        part = dot_tn(kept[:, n * F : (n + 1) * F], k[...]) * SCALE
        out[...] = part.astype(out.dtype)
    total = ext[pl.ds(2, S, stride=3), :] + ext[pl.ds(3, S, stride=3), :] + ext[pl.ds(4, S, stride=3), :]
    sums[...] = total
    first = ext[0:1, :] + ext[1:2, :]
    tail[...] = jnp.broadcast_to(first, (8, E))
    link[0:S, :] = total.astype(BF16)
    link[S : S + 16, :] = jnp.where(iota((16, E), 0) == 15, first, 0.0).astype(BF16)


def full_grads(k, v, qs, cs, ms, stats):
    return pl.pallas_call(
        grads_body,
        grid=(H,),
        in_specs=[head_spec(F), head_spec(F)]
        + [head_spec(F)] * 6
        + [pl.BlockSpec((S + 16, E), lambda h: (0, 0))] * 3
        + [whole_spec(s.shape) for s in stats],
        out_specs=[head_spec(F)] * 5 + [head_spec(S), head_spec(S + 16), head_spec(8)],
        out_shape=[
            jax.ShapeDtypeStruct((F, WIDTH), BF16),
            jax.ShapeDtypeStruct((F, WIDTH), BF16),
            jax.ShapeDtypeStruct((F, WIDTH), F32),
            jax.ShapeDtypeStruct((F, WIDTH), BF16),
            jax.ShapeDtypeStruct((F, WIDTH), BF16),
            jax.ShapeDtypeStruct((S, WIDTH), F32),
            jax.ShapeDtypeStruct((S + 16, WIDTH), BF16),
            jax.ShapeDtypeStruct((8, WIDTH), F32),
        ],
        scratch_shapes=[
            pltpu.VMEM((TILES, S, TILE_W), F32),
            pltpu.VMEM((400, E), F32),
            pltpu.VMEM((3 * H, SPAN_F), F32),
            pltpu.VMEM((F, SPAN_F), BF16),
        ],
        compiler_params=PARAMS,
        cost_estimate=pl.CostEstimate(flops=8_000_000_000, bytes_accessed=14_000_000, transcendentals=0),
        name="full_grads",
    )(k, v, *qs, *cs, *ms, *stats)


def mid_cot_body(sums, tail, w, att, stat, out):
    total = sums[...] + jnp.where(iota((S, WIDTH), 0) == S - 1, tail[0:1, :], 0.0)
    grad = dot_nt(total.astype(BF16), w[...]).astype(BF16)
    out[0:S, :] = grad
    weighed = grad.astype(F32) * att[...]
    for h in range(H):
        cols = slice(h * E, (h + 1) * E)
        delta = jnp.sum(jnp.transpose(weighed[:, cols]), axis=0, keepdims=True)
        rows = [*split3(stat[0:1, cols]), *split3(stat[1:2, cols]), *split3(delta)]
        rows = [row.astype(F32) for row in rows] + [jnp.zeros((7, E), F32)]
        out[S : S + 16, cols] = jnp.concatenate(rows, axis=0).astype(BF16)


def mid_cotangent(sums, tail, w, att, stat):
    return pl.pallas_call(
        mid_cot_body,
        out_shape=jax.ShapeDtypeStruct((S + 16, WIDTH), BF16),
        compiler_params=PARAMS,
        cost_estimate=pl.CostEstimate(flops=600_000_000, bytes_accessed=4_000_000, transcendentals=0),
        name="mid_cotangent",
    )(sums, tail, w, att, stat)


def mid_bwd_body(*refs):
    p4, p3, p2, p1, p0 = refs[0:5]
    ms = refs[5:10]
    gs = refs[10:15]
    dq, dk, dv, back, fore = refs[15:]
    pays = (p4, p3, p2, p1, p0)

    @pl.when(pl.program_id(0) == 0)
    def _():
        mine = p0[2 * S : 2 * S + 16, :].astype(F32)[0:1]
        column = to_column(mine, S)
        causal = iota((S, S), 1) >= iota((S, S), 0)
        for n, pay in enumerate(pays):
            ok = to_column(pay[2 * S : 2 * S + 16, :].astype(F32)[0:1], S) == mine
            if n == REACH:
                ok = ok & causal
            back[n * S : (n + 1) * S, :] = jnp.where(ok, 0.0, NEG)
        for n, pay in enumerate(ms):
            ok = column == doc_row(pay).astype(F32)
            if n == 0:
                ok = ok & causal
            fore[:, n * S : (n + 1) * S] = jnp.where(ok, 0.0, NEG)

    def stats(ref):
        rows = ref[S : S + 16, :].astype(F32)
        return [rows[j : j + 1] + rows[j + 1 : j + 2] + rows[j + 2 : j + 3] for j in (0, 3, 6)]

    k = p0[0:S, :]
    v = p0[S : 2 * S, :]
    keys = jnp.concatenate([pay[0:S, :] for pay in pays], axis=0)
    values = jnp.concatenate([pay[S : 2 * S, :] for pay in pays], axis=0)
    peak, inv, delta = stats(gs[0])
    scores = dot_nt(keys, ms[0][0:S, :]) * LOG2 + back[...]
    probs = jnp.exp2(scores - peak) * inv
    grads = (probs * (dot_nt(values, gs[0][0:S, :]) - delta)).astype(BF16)
    dq[...] = (dot_tn(grads, keys) * SCALE).astype(BF16)
    queries = jnp.concatenate([ref[0:S, :] for ref in ms], axis=0)
    cots = jnp.concatenate([ref[0:S, :] for ref in gs], axis=0)
    every = [stats(ref) for ref in gs]
    peak, inv, delta = (jnp.concatenate([one[j] for one in every], axis=1) for j in range(3))
    scores = dot_nt(k, queries) * LOG2 + fore[...]
    probs = jnp.exp2(scores - peak) * inv
    grads = (probs * (dot_nt(v, cots) - delta)).astype(BF16)
    dk[...] = (dot_nn(grads, queries) * SCALE).astype(BF16)
    dv[...] = dot_nn(probs.astype(BF16), cots).astype(BF16)


def mid_backward(pays, ms, gs):
    return pl.pallas_call(
        mid_bwd_body,
        grid=(H,),
        in_specs=[head_spec(2 * S + 16)] * 5 + [head_spec(S + 16)] * 10,
        out_specs=[head_spec(S)] * 3,
        out_shape=[jax.ShapeDtypeStruct((S, WIDTH), BF16)] * 3,
        scratch_shapes=[pltpu.VMEM((SPAN_M, S), F32), pltpu.VMEM((S, SPAN_M), F32)],
        compiler_params=PARAMS,
        cost_estimate=pl.CostEstimate(flops=3_000_000_000, bytes_accessed=6_000_000, transcendentals=0),
        name="mid_backward",
    )(*pays, *ms, *gs)


def shift(value, steps):
    count = lax.axis_size("ctx")
    first, last = max(0, -steps), min(count, count - steps)
    return lax.ppermute(value, "ctx", [(n, n + steps) for n in range(first, last)])


def swap(value, axis, bit):
    count = lax.axis_size(axis)
    return lax.ppermute(value, axis, [(n, n ^ bit) for n in range(count)])


def halves(value, high, axis):
    low, up = jnp.split(value, 2, axis=axis)
    return jnp.where(high, up, low), jnp.where(high, low, up)


def link_gradient(mid_ext, sum_ext, place):
    core = lax.axis_index("dp") % 2 == 1
    x = place // 16
    z = place // 2 % 8
    other_mid = swap(mid_ext, "dp", 1)
    keep, send = halves(sum_ext, core, 1)
    left = jnp.concatenate([mid_ext, other_mid], axis=0)
    right = jnp.concatenate([keep, swap(send, "dp", 1)], axis=0)
    term = dot_tn(left, right)
    blocks = term.reshape(4, 256, 512)
    outer = jnp.stack([blocks[0], blocks[3]])
    inner = jnp.stack([blocks[1], blocks[2]])
    is_outer = (x == 0) | (x == 3)
    keep = jnp.where(is_outer, outer, inner)
    send = jnp.where(is_outer, inner, outer).astype(BF16)
    got = lax.ppermute(send, "ctx", [(n, n ^ 16) for n in range(64)])
    term = keep + got.astype(F32)
    high = x >= 2
    keep = jnp.where(high, term[1], term[0])
    send = jnp.where(high, term[0], term[1]).astype(BF16)
    got = lax.ppermute(send, "ctx", [(n, n ^ 48) for n in range(64)])
    term = keep + got.astype(F32)
    for bit in (4, 2, 1):
        keep, send = halves(term, z & bit != 0, 0)
        term = keep + swap(send.astype(BF16), "ctx", 2 * bit).astype(F32)
    keep, send = halves(term, place % 2 == 1, 0)
    term = keep + swap(send, "ctx", 1)
    term = term + swap(term, "dp", 2)
    other = swap(term, "dp", 1)
    return jnp.concatenate([jnp.where(core, other, term), jnp.where(core, term, other)], axis=1)


def shards(q_mid, k_mid, v_mid, doc_ids, q_full, k_full, v_base, w_link, cotangent):
    place = lax.axis_index("ctx")
    upper = place % 2 == 1
    q_m, q_f, k_f, cot = q_mid[0], q_full[0], k_full[0], cotangent[0]
    ids = jnp.broadcast_to(jnp.tile((doc_ids + 1).astype(BF16), (1, H)), (16, WIDTH))
    own_kv = jnp.concatenate([k_mid[0], v_mid[0], ids], axis=0)
    own_q = jnp.concatenate([q_m, ids], axis=0)

    kv2 = shift(own_kv, 2)
    kv1 = swap(jnp.where(upper, kv2, own_kv), "ctx", 1)
    kv4 = shift(kv2, 2)
    kv3 = swap(jnp.where(upper, kv4, kv2), "ctx", 1)

    qf2 = shift(q_f, -2)
    qf1 = swap(jnp.where(upper, q_f, qf2), "ctx", 1)
    cf2 = shift(cot, -2)
    cf1 = swap(jnp.where(upper, cot, cf2), "ctx", 1)
    qm2 = shift(own_q, -2)
    qm1 = swap(jnp.where(upper, own_q, qm2), "ctx", 1)
    qm4 = shift(qm2, -2)
    qm3 = swap(jnp.where(upper, qm2, qm4), "ctx", 1)

    pays = (kv4, kv3, kv2, kv1, own_kv)
    mid_out, attended, mid_stat = mid_forward(q_m, pays)
    edge = shift(mid_out[S - 16 :], 1)

    qs, cs, ms = (q_f, qf1, qf2), (cot, cf1, cf2), (own_q, qm1, qm2)
    values, s0, s1, s2 = full_stats(k_f, v_base[0], mid_out, edge, w_link, qs, cs, ms)
    up1 = shift(jnp.concatenate([s1, s2], axis=0), 1)
    up2 = shift(s2, 2)
    down1 = shift(jnp.concatenate([s0, s1], axis=0), -1)
    down2 = shift(s0, -2)
    dk_f, dv_f, dq0, dq1, dq2, sums, sum_ext, tail = full_grads(
        k_f, values, qs, cs, ms, (s0, s1, s2, up1, up2, down1, down2)
    )

    cot_m = mid_cotangent(sums, shift(tail, -1), w_link, attended, mid_stat)
    g2 = shift(cot_m, -2)
    g1 = swap(jnp.where(upper, cot_m, g2), "ctx", 1)
    g4 = shift(g2, -2)
    g3 = swap(jnp.where(upper, g2, g4), "ctx", 1)
    dq_m, dk_m, dv_m = mid_backward(pays, (own_q, qm1, qm2, qm3, qm4), (cot_m, g1, g2, g3, g4))

    near = swap(dq1, "ctx", 1).astype(F32)
    passed = jnp.where(upper, dq2.astype(F32), dq2.astype(F32) + near)
    far = shift(passed.astype(BF16), 2).astype(F32)
    dq_f = (dq0 + far + jnp.where(upper, near, 0.0)).astype(BF16)

    factor = float(lax.axis_size("dp") * lax.axis_size("ctx") * F) ** (-0.5)
    grad_link = link_gradient(jnp.concatenate([mid_out, edge], axis=0), sum_ext, place) * factor
    return (dq_m[None], dk_m[None], dv_m[None], dq_f[None], dk_f[None], dv_f[None], grad_link)


def solution(mesh):
    rows = P("dp", "ctx", None)
    return jax.shard_map(
        shards,
        mesh=mesh,
        in_specs=(rows, rows, rows, P("dp", "ctx"), rows, rows, rows, P(), rows),
        out_specs=(rows,) * 6 + (P("ctx", None),),
        check_vma=False,
    )
```

```python
import math

import jax
import jax.numpy as jnp
from jax import lax
from jax.experimental import pallas as pl
from jax.experimental.pallas import tpu as pltpu
from jax.sharding import PartitionSpec as P

H = 8
E = 128
S = 128
F = 384
REACH = 4
FREACH = 2
WIDTH = H * E
SPAN_M = (REACH + 1) * S
SPAN_F = (FREACH + 1) * F
WIN = FREACH * F
KV = 2 * S + 32
TILES = F // S
TILE_W = WIN + S
SCALE = E ** (-0.5)
LOG2 = SCALE * math.log2(math.e)
NEG = -1e30
F32 = jnp.float32
BF16 = jnp.bfloat16
PARAMS = pltpu.CompilerParams(vmem_limit_bytes=48 * 1024 * 1024)


def dot_nn(a, b):
    return lax.dot_general(a, b, (((1,), (0,)), ((), ())), preferred_element_type=F32)


def dot_nt(a, b):
    return lax.dot_general(a, b, (((1,), (1,)), ((), ())), preferred_element_type=F32)


def dot_tn(a, b):
    return lax.dot_general(a, b, (((0,), (0,)), ((), ())), preferred_element_type=F32)


def iota(shape, axis):
    return lax.broadcasted_iota(jnp.int32, shape, axis)


def to_column(row, size):
    return jnp.transpose(jnp.broadcast_to(row, (size, size)))


def split3(x):
    hi = x.astype(BF16)
    rest = x - hi.astype(F32)
    mid = rest.astype(BF16)
    return hi, mid, (rest - mid.astype(F32)).astype(BF16)


def head_spec(rows):
    return pl.BlockSpec((rows, E), lambda h: (0, h))


def whole_spec(shape):
    return pl.BlockSpec(shape, lambda h: (0,) * len(shape))


def pack_body(flag, q, k, v, ids, qf, kv, qm, first):
    kv[0:S, :] = k[...]
    kv[S : 2 * S, :] = v[...]
    kv[2 * S : 2 * S + 16, :] = ids[...]
    kv[2 * S + 16 : KV, :] = q[S - 16 : S, :]
    qm[0:S, :] = q[...]
    qm[S : S + 16, :] = ids[...]
    first[...] = qf[...]

    @pl.when(flag[0] == 0)
    def _():
        first[0:KV, :] = kv[...]


def pack(flag, q, k, v, ids, qf):
    return pl.pallas_call(
        pack_body,
        grid=(H,),
        in_specs=[FLAG] + [head_spec(S)] * 3 + [whole_spec((16, E)), head_spec(F)],
        out_specs=[head_spec(KV), head_spec(S + 16), head_spec(F)],
        out_shape=[
            jax.ShapeDtypeStruct((KV, WIDTH), BF16),
            jax.ShapeDtypeStruct((S + 16, WIDTH), BF16),
            jax.ShapeDtypeStruct((F, WIDTH), BF16),
        ],
        compiler_params=PARAMS,
        name="pack",
    )(flag, q, k, v, ids, qf)


def pick(flag, upper, lower, rows):
    return jnp.where(flag[0] == 1, upper[0:rows, :], lower[0:rows, :])


def pair_slabs(flag, p4, p3, p2, first, second, p0):
    near = pick(flag, first, second, KV)
    return [p4[...], p3[...], p2[...], near, p0[...]]


def mid_fwd_body(flag, q, p4, p3, p2, first, second, p0, out, att, stat, bias):
    pays = pair_slabs(flag, p4, p3, p2, first, second, p0)

    @pl.when(pl.program_id(0) == 0)
    def _():
        def ids(n):
            return pays[n][2 * S : 2 * S + 16].astype(F32)[0:1]

        mine = to_column(ids(REACH), S)
        edge = to_column(ids(REACH - 1), S)[S - 16 : S]
        for n in range(REACH + 1):
            cols = slice(n * S, (n + 1) * S)
            ok = mine == ids(n)
            ok_edge = edge == ids(n)
            if n == REACH:
                ok = ok & (iota((S, S), 0) >= iota((S, S), 1))
                ok_edge = ok_edge & (iota((16, S), 1) < 0)
            if n == REACH - 1:
                ok_edge = ok_edge & (iota((16, S), 0) + (S - 16) >= iota((16, S), 1))
            bias[0:S, cols] = jnp.where(ok, 0.0, NEG)
            bias[S : S + 16, cols] = jnp.where(ok_edge, 0.0, NEG)

    keys = jnp.concatenate([pay[0:S] for pay in pays], axis=0)
    values = jnp.concatenate([pay[S : 2 * S] for pay in pays], axis=0)
    queries = jnp.concatenate([q[...], pays[REACH - 1][2 * S + 16 : KV]], axis=0)
    scores = dot_nt(queries, keys) * LOG2 + bias[...]
    peak = jnp.max(scores, axis=1, keepdims=True)
    expo = jnp.exp2(scores - peak)
    inv = 1.0 / jnp.sum(expo, axis=1, keepdims=True)
    attended = dot_nn((expo * inv).astype(BF16), values)
    att[...] = attended[0:S]
    out[...] = attended.astype(BF16)
    stat[0:1, :] = jnp.transpose(jnp.broadcast_to(peak[0:S], (S, S)))[0:1]
    stat[1:2, :] = jnp.transpose(jnp.broadcast_to(inv[0:S], (S, S)))[0:1]
    stat[2:8, :] = jnp.zeros((6, S), F32)


def mid_forward(flag, q, pays):
    return pl.pallas_call(
        mid_fwd_body,
        grid=(H,),
        in_specs=[FLAG, head_spec(S)] + PAY_SPECS,
        out_specs=[head_spec(S + 16), head_spec(S), head_spec(8)],
        out_shape=[
            jax.ShapeDtypeStruct((S + 16, WIDTH), BF16),
            jax.ShapeDtypeStruct((S, WIDTH), F32),
            jax.ShapeDtypeStruct((8, WIDTH), F32),
        ],
        scratch_shapes=[pltpu.VMEM((S + 16, SPAN_M), F32)],
        compiler_params=PARAMS,
        cost_estimate=pl.CostEstimate(flops=700_000_000, bytes_accessed=4_000_000, transcendentals=0),
        name="mid_forward",
    )(flag, q, *pays)


FLAG = pl.BlockSpec(memory_space=pltpu.SMEM)
PAY_SPECS = [head_spec(KV)] * 3 + [head_spec(F)] * 2 + [head_spec(KV)]


def full_mask(bias, docs, own_rows, tiles):
    spread = (iota((S, F), 1) // 3 == iota((S, F), 0)).astype(BF16)
    spread_t = (iota((F, S), 0) // 3 == iota((F, S), 1)).astype(BF16)
    rows = jnp.concatenate(
        [dot_nn(jnp.broadcast_to(d, (16, S)), spread)[0:1] for d in docs], axis=1
    )
    column = dot_nn(spread_t, to_column(own_rows.astype(F32), S).astype(BF16))
    for t in range(tiles):
        lo = t * S
        mine = jnp.concatenate([column[lo : lo + S]] * (TILE_W // S), axis=1)
        gap = iota((S, TILE_W), 1) - iota((S, TILE_W), 0)
        ok = (mine == rows[:, lo : lo + TILE_W]) & (gap >= 0) & (gap < WIN)
        bias[t] = jnp.where(ok, 0.0, NEG)


def doc_row(ref):
    return ref[...][0:1]


def stats_body(flag, k, base, mid, w, q0, q1a, q1b, q2, c0, c1, c2, m0, m1, m2, values, s0, s1, s2, bias, ext, part):
    head = pl.program_id(0)

    @pl.when(head == 0)
    def _():
        docs = [doc_row(ref) for ref in (m0, m1, m2)]
        full_mask(bias, docs, docs[0], TILES)
        for t in range(TILES):
            part[t, 0:H, :] = jnp.full((H, SPAN_F), NEG, F32)
            part[t, H : 3 * H, :] = jnp.zeros((2 * H, SPAN_F), F32)

    linked = dot_nn(mid[...], w[...])
    for n in range(2, 5):
        ext[pl.ds(n, S, stride=3), :] = linked[0:S]
    ext[0:2, :] = jnp.broadcast_to(linked[S + 15 : S + 16], (2, E))
    v = (base[...].astype(F32) + ext[0:F, :]).astype(BF16)
    values[...] = v
    queries = jnp.concatenate([q0[...], pick(flag, q1a, q1b, F), q2[...]], axis=0)
    cots = jnp.concatenate([c0[...], c1[...], c2[...]], axis=0)
    for t in range(TILES):
        lo = t * S
        scores = dot_nt(k[lo : lo + S, :], queries[lo : lo + TILE_W]) * LOG2 + bias[t]
        peak = jnp.max(scores, axis=0, keepdims=True)
        expo = jnp.exp2(scores - peak)
        dots = dot_nt(v[lo : lo + S], cots[lo : lo + TILE_W])
        part[t, pl.ds(head, 1), lo : lo + TILE_W] = peak
        part[t, pl.ds(H + head, 1), lo : lo + TILE_W] = jnp.sum(expo, axis=0, keepdims=True)
        part[t, pl.ds(2 * H + head, 1), lo : lo + TILE_W] = jnp.sum(expo * dots, axis=0, keepdims=True)

    @pl.when(head == H - 1)
    def _():
        for n, out in enumerate((s0, s1, s2)):
            cols = slice(n * F, (n + 1) * F)
            merged = merge([(part[t, 0:H, cols], part[t, H : 2 * H, cols], part[t, 2 * H : 3 * H, cols]) for t in range(TILES)])
            for j in range(3):
                out[j * H : (j + 1) * H, :] = merged[j]


def merge(parts):
    peak = parts[0][0]
    for part in parts[1:]:
        peak = jnp.maximum(peak, part[0])
    total, dots = 0.0, 0.0
    for part in parts:
        factor = jnp.exp2(part[0] - peak)
        total = total + part[1] * factor
        dots = dots + part[2] * factor
    return peak, total, dots


def full_stats(flag, k, base, mid, w, qs, cs, ms):
    stat = jax.ShapeDtypeStruct((3 * H, F), F32)
    return pl.pallas_call(
        stats_body,
        grid=(H,),
        in_specs=[FLAG, head_spec(F), head_spec(F), whole_spec((S + 16, WIDTH)), head_spec(WIDTH)]
        + [head_spec(F)] * 7
        + [whole_spec((16, E))] * 3,
        out_specs=[head_spec(F)] + [whole_spec((3 * H, F))] * 3,
        out_shape=[jax.ShapeDtypeStruct((F, WIDTH), BF16), stat, stat, stat],
        scratch_shapes=[
            pltpu.VMEM((TILES, S, TILE_W), F32),
            pltpu.VMEM((400, E), F32),
            pltpu.VMEM((TILES, 3 * H, SPAN_F), F32),
        ],
        compiler_params=PARAMS,
        cost_estimate=pl.CostEstimate(flops=3_000_000_000, bytes_accessed=10_000_000, transcendentals=0),
        name="full_stats",
    )(flag, k, base, mid, w, *qs, *cs, *ms)


def first_body(
    flag, k, v, q0, q1a, q1b, q2, c0, c1, c2, m0, m1, m2, s0, s1, s2, up1, up2, down1, down2, glob, tail, bias
):
    head = pl.program_id(0)

    @pl.when(head == 0)
    def _():
        docs = [doc_row(ref) for ref in (m0, m1, m2)]
        full_mask(bias, docs, docs[0], 1)

        def triple(ref, base):
            peak, total, dots = (ref[base + j * H : base + (j + 1) * H, :] for j in range(3))
            return jnp.where(total > 0.0, peak, NEG), total, dots

        groups = (
            [triple(s0, 0), triple(up1, 0), triple(up2, 0)],
            [triple(s1, 0), triple(up1, 3 * H), triple(down1, 0)],
            [triple(s2, 0), triple(down1, 3 * H), triple(down2, 0)],
        )
        for n, group in enumerate(groups):
            cols = slice(n * F, (n + 1) * F)
            peak, total, dots = merge(group)
            inv = jnp.where(total > 0.0, 1.0 / total, 0.0)
            glob[0:H, cols] = peak
            glob[H : 2 * H, cols] = inv
            glob[2 * H : 3 * H, cols] = dots * inv

    queries = jnp.concatenate([q0[...], pick(flag, q1a, q1b, F), q2[...]], axis=0)
    cots = jnp.concatenate([c0[...], c1[...], c2[...]], axis=0)
    scores = dot_nt(k[...], queries) * LOG2 + bias[0, 0:16, :]
    probs = jnp.exp2(scores - glob[pl.ds(head, 1), 0:TILE_W]) * glob[pl.ds(H + head, 1), 0:TILE_W]
    rows = dot_nn(probs.astype(BF16), cots).astype(BF16).astype(F32)
    tail[...] = jnp.broadcast_to(rows[0:1] + rows[1:2], (8, E))


def full_first(flag, k, v, qs, cs, ms, stats):
    return pl.pallas_call(
        first_body,
        grid=(H,),
        in_specs=[FLAG, head_spec(16), head_spec(16)]
        + [head_spec(F)] * 3 + [head_spec(S)]
        + [head_spec(F)] * 2 + [head_spec(S)]
        + [whole_spec((16, E))] * 3
        + [whole_spec(s.shape) for s in stats],
        out_specs=[whole_spec((3 * H, SPAN_F)), head_spec(8)],
        out_shape=[
            jax.ShapeDtypeStruct((3 * H, SPAN_F), F32),
            jax.ShapeDtypeStruct((8, WIDTH), F32),
        ],
        scratch_shapes=[pltpu.VMEM((1, S, TILE_W), F32)],
        compiler_params=PARAMS,
        cost_estimate=pl.CostEstimate(flops=200_000_000, bytes_accessed=4_000_000, transcendentals=0),
        name="full_first",
    )(flag, k, v, *qs, *cs, *ms, *stats)


def grads_body(
    flag, k, v, q0, q1a, q1b, q2, c0, c1, c2, m0, m1, m2, glob,
    dk, dv, dq0, dq1, dq2, sums, link, bias, ext, kept,
):
    head = pl.program_id(0)

    @pl.when(head == 0)
    def _():
        docs = [doc_row(ref) for ref in (m0, m1, m2)]
        full_mask(bias, docs, docs[0], TILES)
        kept[...] = jnp.zeros((F, SPAN_F), BF16)
        ext[F:400, :] = jnp.zeros((400 - F, E), F32)

    queries = jnp.concatenate([q0[...], pick(flag, q1a, q1b, F), q2[...]], axis=0)
    cots = jnp.concatenate([c0[...], c1[...], c2[...]], axis=0)
    for t in range(TILES):
        lo = t * S
        cols = slice(lo, lo + TILE_W)
        scores = dot_nt(k[lo : lo + S, :], queries[cols]) * LOG2 + bias[t]
        probs = jnp.exp2(scores - glob[pl.ds(head, 1), cols]) * glob[pl.ds(H + head, 1), cols]
        dots = dot_nt(v[lo : lo + S, :], cots[cols])
        grads = (probs * (dots - glob[pl.ds(2 * H + head, 1), cols])).astype(BF16)
        kept[lo : lo + S, cols] = grads
        dk[lo : lo + S, :] = (dot_nn(grads, queries[cols]) * SCALE).astype(BF16)
        grad_v = dot_nn(probs.astype(BF16), cots[cols]).astype(BF16)
        dv[lo : lo + S, :] = grad_v
        ext[lo : lo + S, :] = grad_v.astype(F32)
    for n, out in enumerate((dq0, dq1, dq2)):
        part = dot_tn(kept[:, n * F : (n + 1) * F], k[...]) * SCALE
        out[...] = part.astype(out.dtype)
    total = ext[pl.ds(2, S, stride=3), :] + ext[pl.ds(3, S, stride=3), :] + ext[pl.ds(4, S, stride=3), :]
    sums[...] = total
    first = ext[0:1, :] + ext[1:2, :]
    link[0:S, :] = total.astype(BF16)
    link[S : S + 16, :] = jnp.where(iota((16, E), 0) == 15, first, 0.0).astype(BF16)


def full_grads(flag, k, v, qs, cs, ms, glob):
    return pl.pallas_call(
        grads_body,
        grid=(H,),
        in_specs=[FLAG, head_spec(F), head_spec(F)]
        + [head_spec(F)] * 7
        + [whole_spec((16, E))] * 3
        + [whole_spec(glob.shape)],
        out_specs=[head_spec(F)] * 5 + [head_spec(S), head_spec(S + 16)],
        out_shape=[
            jax.ShapeDtypeStruct((F, WIDTH), BF16),
            jax.ShapeDtypeStruct((F, WIDTH), BF16),
            jax.ShapeDtypeStruct((F, WIDTH), F32),
            jax.ShapeDtypeStruct((F, WIDTH), BF16),
            jax.ShapeDtypeStruct((F, WIDTH), BF16),
            jax.ShapeDtypeStruct((S, WIDTH), F32),
            jax.ShapeDtypeStruct((S + 16, WIDTH), BF16),
        ],
        scratch_shapes=[
            pltpu.VMEM((TILES, S, TILE_W), F32),
            pltpu.VMEM((400, E), F32),
            pltpu.VMEM((F, SPAN_F), BF16),
        ],
        compiler_params=PARAMS,
        cost_estimate=pl.CostEstimate(flops=8_000_000_000, bytes_accessed=14_000_000, transcendentals=0),
        name="full_grads",
    )(flag, k, v, *qs, *cs, *ms, glob)


def mid_cot_body(sums, tail, w, att, stat, out):
    total = sums[...] + jnp.where(iota((S, WIDTH), 0) == S - 1, tail[0:1, :], 0.0)
    grad = dot_nt(total.astype(BF16), w[...]).astype(BF16)
    out[0:S, :] = grad
    weighed = grad.astype(F32) * att[...]
    for h in range(H):
        cols = slice(h * E, (h + 1) * E)
        delta = jnp.sum(jnp.transpose(weighed[:, cols]), axis=0, keepdims=True)
        rows = [*split3(stat[0:1, cols]), *split3(stat[1:2, cols]), *split3(delta)]
        rows = [row.astype(F32) for row in rows] + [jnp.zeros((7, E), F32)]
        out[S : S + 16, cols] = jnp.concatenate(rows, axis=0).astype(BF16)


def mid_cotangent(sums, tail, w, att, stat):
    return pl.pallas_call(
        mid_cot_body,
        out_shape=jax.ShapeDtypeStruct((S + 16, WIDTH), BF16),
        compiler_params=PARAMS,
        cost_estimate=pl.CostEstimate(flops=600_000_000, bytes_accessed=4_000_000, transcendentals=0),
        name="mid_cotangent",
    )(sums, tail, w, att, stat)


def mid_bwd_body(flag, p4, p3, p2, first, second, p0, *refs):
    ms = refs[0:5]
    gs = refs[5:10]
    dq, dk, dv, back, fore = refs[10:]
    pays = pair_slabs(flag, p4, p3, p2, first, second, p0)

    @pl.when(pl.program_id(0) == 0)
    def _():
        mine = p0[2 * S : 2 * S + 16, :].astype(F32)[0:1]
        column = to_column(mine, S)
        causal = iota((S, S), 1) >= iota((S, S), 0)
        for n, pay in enumerate(pays):
            ok = to_column(pay[2 * S : 2 * S + 16].astype(F32)[0:1], S) == mine
            if n == REACH:
                ok = ok & causal
            back[n * S : (n + 1) * S, :] = jnp.where(ok, 0.0, NEG)
        for n, pay in enumerate(ms):
            ok = column == pay[S : S + 16, :].astype(F32)[0:1]
            if n == 0:
                ok = ok & causal
            fore[:, n * S : (n + 1) * S] = jnp.where(ok, 0.0, NEG)

    def stats(ref):
        rows = ref[S : S + 16, :].astype(F32)
        return [rows[j : j + 1] + rows[j + 1 : j + 2] + rows[j + 2 : j + 3] for j in (0, 3, 6)]

    k = p0[0:S, :]
    v = p0[S : 2 * S, :]
    keys = jnp.concatenate([pay[0:S] for pay in pays], axis=0)
    values = jnp.concatenate([pay[S : 2 * S] for pay in pays], axis=0)
    peak, inv, delta = stats(gs[0])
    scores = dot_nt(keys, ms[0][0:S, :]) * LOG2 + back[...]
    probs = jnp.exp2(scores - peak) * inv
    grads = (probs * (dot_nt(values, gs[0][0:S, :]) - delta)).astype(BF16)
    dq[...] = (dot_tn(grads, keys) * SCALE).astype(BF16)
    queries = jnp.concatenate([ref[0:S, :] for ref in ms], axis=0)
    cots = jnp.concatenate([ref[0:S, :] for ref in gs], axis=0)
    every = [stats(ref) for ref in gs]
    peak, inv, delta = (jnp.concatenate([one[j] for one in every], axis=1) for j in range(3))
    scores = dot_nt(k, queries) * LOG2 + fore[...]
    probs = jnp.exp2(scores - peak) * inv
    grads = (probs * (dot_nt(v, cots) - delta)).astype(BF16)
    dk[...] = (dot_nn(grads, queries) * SCALE).astype(BF16)
    dv[...] = dot_nn(probs.astype(BF16), cots).astype(BF16)


def mid_backward(flag, pays, ms, gs):
    return pl.pallas_call(
        mid_bwd_body,
        grid=(H,),
        in_specs=[FLAG] + PAY_SPECS + [head_spec(S + 16)] * 10,
        out_specs=[head_spec(S)] * 3,
        out_shape=[jax.ShapeDtypeStruct((S, WIDTH), BF16)] * 3,
        scratch_shapes=[pltpu.VMEM((SPAN_M, S), F32), pltpu.VMEM((S, SPAN_M), F32)],
        compiler_params=PARAMS,
        cost_estimate=pl.CostEstimate(flops=3_000_000_000, bytes_accessed=6_000_000, transcendentals=0),
        name="mid_backward",
    )(flag, *pays, *ms, *gs)


def shift(value, steps):
    count = lax.axis_size("ctx")
    first, last = max(0, -steps), min(count, count - steps)
    return lax.ppermute(value, "ctx", [(n, n + steps) for n in range(first, last)])


def swap(value, axis, bit):
    count = lax.axis_size(axis)
    return lax.ppermute(value, axis, [(n, n ^ bit) for n in range(count)])


def together(*values):
    return lax.optimization_barrier(values)


def block(value, index, rows):
    return lax.dynamic_slice_in_dim(value, index * rows, rows, 0)


def link_left(mid_ext, place):
    x = place // 16
    parts = [lax.dynamic_slice_in_dim(mid_ext, x * 256, 256, 1)]
    for bits in (1, 2, 3):
        parts.append(swap(lax.dynamic_slice_in_dim(mid_ext, (x ^ bits) * 256, 256, 1), "ctx", 16 * bits))
    return jnp.concatenate(parts, axis=0)


def link_term(left, sum_ext):
    right = jnp.concatenate([sum_ext] + [swap(sum_ext, "ctx", 16 * bits) for bits in (1, 2, 3)], axis=0)
    return dot_tn(left, right)


def link_sum(term, early, late, place):
    z = place // 2 % 8
    total = block(term, z, 32)
    for bits in range(1, 8):
        send = block(early if bits < 4 else late, z ^ bits, 32)
        total = total + swap(send, "ctx", 2 * bits).astype(F32)
    total = block(total, place % 2, 16) + swap(block(total, (place + 1) % 2, 16), "ctx", 1)
    parts = [swap(total, "dp", bits) for bits in (1, 2, 3)]
    return total + parts[0] + parts[1] + parts[2]


def shards(q_mid, k_mid, v_mid, doc_ids, q_full, k_full, v_base, w_link, cotangent):
    place = lax.axis_index("ctx")
    upper = place % 2 == 1
    flag = (place % 2).astype(jnp.int32).reshape(1)
    q_m, q_f, k_f, cot = q_mid[0], q_full[0], k_full[0], cotangent[0]
    ids = jnp.broadcast_to((doc_ids + 1).astype(BF16), (16, S))
    own_kv, own_q, swap_a = pack(flag, q_m, k_mid[0], v_mid[0], ids, q_f)

    kv2 = shift(own_kv, 2)
    got_a = swap(swap_a, "ctx", 1)
    qf2 = shift(q_f, -2)
    late_cot, qf2, got_a = together(cot, qf2, got_a)
    swap_b = jnp.concatenate([jnp.where(upper, kv2, qf2[:KV]), qf2[KV:]], axis=0)
    got_b = swap(swap_b, "ctx", 1)
    kv4 = shift(kv2, 2)
    kv2, kv4 = together(kv2, kv4)
    kv3 = swap(jnp.where(upper, kv4, kv2), "ctx", 1)
    cf2 = shift(late_cot, -2)
    cf1 = swap(jnp.where(upper, cot, cf2), "ctx", 1)
    own_q, cf2 = together(own_q, cf2)
    qm2 = shift(own_q, -2)

    pays = (kv4, kv3, kv2, got_a, got_b, own_kv)
    mid_ext, attended, mid_stat = mid_forward(flag, q_m, pays)

    qm1 = swap(jnp.where(upper, own_q, qm2), "ctx", 1)
    qm4 = shift(qm2, -2)
    qm3 = swap(jnp.where(upper, qm2, qm4), "ctx", 1)

    qs, cs, ms = (q_f, got_b, got_a, qf2), (cot, cf1, cf2), (ids, shift(ids, -1), shift(ids, -2))
    values, s0, s1, s2 = full_stats(flag, k_f, v_base[0], mid_ext, w_link, qs, cs, ms)
    up1 = shift(jnp.concatenate([s1, s2], axis=0), 1)
    up2 = shift(s2, 2)
    down1 = shift(jnp.concatenate([s0, s1], axis=0), -1)
    down2 = shift(s0, -2)
    left = link_left(mid_ext, place)
    values, qm1, qm4, left = together(values, qm1, qm4, left)
    glob, tail = full_first(flag, k_f, values, qs, cs, ms, (s0, s1, s2, up1, up2, down1, down2))
    next_tail = shift(tail, -1)
    dk_f, dv_f, dq0, dq1, dq2, sums, sum_ext = full_grads(flag, k_f, values, qs, cs, ms, glob)
    sums, qm3 = together(sums, qm3)

    cot_m = mid_cotangent(sums, next_tail, w_link, attended, mid_stat)
    cot_m, sum_ext, dq1 = together(cot_m, sum_ext, dq1)
    g2 = shift(cot_m, -2)
    g1 = swap(jnp.where(upper, cot_m, g2), "ctx", 1)
    g4 = shift(g2, -2)
    g3 = swap(jnp.where(upper, g2, g4), "ctx", 1)
    term = link_term(left, sum_ext)
    early, g1 = together(term.astype(BF16), g1)
    late, g3 = together(early, g3)
    dq_m, dk_m, dv_m = mid_backward(flag, pays, (own_q, qm1, qm2, qm3, qm4), (cot_m, g1, g2, g3, g4))

    near = swap(dq1, "ctx", 1).astype(F32)
    passed = jnp.where(upper, dq2.astype(F32), dq2.astype(F32) + near)
    far = shift(passed.astype(BF16), 2).astype(F32)
    dq_f = (dq0 + far + jnp.where(upper, near, 0.0)).astype(BF16)

    factor = float(lax.axis_size("dp") * lax.axis_size("ctx") * F) ** (-0.5)
    grad_link = link_sum(term, early, late, place) * factor
    return (dq_m[None], dk_m[None], dv_m[None], dq_f[None], dk_f[None], dv_f[None], grad_link)


def solution(mesh):
    rows = P("dp", "ctx", None)
    return jax.shard_map(
        shards,
        mesh=mesh,
        in_specs=(rows, rows, rows, P("dp", "ctx"), rows, rows, rows, P(), rows),
        out_specs=(rows,) * 6 + (P("ctx", None),),
        check_vma=False,
    )
```

```python
import math

import jax
import jax.numpy as jnp
from jax import lax
from jax.experimental import pallas as pl
from jax.experimental.pallas import tpu as pltpu
from jax.sharding import PartitionSpec as P

H = 8
E = 128
S = 128
F = 384
REACH = 4
FREACH = 2
WIDTH = H * E
SPAN_M = (REACH + 1) * S
SPAN_F = (FREACH + 1) * F
WIN = FREACH * F
KV = 2 * S + 32
TILES = F // S
TILE_W = WIN + S
SCALE = E ** (-0.5)
LOG2 = SCALE * math.log2(math.e)
NEG = -1e30
F32 = jnp.float32
BF16 = jnp.bfloat16
PARAMS = pltpu.CompilerParams(vmem_limit_bytes=16 * 1024 * 1024)


def dot_nn(a, b):
    return lax.dot_general(a, b, (((1,), (0,)), ((), ())), preferred_element_type=F32)


def dot_nt(a, b):
    return lax.dot_general(a, b, (((1,), (1,)), ((), ())), preferred_element_type=F32)


def dot_tn(a, b):
    return lax.dot_general(a, b, (((0,), (0,)), ((), ())), preferred_element_type=F32)


def iota(shape, axis):
    return lax.broadcasted_iota(jnp.int32, shape, axis)


def to_column(row, size):
    return jnp.transpose(jnp.broadcast_to(row, (size, size)))


def split3(x):
    hi = x.astype(BF16)
    rest = x - hi.astype(F32)
    mid = rest.astype(BF16)
    return hi, mid, (rest - mid.astype(F32)).astype(BF16)


def head_spec(rows):
    return pl.BlockSpec((rows, E), lambda h: (0, h))


def whole_spec(shape):
    return pl.BlockSpec(shape, lambda h: (0,) * len(shape))


def pack_body(flag, q, k, v, ids, qf, kv, qm, first):
    kv[0:S, :] = k[...]
    kv[S : 2 * S, :] = v[...]
    kv[2 * S : 2 * S + 16, :] = ids[...]
    kv[2 * S + 16 : KV, :] = q[S - 16 : S, :]
    qm[0:S, :] = q[...]
    qm[S : S + 16, :] = ids[...]
    first[...] = qf[...]

    @pl.when(flag[0] == 0)
    def _():
        first[0:KV, :] = kv[...]


def pack(flag, q, k, v, ids, qf):
    return pl.pallas_call(
        pack_body,
        grid=(H,),
        in_specs=[FLAG] + [head_spec(S)] * 3 + [whole_spec((16, E)), head_spec(F)],
        out_specs=[head_spec(KV), head_spec(S + 16), head_spec(F)],
        out_shape=[
            jax.ShapeDtypeStruct((KV, WIDTH), BF16),
            jax.ShapeDtypeStruct((S + 16, WIDTH), BF16),
            jax.ShapeDtypeStruct((F, WIDTH), BF16),
        ],
        compiler_params=pltpu.CompilerParams(vmem_limit_bytes=60 * 1024 * 1024),
        name="pack",
    )(flag, q, k, v, ids, qf)


def pick(flag, upper, lower, rows):
    return jnp.where(flag[0] == 1, upper[0:rows, :], lower[0:rows, :])


def pair_slabs(flag, p4, p3, p2, first, second, p0):
    near = pick(flag, first, second, KV)
    return [p4[...], p3[...], p2[...], near, p0[...]]


def mid_fwd_body(flag, q, p4, p3, p2, first, second, p0, out, att, stat, bias):
    pays = pair_slabs(flag, p4, p3, p2, first, second, p0)

    @pl.when(pl.program_id(0) == 0)
    def _():
        def ids(n):
            return pays[n][2 * S : 2 * S + 16].astype(F32)[0:1]

        mine = to_column(ids(REACH), S)
        edge = to_column(ids(REACH - 1), S)[S - 16 : S]
        for n in range(REACH + 1):
            cols = slice(n * S, (n + 1) * S)
            ok = mine == ids(n)
            ok_edge = edge == ids(n)
            if n == REACH:
                ok = ok & (iota((S, S), 0) >= iota((S, S), 1))
                ok_edge = ok_edge & (iota((16, S), 1) < 0)
            if n == REACH - 1:
                ok_edge = ok_edge & (iota((16, S), 0) + (S - 16) >= iota((16, S), 1))
            bias[0:S, cols] = jnp.where(ok, 0.0, NEG)
            bias[S : S + 16, cols] = jnp.where(ok_edge, 0.0, NEG)

    keys = jnp.concatenate([pay[0:S] for pay in pays], axis=0)
    values = jnp.concatenate([pay[S : 2 * S] for pay in pays], axis=0)
    queries = jnp.concatenate([q[...], pays[REACH - 1][2 * S + 16 : KV]], axis=0)
    scores = dot_nt(queries, keys) * LOG2 + bias[...]
    peak = jnp.max(scores, axis=1, keepdims=True)
    expo = jnp.exp2(scores - peak)
    inv = 1.0 / jnp.sum(expo, axis=1, keepdims=True)
    attended = dot_nn((expo * inv).astype(BF16), values)
    att[...] = attended[0:S]
    out[...] = attended.astype(BF16)
    stat[0:1, :] = jnp.transpose(jnp.broadcast_to(peak[0:S], (S, S)))[0:1]
    stat[1:2, :] = jnp.transpose(jnp.broadcast_to(inv[0:S], (S, S)))[0:1]
    stat[2:8, :] = jnp.zeros((6, S), F32)


def mid_forward(flag, q, pays):
    return pl.pallas_call(
        mid_fwd_body,
        grid=(H,),
        in_specs=[FLAG, head_spec(S)] + PAY_SPECS,
        out_specs=[head_spec(S + 16), head_spec(S), head_spec(8)],
        out_shape=[
            jax.ShapeDtypeStruct((S + 16, WIDTH), BF16),
            jax.ShapeDtypeStruct((S, WIDTH), F32),
            jax.ShapeDtypeStruct((8, WIDTH), F32),
        ],
        scratch_shapes=[pltpu.VMEM((S + 16, SPAN_M), F32)],
        compiler_params=PARAMS,
        cost_estimate=pl.CostEstimate(flops=700_000_000, bytes_accessed=4_000_000, transcendentals=0),
        name="mid_forward",
    )(flag, q, *pays)


FLAG = pl.BlockSpec(memory_space=pltpu.SMEM)
PAY_SPECS = [head_spec(KV)] * 3 + [head_spec(F)] * 2 + [head_spec(KV)]


def full_mask(bias, docs, own_rows, tiles):
    spread = (iota((S, F), 1) // 3 == iota((S, F), 0)).astype(BF16)
    spread_t = (iota((F, S), 0) // 3 == iota((F, S), 1)).astype(BF16)
    rows = jnp.concatenate(
        [dot_nn(jnp.broadcast_to(d, (16, S)), spread)[0:1] for d in docs], axis=1
    )
    column = dot_nn(spread_t, to_column(own_rows.astype(F32), S).astype(BF16))
    for t in range(tiles):
        lo = t * S
        mine = jnp.concatenate([column[lo : lo + S]] * (TILE_W // S), axis=1)
        gap = iota((S, TILE_W), 1) - iota((S, TILE_W), 0)
        ok = (mine == rows[:, lo : lo + TILE_W]) & (gap >= 0) & (gap < WIN)
        bias[t] = jnp.where(ok, 0.0, NEG)


def doc_row(ref):
    return ref[...][0:1]


def stats_body(flag, k, base, mid, w, q0, q1a, q1b, q2, c0, c1, c2, m0, m1, m2, values, s0, s1, s2, bias, ext, part):
    head = pl.program_id(0)

    @pl.when(head == 0)
    def _():
        docs = [doc_row(ref) for ref in (m0, m1, m2)]
        full_mask(bias, docs, docs[0], TILES)
        for t in range(TILES):
            part[t, 0:H, :] = jnp.full((H, SPAN_F), NEG, F32)
            part[t, H : 3 * H, :] = jnp.zeros((2 * H, SPAN_F), F32)

    linked = dot_nn(mid[...], w[...])
    for n in range(2, 5):
        ext[pl.ds(n, S, stride=3), :] = linked[0:S]
    ext[0:2, :] = jnp.broadcast_to(linked[S + 15 : S + 16], (2, E))
    v = (base[...].astype(F32) + ext[0:F, :]).astype(BF16)
    values[...] = v
    queries = jnp.concatenate([q0[...], pick(flag, q1a, q1b, F), q2[...]], axis=0)
    cots = jnp.concatenate([c0[...], c1[...], c2[...]], axis=0)
    for t in range(TILES):
        lo = t * S
        scores = dot_nt(k[lo : lo + S, :], queries[lo : lo + TILE_W]) * LOG2 + bias[t]
        peak = jnp.max(scores, axis=0, keepdims=True)
        expo = jnp.exp2(scores - peak)
        dots = dot_nt(v[lo : lo + S], cots[lo : lo + TILE_W])
        part[t, pl.ds(head, 1), lo : lo + TILE_W] = peak
        part[t, pl.ds(H + head, 1), lo : lo + TILE_W] = jnp.sum(expo, axis=0, keepdims=True)
        part[t, pl.ds(2 * H + head, 1), lo : lo + TILE_W] = jnp.sum(expo * dots, axis=0, keepdims=True)

    @pl.when(head == H - 1)
    def _():
        for n, out in enumerate((s0, s1, s2)):
            cols = slice(n * F, (n + 1) * F)
            merged = merge([(part[t, 0:H, cols], part[t, H : 2 * H, cols], part[t, 2 * H : 3 * H, cols]) for t in range(TILES)])
            for j in range(3):
                out[j * H : (j + 1) * H, :] = merged[j]


def merge(parts):
    peak = parts[0][0]
    for part in parts[1:]:
        peak = jnp.maximum(peak, part[0])
    total, dots = 0.0, 0.0
    for part in parts:
        factor = jnp.exp2(part[0] - peak)
        total = total + part[1] * factor
        dots = dots + part[2] * factor
    return peak, total, dots


def full_stats(flag, k, base, mid, w, qs, cs, ms):
    stat = jax.ShapeDtypeStruct((3 * H, F), F32)
    return pl.pallas_call(
        stats_body,
        grid=(H,),
        in_specs=[FLAG, head_spec(F), head_spec(F), whole_spec((S + 16, WIDTH)), head_spec(WIDTH)]
        + [head_spec(F)] * 7
        + [whole_spec((16, E))] * 3,
        out_specs=[head_spec(F)] + [whole_spec((3 * H, F))] * 3,
        out_shape=[jax.ShapeDtypeStruct((F, WIDTH), BF16), stat, stat, stat],
        scratch_shapes=[
            pltpu.VMEM((TILES, S, TILE_W), F32),
            pltpu.VMEM((400, E), F32),
            pltpu.VMEM((TILES, 3 * H, SPAN_F), F32),
        ],
        compiler_params=PARAMS,
        cost_estimate=pl.CostEstimate(flops=3_000_000_000, bytes_accessed=10_000_000, transcendentals=0),
        name="full_stats",
    )(flag, k, base, mid, w, *qs, *cs, *ms)


def first_body(
    flag, k, v, q0, q1a, q1b, q2, c0, c1, c2, m0, m1, m2, s0, s1, s2, up1, up2, down1, down2, glob, tail, bias
):
    head = pl.program_id(0)

    @pl.when(head == 0)
    def _():
        docs = [doc_row(ref) for ref in (m0, m1, m2)]
        full_mask(bias, docs, docs[0], 1)

        def triple(ref, base):
            peak, total, dots = (ref[base + j * H : base + (j + 1) * H, :] for j in range(3))
            return jnp.where(total > 0.0, peak, NEG), total, dots

        groups = (
            [triple(s0, 0), triple(up1, 0), triple(up2, 0)],
            [triple(s1, 0), triple(up1, 3 * H), triple(down1, 0)],
            [triple(s2, 0), triple(down1, 3 * H), triple(down2, 0)],
        )
        for n, group in enumerate(groups):
            cols = slice(n * F, (n + 1) * F)
            peak, total, dots = merge(group)
            inv = jnp.where(total > 0.0, 1.0 / total, 0.0)
            glob[0:H, cols] = peak
            glob[H : 2 * H, cols] = inv
            glob[2 * H : 3 * H, cols] = dots * inv

    queries = jnp.concatenate([q0[...], pick(flag, q1a, q1b, F), q2[...]], axis=0)
    cots = jnp.concatenate([c0[...], c1[...], c2[...]], axis=0)
    scores = dot_nt(k[...], queries) * LOG2 + bias[0, 0:16, :]
    probs = jnp.exp2(scores - glob[pl.ds(head, 1), 0:TILE_W]) * glob[pl.ds(H + head, 1), 0:TILE_W]
    rows = dot_nn(probs.astype(BF16), cots).astype(BF16).astype(F32)
    tail[...] = jnp.broadcast_to(rows[0:1] + rows[1:2], (8, E))


def full_first(flag, k, v, qs, cs, ms, stats):
    return pl.pallas_call(
        first_body,
        grid=(H,),
        in_specs=[FLAG, head_spec(16), head_spec(16)]
        + [head_spec(F)] * 3 + [head_spec(S)]
        + [head_spec(F)] * 2 + [head_spec(S)]
        + [whole_spec((16, E))] * 3
        + [whole_spec(s.shape) for s in stats],
        out_specs=[whole_spec((3 * H, SPAN_F)), head_spec(8)],
        out_shape=[
            jax.ShapeDtypeStruct((3 * H, SPAN_F), F32),
            jax.ShapeDtypeStruct((8, WIDTH), F32),
        ],
        scratch_shapes=[pltpu.VMEM((1, S, TILE_W), F32)],
        compiler_params=PARAMS,
        cost_estimate=pl.CostEstimate(flops=200_000_000, bytes_accessed=4_000_000, transcendentals=0),
        name="full_first",
    )(flag, k, v, *qs, *cs, *ms, *stats)


def grads_body(
    flag, k, v, q0, q1a, q1b, q2, c0, c1, c2, m0, m1, m2, glob,
    dk, dv, dq0, dq1, dq2, sums, link, bias, ext, kept,
):
    head = pl.program_id(0)

    @pl.when(head == 0)
    def _():
        docs = [doc_row(ref) for ref in (m0, m1, m2)]
        full_mask(bias, docs, docs[0], TILES)
        kept[...] = jnp.zeros((F, SPAN_F), BF16)
        ext[F:400, :] = jnp.zeros((400 - F, E), F32)

    queries = jnp.concatenate([q0[...], pick(flag, q1a, q1b, F), q2[...]], axis=0)
    cots = jnp.concatenate([c0[...], c1[...], c2[...]], axis=0)
    for t in range(TILES):
        lo = t * S
        cols = slice(lo, lo + TILE_W)
        scores = dot_nt(k[lo : lo + S, :], queries[cols]) * LOG2 + bias[t]
        probs = jnp.exp2(scores - glob[pl.ds(head, 1), cols]) * glob[pl.ds(H + head, 1), cols]
        dots = dot_nt(v[lo : lo + S, :], cots[cols])
        grads = (probs * (dots - glob[pl.ds(2 * H + head, 1), cols])).astype(BF16)
        kept[lo : lo + S, cols] = grads
        dk[lo : lo + S, :] = (dot_nn(grads, queries[cols]) * SCALE).astype(BF16)
        grad_v = dot_nn(probs.astype(BF16), cots[cols]).astype(BF16)
        dv[lo : lo + S, :] = grad_v
        ext[lo : lo + S, :] = grad_v.astype(F32)
    for n, out in enumerate((dq0, dq1, dq2)):
        part = dot_tn(kept[:, n * F : (n + 1) * F], k[...]) * SCALE
        out[...] = part.astype(out.dtype)
    total = ext[pl.ds(2, S, stride=3), :] + ext[pl.ds(3, S, stride=3), :] + ext[pl.ds(4, S, stride=3), :]
    sums[...] = total
    first = ext[0:1, :] + ext[1:2, :]
    link[0:S, :] = total.astype(BF16)
    link[S : S + 16, :] = jnp.where(iota((16, E), 0) == 15, first, 0.0).astype(BF16)


def full_grads(flag, k, v, qs, cs, ms, glob):
    return pl.pallas_call(
        grads_body,
        grid=(H,),
        in_specs=[FLAG, head_spec(F), head_spec(F)]
        + [head_spec(F)] * 7
        + [whole_spec((16, E))] * 3
        + [whole_spec(glob.shape)],
        out_specs=[head_spec(F)] * 5 + [head_spec(S), head_spec(S + 16)],
        out_shape=[
            jax.ShapeDtypeStruct((F, WIDTH), BF16),
            jax.ShapeDtypeStruct((F, WIDTH), BF16),
            jax.ShapeDtypeStruct((F, WIDTH), F32),
            jax.ShapeDtypeStruct((F, WIDTH), BF16),
            jax.ShapeDtypeStruct((F, WIDTH), BF16),
            jax.ShapeDtypeStruct((S, WIDTH), F32),
            jax.ShapeDtypeStruct((S + 16, WIDTH), BF16),
        ],
        scratch_shapes=[
            pltpu.VMEM((TILES, S, TILE_W), F32),
            pltpu.VMEM((400, E), F32),
            pltpu.VMEM((F, SPAN_F), BF16),
        ],
        compiler_params=PARAMS,
        cost_estimate=pl.CostEstimate(flops=8_000_000_000, bytes_accessed=14_000_000, transcendentals=0),
        name="full_grads",
    )(flag, k, v, *qs, *cs, *ms, glob)


def mid_cot_body(sums, tail, w, att, stat, out):
    total = sums[...] + jnp.where(iota((S, WIDTH), 0) == S - 1, tail[0:1, :], 0.0)
    grad = dot_nt(total.astype(BF16), w[...]).astype(BF16)
    out[0:S, :] = grad
    weighed = grad.astype(F32) * att[...]
    for h in range(H):
        cols = slice(h * E, (h + 1) * E)
        delta = jnp.sum(jnp.transpose(weighed[:, cols]), axis=0, keepdims=True)
        rows = [*split3(stat[0:1, cols]), *split3(stat[1:2, cols]), *split3(delta)]
        rows = [row.astype(F32) for row in rows] + [jnp.zeros((7, E), F32)]
        out[S : S + 16, cols] = jnp.concatenate(rows, axis=0).astype(BF16)


def mid_cotangent(sums, tail, w, att, stat):
    return pl.pallas_call(
        mid_cot_body,
        out_shape=jax.ShapeDtypeStruct((S + 16, WIDTH), BF16),
        compiler_params=PARAMS,
        cost_estimate=pl.CostEstimate(flops=600_000_000, bytes_accessed=4_000_000, transcendentals=0),
        name="mid_cotangent",
    )(sums, tail, w, att, stat)


def mid_bwd_body(flag, p4, p3, p2, first, second, p0, *refs):
    ms = refs[0:5]
    gs = refs[5:10]
    dq, dk, dv, back, fore = refs[10:]
    pays = pair_slabs(flag, p4, p3, p2, first, second, p0)

    @pl.when(pl.program_id(0) == 0)
    def _():
        mine = p0[2 * S : 2 * S + 16, :].astype(F32)[0:1]
        column = to_column(mine, S)
        causal = iota((S, S), 1) >= iota((S, S), 0)
        for n, pay in enumerate(pays):
            ok = to_column(pay[2 * S : 2 * S + 16].astype(F32)[0:1], S) == mine
            if n == REACH:
                ok = ok & causal
            back[n * S : (n + 1) * S, :] = jnp.where(ok, 0.0, NEG)
        for n, pay in enumerate(ms):
            ok = column == pay[S : S + 16, :].astype(F32)[0:1]
            if n == 0:
                ok = ok & causal
            fore[:, n * S : (n + 1) * S] = jnp.where(ok, 0.0, NEG)

    def stats(ref):
        rows = ref[S : S + 16, :].astype(F32)
        return [rows[j : j + 1] + rows[j + 1 : j + 2] + rows[j + 2 : j + 3] for j in (0, 3, 6)]

    k = p0[0:S, :]
    v = p0[S : 2 * S, :]
    keys = jnp.concatenate([pay[0:S] for pay in pays], axis=0)
    values = jnp.concatenate([pay[S : 2 * S] for pay in pays], axis=0)
    peak, inv, delta = stats(gs[0])
    scores = dot_nt(keys, ms[0][0:S, :]) * LOG2 + back[...]
    probs = jnp.exp2(scores - peak) * inv
    grads = (probs * (dot_nt(values, gs[0][0:S, :]) - delta)).astype(BF16)
    dq[...] = (dot_tn(grads, keys) * SCALE).astype(BF16)
    queries = jnp.concatenate([ref[0:S, :] for ref in ms], axis=0)
    cots = jnp.concatenate([ref[0:S, :] for ref in gs], axis=0)
    every = [stats(ref) for ref in gs]
    peak, inv, delta = (jnp.concatenate([one[j] for one in every], axis=1) for j in range(3))
    scores = dot_nt(k, queries) * LOG2 + fore[...]
    probs = jnp.exp2(scores - peak) * inv
    grads = (probs * (dot_nt(v, cots) - delta)).astype(BF16)
    dk[...] = (dot_nn(grads, queries) * SCALE).astype(BF16)
    dv[...] = dot_nn(probs.astype(BF16), cots).astype(BF16)


def mid_backward(flag, pays, ms, gs):
    return pl.pallas_call(
        mid_bwd_body,
        grid=(H,),
        in_specs=[FLAG] + PAY_SPECS + [head_spec(S + 16)] * 10,
        out_specs=[head_spec(S)] * 3,
        out_shape=[jax.ShapeDtypeStruct((S, WIDTH), BF16)] * 3,
        scratch_shapes=[pltpu.VMEM((SPAN_M, S), F32), pltpu.VMEM((S, SPAN_M), F32)],
        compiler_params=PARAMS,
        cost_estimate=pl.CostEstimate(flops=3_000_000_000, bytes_accessed=6_000_000, transcendentals=0),
        name="mid_backward",
    )(flag, *pays, *ms, *gs)


def shift(value, steps):
    count = lax.axis_size("ctx")
    first, last = max(0, -steps), min(count, count - steps)
    return lax.ppermute(value, "ctx", [(n, n + steps) for n in range(first, last)])


def swap(value, axis, bit):
    count = lax.axis_size(axis)
    return lax.ppermute(value, axis, [(n, n ^ bit) for n in range(count)])


def together(*values):
    return lax.optimization_barrier(values)


def block(value, index, rows):
    return lax.dynamic_slice_in_dim(value, index * rows, rows, 0)


def link_left(mid_ext, place):
    groups = [[first + 16 * n for n in range(4)] for first in range(16)]
    every = lax.all_gather(mid_ext, "ctx", axis_index_groups=groups, tiled=True)
    return lax.dynamic_slice_in_dim(every, place // 16 * 256, 256, 1)


def link_term(left, sum_ext):
    groups = [[first + 16 * n for n in range(4)] for first in range(16)]
    right = lax.all_gather(sum_ext, "ctx", axis_index_groups=groups, tiled=True)
    return dot_tn(left, right)


def link_sum(term):
    groups = [[16 * first + n for n in range(16)] for first in range(4)]
    rows = lax.psum_scatter(term, "ctx", scatter_dimension=0, axis_index_groups=groups, tiled=True)
    return lax.psum(rows, "dp")


def shards(q_mid, k_mid, v_mid, doc_ids, q_full, k_full, v_base, w_link, cotangent):
    place = lax.axis_index("ctx")
    upper = place % 2 == 1
    flag = (place % 2).astype(jnp.int32).reshape(1)
    q_m, q_f, k_f, cot = q_mid[0], q_full[0], k_full[0], cotangent[0]
    ids = jnp.broadcast_to((doc_ids + 1).astype(BF16), (16, S))
    own_kv, own_q, swap_a = pack(flag, q_m, k_mid[0], v_mid[0], ids, q_f)

    kv2 = shift(own_kv, 2)
    got_a = swap(swap_a, "ctx", 1)
    qf2 = shift(q_f, -2)
    late_cot, qf2, got_a = together(cot, qf2, got_a)
    swap_b = jnp.concatenate([jnp.where(upper, kv2, qf2[:KV]), qf2[KV:]], axis=0)
    got_b = swap(swap_b, "ctx", 1)
    kv4 = shift(kv2, 2)
    kv2, kv4 = together(kv2, kv4)
    kv3 = swap(jnp.where(upper, kv4, kv2), "ctx", 1)
    cf2 = shift(late_cot, -2)
    cf1 = swap(jnp.where(upper, cot, cf2), "ctx", 1)
    own_q, cf2 = together(own_q, cf2)
    qm2 = shift(own_q, -2)

    pays = (kv4, kv3, kv2, got_a, got_b, own_kv)
    mid_ext, attended, mid_stat = mid_forward(flag, q_m, pays)

    qm1 = swap(jnp.where(upper, own_q, qm2), "ctx", 1)
    qm4 = shift(qm2, -2)
    qm3 = swap(jnp.where(upper, qm2, qm4), "ctx", 1)

    qs, cs, ms = (q_f, got_b, got_a, qf2), (cot, cf1, cf2), (ids, shift(ids, -1), shift(ids, -2))
    values, s0, s1, s2 = full_stats(flag, k_f, v_base[0], mid_ext, w_link, qs, cs, ms)
    up1 = shift(jnp.concatenate([s1, s2], axis=0), 1)
    up2 = shift(s2, 2)
    down1 = shift(jnp.concatenate([s0, s1], axis=0), -1)
    down2 = shift(s0, -2)
    left = link_left(mid_ext, place)
    values, qm1, qm4, left = together(values, qm1, qm4, left)
    glob, tail = full_first(flag, k_f, values, qs, cs, ms, (s0, s1, s2, up1, up2, down1, down2))
    next_tail = shift(tail, -1)
    dk_f, dv_f, dq0, dq1, dq2, sums, sum_ext = full_grads(flag, k_f, values, qs, cs, ms, glob)
    sums, qm3 = together(sums, qm3)

    cot_m = mid_cotangent(sums, next_tail, w_link, attended, mid_stat)
    cot_m, dq1 = together(cot_m, dq1)
    g2 = shift(cot_m, -2)
    g1 = swap(jnp.where(upper, cot_m, g2), "ctx", 1)
    g4 = shift(g2, -2)
    g3 = swap(jnp.where(upper, g2, g4), "ctx", 1)
    term = link_term(left, sum_ext)
    dq_m, dk_m, dv_m = mid_backward(flag, pays, (own_q, qm1, qm2, qm3, qm4), (cot_m, g1, g2, g3, g4))

    near = swap(dq1, "ctx", 1).astype(F32)
    passed = jnp.where(upper, dq2.astype(F32), dq2.astype(F32) + near)
    far = shift(passed.astype(BF16), 2).astype(F32)
    dq_f = (dq0 + far + jnp.where(upper, near, 0.0)).astype(BF16)

    factor = float(lax.axis_size("dp") * lax.axis_size("ctx") * F) ** (-0.5)
    grad_link = link_sum(term) * factor
    return (dq_m[None], dk_m[None], dv_m[None], dq_f[None], dk_f[None], dv_f[None], grad_link)


def solution(mesh):
    rows = P("dp", "ctx", None)
    return jax.shard_map(
        shards,
        mesh=mesh,
        in_specs=(rows, rows, rows, P("dp", "ctx"), rows, rows, rows, P(), rows),
        out_specs=(rows,) * 6 + (P("ctx", None),),
        check_vma=False,
    )
```

```python
import math

import jax
import jax.numpy as jnp
from jax import lax
from jax.experimental import pallas as pl
from jax.experimental.pallas import tpu as pltpu
from jax.sharding import PartitionSpec as P

H = 8
E = 128
S = 128
F = 384
REACH = 4
FREACH = 2
WIDTH = H * E
SPAN_M = (REACH + 1) * S
SPAN_F = (FREACH + 1) * F
WIN = FREACH * F
KV = 2 * S + 32
CQ = F + S + 16
TILES = F // S
TILE_W = WIN + S
SCALE = E ** (-0.5)
LOG2 = SCALE * math.log2(math.e)
NEG = -1e30
F32 = jnp.float32
BF16 = jnp.bfloat16
PARAMS = pltpu.CompilerParams(vmem_limit_bytes=16 * 1024 * 1024)


def dot_nn(a, b):
    return lax.dot_general(a, b, (((1,), (0,)), ((), ())), preferred_element_type=F32)


def dot_nt(a, b):
    return lax.dot_general(a, b, (((1,), (1,)), ((), ())), preferred_element_type=F32)


def dot_tn(a, b):
    return lax.dot_general(a, b, (((0,), (0,)), ((), ())), preferred_element_type=F32)


def iota(shape, axis):
    return lax.broadcasted_iota(jnp.int32, shape, axis)


def to_column(row, size):
    return jnp.transpose(jnp.broadcast_to(row, (size, size)))


def split3(x):
    hi = x.astype(BF16)
    rest = x - hi.astype(F32)
    mid = rest.astype(BF16)
    return hi, mid, (rest - mid.astype(F32)).astype(BF16)


def head_spec(rows):
    return pl.BlockSpec((rows, E), lambda h: (0, h))


def whole_spec(shape):
    return pl.BlockSpec(shape, lambda h: (0,) * len(shape))


def pack_body(flag, q, k, v, ids, qf, cot, kv, cq, first):
    kv[0:S, :] = k[...]
    kv[S : 2 * S, :] = v[...]
    kv[2 * S : 2 * S + 16, :] = ids[...]
    kv[2 * S + 16 : KV, :] = q[S - 16 : S, :]
    cq[0:F, :] = cot[...]
    cq[F : F + S, :] = q[...]
    cq[F + S : CQ, :] = ids[...]
    first[...] = qf[...]

    @pl.when(flag[0] == 0)
    def _():
        first[0:KV, :] = kv[...]


def pack(flag, q, k, v, ids, qf, cot):
    def wide(rows):
        return pl.BlockSpec((rows, 2 * E), lambda h: (0, h))

    return pl.pallas_call(
        pack_body,
        grid=(H // 2,),
        in_specs=[FLAG] + [wide(S)] * 3 + [whole_spec((16, 2 * E)), wide(F), wide(F)],
        out_specs=[wide(KV), wide(CQ), wide(F)],
        out_shape=[
            jax.ShapeDtypeStruct((KV, WIDTH), BF16),
            jax.ShapeDtypeStruct((CQ, WIDTH), BF16),
            jax.ShapeDtypeStruct((F, WIDTH), BF16),
        ],
        compiler_params=pltpu.CompilerParams(vmem_limit_bytes=60 * 1024 * 1024),
        name="pack",
    )(flag, q, k, v, ids, qf, cot)


def pick(flag, upper, lower, rows):
    return jnp.where(flag[0] == 1, upper[0:rows, :], lower[0:rows, :])


def pair_slabs(flag, p4, p3, p2, first, second, p0):
    near = pick(flag, first, second, KV)
    return [p4[...], p3[...], p2[...], near, p0[...]]


def mid_fwd_body(flag, q, p4, p3, p2, first, second, p0, out, att, stat, bias):
    pays = pair_slabs(flag, p4, p3, p2, first, second, p0)

    @pl.when(pl.program_id(0) == 0)
    def _():
        def ids(n):
            return pays[n][2 * S : 2 * S + 16].astype(F32)[0:1]

        mine = to_column(ids(REACH), S)
        edge = to_column(ids(REACH - 1), S)[S - 16 : S]
        for n in range(REACH + 1):
            cols = slice(n * S, (n + 1) * S)
            ok = mine == ids(n)
            ok_edge = edge == ids(n)
            if n == REACH:
                ok = ok & (iota((S, S), 0) >= iota((S, S), 1))
                ok_edge = ok_edge & (iota((16, S), 1) < 0)
            if n == REACH - 1:
                ok_edge = ok_edge & (iota((16, S), 0) + (S - 16) >= iota((16, S), 1))
            bias[0:S, cols] = jnp.where(ok, 0.0, NEG)
            bias[S : S + 16, cols] = jnp.where(ok_edge, 0.0, NEG)

    keys = jnp.concatenate([pay[0:S] for pay in pays], axis=0)
    values = jnp.concatenate([pay[S : 2 * S] for pay in pays], axis=0)
    queries = jnp.concatenate([q[...], pays[REACH - 1][2 * S + 16 : KV]], axis=0)
    scores = dot_nt(queries, keys) * LOG2 + bias[...]
    peak = jnp.max(scores, axis=1, keepdims=True)
    expo = jnp.exp2(scores - peak)
    inv = 1.0 / jnp.sum(expo, axis=1, keepdims=True)
    attended = dot_nn((expo * inv).astype(BF16), values)
    att[...] = attended[0:S]
    out[...] = attended.astype(BF16)
    stat[0:1, :] = jnp.transpose(jnp.broadcast_to(peak[0:S], (S, S)))[0:1]
    stat[1:2, :] = jnp.transpose(jnp.broadcast_to(inv[0:S], (S, S)))[0:1]
    stat[2:8, :] = jnp.zeros((6, S), F32)


def mid_forward(flag, q, pays):
    return pl.pallas_call(
        mid_fwd_body,
        grid=(H,),
        in_specs=[FLAG, head_spec(S)] + PAY_SPECS,
        out_specs=[head_spec(S + 16), head_spec(S), head_spec(8)],
        out_shape=[
            jax.ShapeDtypeStruct((S + 16, WIDTH), BF16),
            jax.ShapeDtypeStruct((S, WIDTH), F32),
            jax.ShapeDtypeStruct((8, WIDTH), F32),
        ],
        scratch_shapes=[pltpu.VMEM((S + 16, SPAN_M), F32)],
        compiler_params=PARAMS,
        cost_estimate=pl.CostEstimate(flops=700_000_000, bytes_accessed=4_000_000, transcendentals=0),
        name="mid_forward",
    )(flag, q, *pays)


FLAG = pl.BlockSpec(memory_space=pltpu.SMEM)
PAY_SPECS = [head_spec(KV)] * 3 + [head_spec(F)] * 2 + [head_spec(KV)]


def full_mask(bias, docs, own_rows):
    spread = (iota((S, F), 1) // 3 == iota((S, F), 0)).astype(BF16)
    spread_t = (iota((F, S), 0) // 3 == iota((F, S), 1)).astype(BF16)
    rows = jnp.concatenate(
        [dot_nn(jnp.broadcast_to(d, (16, S)), spread)[0:1] for d in docs], axis=1
    )
    column = dot_nn(spread_t, to_column(own_rows.astype(F32), S).astype(BF16))
    for t in range(TILES):
        lo = t * S
        mine = jnp.concatenate([column[lo : lo + S]] * (TILE_W // S), axis=1)
        gap = iota((S, TILE_W), 1) - iota((S, TILE_W), 0)
        ok = (mine == rows[:, lo : lo + TILE_W]) & (gap >= 0) & (gap < WIN)
        bias[t] = jnp.where(ok, 0.0, NEG)


def doc_row(ref):
    return ref[F + S : CQ, 0:S][0:1]


def stats_body(flag, k, base, mid, w, q0, q1a, q1b, q2, c0, c1, c2, values, s0, s1, s2, bias, ext, part):
    head = pl.program_id(0)

    @pl.when(head == 0)
    def _():
        docs = [doc_row(ref) for ref in (c0, c1, c2)]
        full_mask(bias, docs, docs[0])
        for t in range(TILES):
            part[t, 0:H, :] = jnp.full((H, SPAN_F), NEG, F32)
            part[t, H : 3 * H, :] = jnp.zeros((2 * H, SPAN_F), F32)

    linked = dot_nn(mid[...], w[...])
    for n in range(2, 5):
        ext[pl.ds(n, S, stride=3), :] = linked[0:S]
    ext[0:2, :] = jnp.broadcast_to(linked[S + 15 : S + 16], (2, E))
    v = (base[...].astype(F32) + ext[0:F, :]).astype(BF16)
    values[...] = v
    queries = jnp.concatenate([q0[...], pick(flag, q1a, q1b, F), q2[...]], axis=0)
    cots = jnp.concatenate([c0[0:F, :], c1[0:F, :], c2[0:F, :]], axis=0)
    for t in range(TILES):
        lo = t * S
        scores = dot_nt(k[lo : lo + S, :], queries[lo : lo + TILE_W]) * LOG2 + bias[t]
        peak = jnp.max(scores, axis=0, keepdims=True)
        expo = jnp.exp2(scores - peak)
        dots = dot_nt(v[lo : lo + S], cots[lo : lo + TILE_W])
        part[t, pl.ds(head, 1), lo : lo + TILE_W] = peak
        part[t, pl.ds(H + head, 1), lo : lo + TILE_W] = jnp.sum(expo, axis=0, keepdims=True)
        part[t, pl.ds(2 * H + head, 1), lo : lo + TILE_W] = jnp.sum(expo * dots, axis=0, keepdims=True)

    @pl.when(head == H - 1)
    def _():
        for n, out in enumerate((s0, s1, s2)):
            cols = slice(n * F, (n + 1) * F)
            merged = merge([(part[t, 0:H, cols], part[t, H : 2 * H, cols], part[t, 2 * H : 3 * H, cols]) for t in range(TILES)])
            for j in range(3):
                out[j * H : (j + 1) * H, :] = merged[j]


def merge(parts):
    peak = parts[0][0]
    for part in parts[1:]:
        peak = jnp.maximum(peak, part[0])
    total, dots = 0.0, 0.0
    for part in parts:
        factor = jnp.exp2(part[0] - peak)
        total = total + part[1] * factor
        dots = dots + part[2] * factor
    return peak, total, dots


def full_stats(flag, k, base, mid, w, qs, cs):
    stat = jax.ShapeDtypeStruct((3 * H, F), F32)
    return pl.pallas_call(
        stats_body,
        grid=(H,),
        in_specs=[FLAG, head_spec(F), head_spec(F), whole_spec((S + 16, WIDTH)), head_spec(WIDTH)]
        + [head_spec(F)] * 4
        + [head_spec(CQ)] * 3,
        out_specs=[head_spec(F)] + [whole_spec((3 * H, F))] * 3,
        out_shape=[jax.ShapeDtypeStruct((F, WIDTH), BF16), stat, stat, stat],
        scratch_shapes=[
            pltpu.VMEM((TILES, S, TILE_W), F32),
            pltpu.VMEM((400, E), F32),
            pltpu.VMEM((TILES, 3 * H, SPAN_F), F32),
        ],
        compiler_params=PARAMS,
        cost_estimate=pl.CostEstimate(flops=3_000_000_000, bytes_accessed=10_000_000, transcendentals=0),
        name="full_stats",
    )(flag, k, base, mid, w, *qs, *cs)


def grads_body(
    flag, k, v, q0, q1a, q1b, q2, c0, c1, c2, s0, s1, s2, up1, up2, down1, down2,
    dk, dv, dq0, dq1, dq2, sums, link, tail, bias, ext, glob, kept,
):
    head = pl.program_id(0)

    @pl.when(head == 0)
    def _():
        docs = [doc_row(ref) for ref in (c0, c1, c2)]
        full_mask(bias, docs, docs[0])

        def triple(ref, base):
            peak, total, dots = (ref[base + j * H : base + (j + 1) * H, :] for j in range(3))
            return jnp.where(total > 0.0, peak, NEG), total, dots

        groups = (
            [triple(s0, 0), triple(up1, 0), triple(up2, 0)],
            [triple(s1, 0), triple(up1, 3 * H), triple(down1, 0)],
            [triple(s2, 0), triple(down1, 3 * H), triple(down2, 0)],
        )
        for n, group in enumerate(groups):
            cols = slice(n * F, (n + 1) * F)
            peak, total, dots = merge(group)
            inv = jnp.where(total > 0.0, 1.0 / total, 0.0)
            glob[0:H, cols] = peak
            glob[H : 2 * H, cols] = inv
            glob[2 * H : 3 * H, cols] = dots * inv
        kept[...] = jnp.zeros((F, SPAN_F), BF16)
        ext[F:400, :] = jnp.zeros((400 - F, E), F32)

    queries = jnp.concatenate([q0[...], pick(flag, q1a, q1b, F), q2[...]], axis=0)
    cots = jnp.concatenate([c0[0:F, :], c1[0:F, :], c2[0:F, :]], axis=0)
    for t in range(TILES):
        lo = t * S
        cols = slice(lo, lo + TILE_W)
        scores = dot_nt(k[lo : lo + S, :], queries[cols]) * LOG2 + bias[t]
        probs = jnp.exp2(scores - glob[pl.ds(head, 1), cols]) * glob[pl.ds(H + head, 1), cols]
        dots = dot_nt(v[lo : lo + S, :], cots[cols])
        grads = (probs * (dots - glob[pl.ds(2 * H + head, 1), cols])).astype(BF16)
        kept[lo : lo + S, cols] = grads
        dk[lo : lo + S, :] = (dot_nn(grads, queries[cols]) * SCALE).astype(BF16)
        grad_v = dot_nn(probs.astype(BF16), cots[cols]).astype(BF16)
        dv[lo : lo + S, :] = grad_v
        ext[lo : lo + S, :] = grad_v.astype(F32)
    for n, out in enumerate((dq0, dq1, dq2)):
        part = dot_tn(kept[:, n * F : (n + 1) * F], k[...]) * SCALE
        out[...] = part.astype(out.dtype)
    total = ext[pl.ds(2, S, stride=3), :] + ext[pl.ds(3, S, stride=3), :] + ext[pl.ds(4, S, stride=3), :]
    sums[...] = total
    first = ext[0:1, :] + ext[1:2, :]
    tail[...] = jnp.broadcast_to(first, (8, E))
    link[0:S, :] = total.astype(BF16)
    link[S : S + 16, :] = jnp.where(iota((16, E), 0) == 15, first, 0.0).astype(BF16)


def full_grads(flag, k, v, qs, cs, stats):
    return pl.pallas_call(
        grads_body,
        grid=(H,),
        in_specs=[FLAG, head_spec(F), head_spec(F)]
        + [head_spec(F)] * 4
        + [head_spec(CQ)] * 3
        + [whole_spec(s.shape) for s in stats],
        out_specs=[head_spec(F)] * 5 + [head_spec(S), head_spec(S + 16), head_spec(8)],
        out_shape=[
            jax.ShapeDtypeStruct((F, WIDTH), BF16),
            jax.ShapeDtypeStruct((F, WIDTH), BF16),
            jax.ShapeDtypeStruct((F, WIDTH), F32),
            jax.ShapeDtypeStruct((F, WIDTH), BF16),
            jax.ShapeDtypeStruct((F, WIDTH), BF16),
            jax.ShapeDtypeStruct((S, WIDTH), F32),
            jax.ShapeDtypeStruct((S + 16, WIDTH), BF16),
            jax.ShapeDtypeStruct((8, WIDTH), F32),
        ],
        scratch_shapes=[
            pltpu.VMEM((TILES, S, TILE_W), F32),
            pltpu.VMEM((400, E), F32),
            pltpu.VMEM((3 * H, SPAN_F), F32),
            pltpu.VMEM((F, SPAN_F), BF16),
        ],
        compiler_params=PARAMS,
        cost_estimate=pl.CostEstimate(flops=8_000_000_000, bytes_accessed=14_000_000, transcendentals=0),
        name="full_grads",
    )(flag, k, v, *qs, *cs, *stats)


def mid_cot_body(sums, tail, w, att, stat, out):
    total = sums[...] + jnp.where(iota((S, WIDTH), 0) == S - 1, tail[0:1, :], 0.0)
    grad = dot_nt(total.astype(BF16), w[...]).astype(BF16)
    out[0:S, :] = grad
    weighed = grad.astype(F32) * att[...]
    for h in range(H):
        cols = slice(h * E, (h + 1) * E)
        delta = jnp.sum(jnp.transpose(weighed[:, cols]), axis=0, keepdims=True)
        rows = [*split3(stat[0:1, cols]), *split3(stat[1:2, cols]), *split3(delta)]
        rows = [row.astype(F32) for row in rows] + [jnp.zeros((7, E), F32)]
        out[S : S + 16, cols] = jnp.concatenate(rows, axis=0).astype(BF16)


def mid_cotangent(sums, tail, w, att, stat):
    return pl.pallas_call(
        mid_cot_body,
        out_shape=jax.ShapeDtypeStruct((S + 16, WIDTH), BF16),
        compiler_params=PARAMS,
        cost_estimate=pl.CostEstimate(flops=600_000_000, bytes_accessed=4_000_000, transcendentals=0),
        name="mid_cotangent",
    )(sums, tail, w, att, stat)


def mid_bwd_body(flag, p4, p3, p2, first, second, p0, *refs):
    ms = [ref[F:CQ, :] for ref in refs[0:3]] + [ref[...] for ref in refs[3:5]]
    gs = refs[5:10]
    dq, dk, dv, back, fore = refs[10:]
    pays = pair_slabs(flag, p4, p3, p2, first, second, p0)

    @pl.when(pl.program_id(0) == 0)
    def _():
        mine = p0[2 * S : 2 * S + 16, :].astype(F32)[0:1]
        column = to_column(mine, S)
        causal = iota((S, S), 1) >= iota((S, S), 0)
        for n, pay in enumerate(pays):
            ok = to_column(pay[2 * S : 2 * S + 16].astype(F32)[0:1], S) == mine
            if n == REACH:
                ok = ok & causal
            back[n * S : (n + 1) * S, :] = jnp.where(ok, 0.0, NEG)
        for n, pay in enumerate(ms):
            ok = column == pay[S : S + 16].astype(F32)[0:1]
            if n == 0:
                ok = ok & causal
            fore[:, n * S : (n + 1) * S] = jnp.where(ok, 0.0, NEG)

    def stats(ref):
        rows = ref[S : S + 16, :].astype(F32)
        return [rows[j : j + 1] + rows[j + 1 : j + 2] + rows[j + 2 : j + 3] for j in (0, 3, 6)]

    k = p0[0:S, :]
    v = p0[S : 2 * S, :]
    keys = jnp.concatenate([pay[0:S] for pay in pays], axis=0)
    values = jnp.concatenate([pay[S : 2 * S] for pay in pays], axis=0)
    peak, inv, delta = stats(gs[0])
    scores = dot_nt(keys, ms[0][0:S]) * LOG2 + back[...]
    probs = jnp.exp2(scores - peak) * inv
    grads = (probs * (dot_nt(values, gs[0][0:S, :]) - delta)).astype(BF16)
    dq[...] = (dot_tn(grads, keys) * SCALE).astype(BF16)
    queries = jnp.concatenate([one[0:S] for one in ms], axis=0)
    cots = jnp.concatenate([ref[0:S, :] for ref in gs], axis=0)
    every = [stats(ref) for ref in gs]
    peak, inv, delta = (jnp.concatenate([one[j] for one in every], axis=1) for j in range(3))
    scores = dot_nt(k, queries) * LOG2 + fore[...]
    probs = jnp.exp2(scores - peak) * inv
    grads = (probs * (dot_nt(v, cots) - delta)).astype(BF16)
    dk[...] = (dot_nn(grads, queries) * SCALE).astype(BF16)
    dv[...] = dot_nn(probs.astype(BF16), cots).astype(BF16)


def mid_backward(flag, pays, ms, gs):
    return pl.pallas_call(
        mid_bwd_body,
        grid=(H,),
        in_specs=[FLAG] + PAY_SPECS + [head_spec(CQ)] * 3 + [head_spec(S + 16)] * 7,
        out_specs=[head_spec(S)] * 3,
        out_shape=[jax.ShapeDtypeStruct((S, WIDTH), BF16)] * 3,
        scratch_shapes=[pltpu.VMEM((SPAN_M, S), F32), pltpu.VMEM((S, SPAN_M), F32)],
        compiler_params=PARAMS,
        cost_estimate=pl.CostEstimate(flops=3_000_000_000, bytes_accessed=6_000_000, transcendentals=0),
        name="mid_backward",
    )(flag, *pays, *ms, *gs)


def shift(value, steps):
    count = lax.axis_size("ctx")
    first, last = max(0, -steps), min(count, count - steps)
    return lax.ppermute(value, "ctx", [(n, n + steps) for n in range(first, last)])


def swap(value, axis, bit):
    count = lax.axis_size(axis)
    return lax.ppermute(value, axis, [(n, n ^ bit) for n in range(count)])


def together(*values):
    return lax.optimization_barrier(values)


def block(value, index, rows):
    return lax.dynamic_slice_in_dim(value, index * rows, rows, 0)


X_GROUPS = [[first + 16 * n for n in range(4)] for first in range(16)]
YZ_GROUPS = [[16 * first + n for n in range(16)] for first in range(4)]


def exchange(value, axis, groups):
    return lax.all_to_all(value, axis, 0, 0, axis_index_groups=groups, tiled=True)


def shards(q_mid, k_mid, v_mid, doc_ids, q_full, k_full, v_base, w_link, cotangent):
    place = lax.axis_index("ctx")
    upper = place % 2 == 1
    flag = (place % 2).astype(jnp.int32).reshape(1)
    q_m, q_f, k_f = q_mid[0], q_full[0], k_full[0]
    ids = jnp.broadcast_to(jnp.tile((doc_ids + 1).astype(BF16), (1, 2)), (16, 2 * S))
    own_kv, own_cq, swap_a = pack(flag, q_m, k_mid[0], v_mid[0], ids, q_f, cotangent[0])

    kv2 = shift(own_kv, 2)
    got_a = swap(swap_a, "ctx", 1)
    qf2 = shift(q_f, -2)
    late_cq, qf2, kv2, got_a = together(own_cq, qf2, kv2, got_a)
    swap_b = jnp.concatenate([jnp.where(upper, kv2, qf2[:KV]), qf2[KV:]], axis=0)
    got_b = swap(swap_b, "ctx", 1)
    kv4 = shift(kv2, 2)
    kv2, kv4 = together(kv2, kv4)
    kv3 = swap(jnp.where(upper, kv4, kv2), "ctx", 1)
    cq2 = shift(late_cq, -2)
    cq2, got_b = together(cq2, got_b)
    cq1 = swap(jnp.where(upper, late_cq, cq2), "ctx", 1)

    pays = (kv4, kv3, kv2, got_a, got_b, own_kv)
    mid_ext, attended, mid_stat = mid_forward(flag, q_m, pays)
    parts = jnp.concatenate([mid_ext[:, n * 256 : (n + 1) * 256] for n in range(4)], axis=0)
    left, cq1 = together(exchange(parts, "ctx", X_GROUPS), cq1)
    qm2, cq1 = together(cq2[F:], cq1)
    qm4 = shift(qm2, -2)
    qs, cs = (q_f, got_b, got_a, qf2), (late_cq, cq1, cq2)
    values, s0, s1, s2 = full_stats(flag, k_f, v_base[0], mid_ext, w_link, qs, cs)
    up1 = shift(jnp.concatenate([s1, s2], axis=0), 1)
    up2 = shift(s2, 2)
    down1 = shift(jnp.concatenate([s0, s1], axis=0), -1)
    down2 = shift(s0, -2)

    qm4, up1 = together(qm4, up1)
    qm3 = swap(jnp.where(upper, qm2, qm4), "ctx", 1)
    dk_f, dv_f, dq0, dq1, dq2, sums, sum_ext, tail = full_grads(
        flag, k_f, values, qs, cs, (s0, s1, s2, up1, up2, down1, down2)
    )

    next_tail = shift(tail, -1)
    near = swap(dq1, "ctx", 1)
    right = exchange(jnp.concatenate([sum_ext] * 4, axis=0), "ctx", X_GROUPS)
    sums, right, qm3 = together(sums, right, qm3)
    cot_m = mid_cotangent(sums, next_tail, w_link, attended, mid_stat)
    g2 = shift(cot_m, -2)
    term = dot_tn(left, right).astype(BF16)
    term, g2, near = together(term, g2, near)
    g1 = swap(jnp.where(upper, cot_m, g2), "ctx", 1)
    g4 = shift(g2, -2)
    total = jnp.sum(exchange(term, "ctx", YZ_GROUPS).astype(F32).reshape(16, 16, WIDTH), axis=0)
    total, g4 = together(total, g4)
    g3 = swap(jnp.where(upper, g2, g4), "ctx", 1)
    every = exchange(jnp.concatenate([total] * 4, axis=0), "dp", None)
    factor = float(lax.axis_size("dp") * lax.axis_size("ctx") * F) ** (-0.5)
    grad_link = jnp.sum(every.reshape(4, 16, WIDTH), axis=0) * factor
    dq_m, dk_m, dv_m = mid_backward(flag, pays, (late_cq, cq1, cq2, qm3, qm4), (cot_m, g1, g2, g3, g4))

    near = near.astype(F32)
    passed = jnp.where(upper, dq2.astype(F32), dq2.astype(F32) + near)
    far = shift(passed.astype(BF16), 2).astype(F32)
    dq_f = (dq0 + far + jnp.where(upper, near, 0.0)).astype(BF16)
    return (dq_m[None], dk_m[None], dv_m[None], dq_f[None], dk_f[None], dv_f[None], grad_link)


def solution(mesh):
    rows = P("dp", "ctx", None)
    return jax.shard_map(
        shards,
        mesh=mesh,
        in_specs=(rows, rows, rows, P("dp", "ctx"), rows, rows, rows, P(), rows),
        out_specs=(rows,) * 6 + (P("ctx", None),),
        check_vma=False,
    )
```

```python
import math

import jax
import jax.numpy as jnp
from jax import lax
from jax.experimental import pallas as pl
from jax.experimental.pallas import tpu as pltpu
from jax.sharding import PartitionSpec as P

H = 8
E = 128
S = 128
F = 384
REACH = 4
FREACH = 2
WIDTH = H * E
SPAN_M = (REACH + 1) * S
SPAN_F = (FREACH + 1) * F
WIN = FREACH * F
KV = 2 * S + 32
CQ = F + S + 16
TILES = F // S
TILE_W = WIN + S
SCALE = E ** (-0.5)
LOG2 = SCALE * math.log2(math.e)
NEG = -1e30
F32 = jnp.float32
BF16 = jnp.bfloat16


def dot_nn(a, b):
    return lax.dot_general(a, b, (((1,), (0,)), ((), ())), preferred_element_type=F32)


def dot_nt(a, b):
    return lax.dot_general(a, b, (((1,), (1,)), ((), ())), preferred_element_type=F32)


def dot_tn(a, b):
    return lax.dot_general(a, b, (((0,), (0,)), ((), ())), preferred_element_type=F32)


def iota(shape, axis):
    return lax.broadcasted_iota(jnp.int32, shape, axis)


def to_column(row, size):
    return jnp.transpose(jnp.broadcast_to(row, (size, size)))


def split3(x):
    hi = x.astype(BF16)
    rest = x - hi.astype(F32)
    mid = rest.astype(BF16)
    return hi, mid, (rest - mid.astype(F32)).astype(BF16)


def head_spec(rows):
    return pl.BlockSpec((rows, E), lambda h: (0, h))


def whole_spec(shape):
    return pl.BlockSpec(shape, lambda h: (0,) * len(shape))


def pack_body(flag, q, k, v, ids, qf, cot, kv, cq, first):
    kv[0:S, :] = k[...]
    kv[S : 2 * S, :] = v[...]
    kv[2 * S : 2 * S + 16, :] = ids[...]
    kv[2 * S + 16 : KV, :] = q[S - 16 : S, :]
    cq[0:F, :] = cot[...]
    cq[F : F + S, :] = q[...]
    cq[F + S : CQ, :] = ids[...]
    first[...] = qf[...]

    @pl.when(flag[0] == 0)
    def _():
        first[0:KV, :] = kv[...]


def pack(flag, q, k, v, ids, qf, cot):
    def wide(rows):
        return pl.BlockSpec((rows, 2 * E), lambda h: (0, h))

    return pl.pallas_call(
        pack_body,
        grid=(H // 2,),
        in_specs=[FLAG] + [wide(S)] * 3 + [whole_spec((16, 2 * E)), wide(F), wide(F)],
        out_specs=[wide(KV), wide(CQ), wide(F)],
        out_shape=[
            jax.ShapeDtypeStruct((KV, WIDTH), BF16),
            jax.ShapeDtypeStruct((CQ, WIDTH), BF16),
            jax.ShapeDtypeStruct((F, WIDTH), BF16),
        ],
        name="pack",
    )(flag, q, k, v, ids, qf, cot)


def pick(flag, upper, lower, rows):
    return jnp.where(flag[0] == 1, upper[0:rows, :], lower[0:rows, :])


def pair_slabs(flag, p4, p3, p2, first, second, p0):
    near = pick(flag, first, second, KV)
    return [p4[...], p3[...], p2[...], near, p0[...]]


def mid_fwd_body(flag, q, p4, p3, p2, first, second, p0, out, att, stat, bias):
    pays = pair_slabs(flag, p4, p3, p2, first, second, p0)

    @pl.when(pl.program_id(0) == 0)
    def _():
        def ids(n):
            return pays[n][2 * S : 2 * S + 16].astype(F32)[0:1]

        mine = to_column(ids(REACH), S)
        edge = to_column(ids(REACH - 1), S)[S - 16 : S]
        for n in range(REACH + 1):
            cols = slice(n * S, (n + 1) * S)
            ok = mine == ids(n)
            ok_edge = edge == ids(n)
            if n == REACH:
                ok = ok & (iota((S, S), 0) >= iota((S, S), 1))
                ok_edge = ok_edge & (iota((16, S), 1) < 0)
            if n == REACH - 1:
                ok_edge = ok_edge & (iota((16, S), 0) + (S - 16) >= iota((16, S), 1))
            bias[0:S, cols] = jnp.where(ok, 0.0, NEG)
            bias[S : S + 16, cols] = jnp.where(ok_edge, 0.0, NEG)

    keys = jnp.concatenate([pay[0:S] for pay in pays], axis=0)
    values = jnp.concatenate([pay[S : 2 * S] for pay in pays], axis=0)
    queries = jnp.concatenate([q[...], pays[REACH - 1][2 * S + 16 : KV]], axis=0)
    scores = dot_nt(queries, keys) * LOG2 + bias[...]
    peak = jnp.max(scores, axis=1, keepdims=True)
    expo = jnp.exp2(scores - peak)
    inv = 1.0 / jnp.sum(expo, axis=1, keepdims=True)
    attended = dot_nn((expo * inv).astype(BF16), values)
    att[...] = attended[0:S]
    out[...] = attended.astype(BF16)
    stat[0:1, :] = jnp.transpose(jnp.broadcast_to(peak[0:S], (S, S)))[0:1]
    stat[1:2, :] = jnp.transpose(jnp.broadcast_to(inv[0:S], (S, S)))[0:1]
    stat[2:8, :] = jnp.zeros((6, S), F32)


def mid_forward(flag, q, pays):
    return pl.pallas_call(
        mid_fwd_body,
        grid=(H,),
        in_specs=[FLAG, head_spec(S)] + PAY_SPECS,
        out_specs=[head_spec(S + 16), head_spec(S), head_spec(8)],
        out_shape=[
            jax.ShapeDtypeStruct((S + 16, WIDTH), BF16),
            jax.ShapeDtypeStruct((S, WIDTH), F32),
            jax.ShapeDtypeStruct((8, WIDTH), F32),
        ],
        scratch_shapes=[pltpu.VMEM((S + 16, SPAN_M), F32)],
        cost_estimate=pl.CostEstimate(flops=700_000_000, bytes_accessed=4_000_000, transcendentals=0),
        name="mid_forward",
    )(flag, q, *pays)


FLAG = pl.BlockSpec(memory_space=pltpu.SMEM)
PAY_SPECS = [head_spec(KV)] * 3 + [head_spec(F)] * 2 + [head_spec(KV)]


def full_mask(bias, docs):
    spread = (iota((S, F), 1) // 3 == iota((S, F), 0)).astype(BF16)
    spread_t = (iota((F, S), 0) // 3 == iota((F, S), 1)).astype(BF16)
    rows = jnp.concatenate(
        [dot_nn(jnp.broadcast_to(d, (16, S)), spread)[0:1] for d in docs], axis=1
    )
    column = dot_nn(spread_t, to_column(docs[0].astype(F32), S).astype(BF16))
    for t in range(TILES):
        lo = t * S
        mine = jnp.concatenate([column[lo : lo + S]] * (TILE_W // S), axis=1)
        gap = iota((S, TILE_W), 1) - iota((S, TILE_W), 0)
        ok = (mine == rows[:, lo : lo + TILE_W]) & (gap >= 0) & (gap < WIN)
        bias[t] = jnp.where(ok, 0.0, NEG)


def doc_row(ref):
    return ref[F + S : CQ, 0:S][0:1]


def stats_body(k, base, mid, w, q0, q2, c0, c2, values, s0, s2, bias, ext, part):
    head = pl.program_id(0)

    @pl.when(head == 0)
    def _():
        full_mask(bias, [doc_row(ref) for ref in (c0, c0, c2)])

    linked = dot_nn(mid[...], w[...])
    for n in range(2, 5):
        ext[pl.ds(n, S, stride=3), :] = linked[0:S]
    ext[0:2, :] = jnp.broadcast_to(linked[S + 15 : S + 16], (2, E))
    v = (base[...].astype(F32) + ext[0:F, :]).astype(BF16)
    values[...] = v
    for t in range(TILES):
        lo, first, last = t * S, F - t * S, (t + 1) * S
        queries = jnp.concatenate([q0[lo:F, :], q2[0:last, :]], axis=0)
        cots = jnp.concatenate([c0[lo:F, :], c2[0:last, :]], axis=0)
        mask = jnp.concatenate([bias[t, :, 0:first], bias[t, :, first + F : first + F + last]], axis=1)
        rows = partial_stats(k[lo : lo + S, :], v[lo : lo + S], queries, cots, mask)
        for j, empty in enumerate((NEG, 0.0, 0.0)):
            pieces = [jnp.full((1, lo), empty, F32)] if lo else []
            pieces += [rows[j]] + ([jnp.full((1, F - last), empty, F32)] if last < F else [])
            part[t, pl.ds(j * H + head, 1), :] = jnp.concatenate(pieces, axis=1)

    @pl.when(head == H - 1)
    def _():
        for out, cols in ((s0, slice(0, F)), (s2, slice(F, 2 * F))):
            merge_into(out, part, cols)


def partial_stats(k, v, queries, cots, mask):
    scores = dot_nt(k, queries) * LOG2 + mask
    peak = jnp.max(scores, axis=0, keepdims=True)
    expo = jnp.exp2(scores - peak)
    dots = dot_nt(v, cots)
    return peak, jnp.sum(expo, axis=0, keepdims=True), jnp.sum(expo * dots, axis=0, keepdims=True)


def merge_into(out, part, cols):
    merged = merge([tuple(part[t, j * H : (j + 1) * H, cols] for j in range(3)) for t in range(TILES)])
    for j in range(3):
        out[j * H : (j + 1) * H, :] = merged[j]


def stats_next_body(flag, k, v, q1a, q1b, c0, c1, s1, bias, part):
    head = pl.program_id(0)

    @pl.when(head == 0)
    def _():
        full_mask(bias, [doc_row(ref) for ref in (c0, c1, c1)])

    queries = pick(flag, q1a, q1b, F)
    for t in range(TILES):
        lo = t * S
        mask = bias[t, :, F - lo : 2 * F - lo]
        rows = partial_stats(k[lo : lo + S, :], v[lo : lo + S, :], queries, c1[0:F, :], mask)
        for j in range(3):
            part[t, pl.ds(j * H + head, 1), :] = rows[j]

    @pl.when(head == H - 1)
    def _():
        merge_into(s1, part, slice(0, F))


def merge(parts):
    peak = parts[0][0]
    for part in parts[1:]:
        peak = jnp.maximum(peak, part[0])
    total, dots = 0.0, 0.0
    for part in parts:
        factor = jnp.exp2(part[0] - peak)
        total = total + part[1] * factor
        dots = dots + part[2] * factor
    return peak, total, dots


def full_stats(k, base, mid, w, q0, q2, c0, c2):
    stat = jax.ShapeDtypeStruct((3 * H, F), F32)
    return pl.pallas_call(
        stats_body,
        grid=(H,),
        in_specs=[head_spec(F), head_spec(F), whole_spec((S + 16, WIDTH)), head_spec(WIDTH)]
        + [head_spec(F)] * 2
        + [head_spec(CQ)] * 2,
        out_specs=[head_spec(F)] + [whole_spec((3 * H, F))] * 2,
        out_shape=[jax.ShapeDtypeStruct((F, WIDTH), BF16), stat, stat],
        scratch_shapes=[
            pltpu.VMEM((TILES, S, TILE_W), F32),
            pltpu.VMEM((400, E), F32),
            pltpu.VMEM((TILES, 3 * H, 2 * F), F32),
        ],
        cost_estimate=pl.CostEstimate(flops=2_000_000_000, bytes_accessed=8_000_000, transcendentals=0),
        name="full_stats",
    )(k, base, mid, w, q0, q2, c0, c2)


def next_stats(flag, k, v, q1a, q1b, c0, c1):
    return pl.pallas_call(
        stats_next_body,
        grid=(H,),
        in_specs=[FLAG] + [head_spec(F)] * 4 + [head_spec(CQ)] * 2,
        out_specs=whole_spec((3 * H, F)),
        out_shape=jax.ShapeDtypeStruct((3 * H, F), F32),
        scratch_shapes=[
            pltpu.VMEM((TILES, S, TILE_W), F32),
            pltpu.VMEM((TILES, 3 * H, F), F32),
        ],
        cost_estimate=pl.CostEstimate(flops=1_000_000_000, bytes_accessed=6_000_000, transcendentals=0),
        name="next_stats",
    )(flag, k, v, q1a, q1b, c0, c1)


def grads_body(
    flag, k, v, q0, q1a, q1b, q2, c0, c1, c2, s0, s1, s2, up1, up1_far, up2, down1, down1_far, down2,
    dk, dv, dq0, dq1, dq2, sums, link, tail, bias, ext, glob, kept,
):
    head = pl.program_id(0)

    @pl.when(head == 0)
    def _():
        full_mask(bias, [doc_row(ref) for ref in (c0, c1, c2)])

        def triple(ref):
            peak, total, dots = (ref[j * H : (j + 1) * H, :] for j in range(3))
            return jnp.where(total > 0.0, peak, NEG), total, dots

        for n, group in enumerate(((s0, up1, up2), (s1, up1_far, down1_far), (s2, down1, down2))):
            cols = slice(n * F, (n + 1) * F)
            peak, total, dots = merge([triple(ref) for ref in group])
            inv = jnp.where(total > 0.0, 1.0 / total, 0.0)
            glob[0:H, cols] = peak
            glob[H : 2 * H, cols] = inv
            glob[2 * H : 3 * H, cols] = dots * inv
        kept[...] = jnp.zeros((F, SPAN_F), BF16)
        ext[F:400, :] = jnp.zeros((400 - F, E), F32)

    queries = jnp.concatenate([q0[...], pick(flag, q1a, q1b, F), q2[...]], axis=0)
    cots = jnp.concatenate([c0[0:F, :], c1[0:F, :], c2[0:F, :]], axis=0)
    for t in range(TILES):
        lo = t * S
        cols = slice(lo, lo + TILE_W)
        scores = dot_nt(k[lo : lo + S, :], queries[cols]) * LOG2 + bias[t]
        probs = jnp.exp2(scores - glob[pl.ds(head, 1), cols]) * glob[pl.ds(H + head, 1), cols]
        dots = dot_nt(v[lo : lo + S, :], cots[cols])
        grads = (probs * (dots - glob[pl.ds(2 * H + head, 1), cols])).astype(BF16)
        kept[lo : lo + S, cols] = grads
        dk[lo : lo + S, :] = (dot_nn(grads, queries[cols]) * SCALE).astype(BF16)
        grad_v = dot_nn(probs.astype(BF16), cots[cols]).astype(BF16)
        dv[lo : lo + S, :] = grad_v
        ext[lo : lo + S, :] = grad_v.astype(F32)
    for n, out in enumerate((dq0, dq1, dq2)):
        part = dot_tn(kept[:, n * F : (n + 1) * F], k[...]) * SCALE
        out[...] = part.astype(out.dtype)
    total = ext[pl.ds(2, S, stride=3), :] + ext[pl.ds(3, S, stride=3), :] + ext[pl.ds(4, S, stride=3), :]
    sums[...] = total
    first = ext[0:1, :] + ext[1:2, :]
    tail[...] = jnp.broadcast_to(first, (8, E))
    link[0:S, :] = total.astype(BF16)
    link[S : S + 16, :] = jnp.where(iota((16, E), 0) == 15, first, 0.0).astype(BF16)


def full_grads(flag, k, v, qs, cs, stats):
    return pl.pallas_call(
        grads_body,
        grid=(H,),
        in_specs=[FLAG, head_spec(F), head_spec(F)]
        + [head_spec(F)] * 4
        + [head_spec(CQ)] * 3
        + [whole_spec(s.shape) for s in stats],
        out_specs=[head_spec(F)] * 5 + [head_spec(S), head_spec(S + 16), head_spec(8)],
        out_shape=[
            jax.ShapeDtypeStruct((F, WIDTH), BF16),
            jax.ShapeDtypeStruct((F, WIDTH), BF16),
            jax.ShapeDtypeStruct((F, WIDTH), F32),
            jax.ShapeDtypeStruct((F, WIDTH), BF16),
            jax.ShapeDtypeStruct((F, WIDTH), BF16),
            jax.ShapeDtypeStruct((S, WIDTH), F32),
            jax.ShapeDtypeStruct((S + 16, WIDTH), BF16),
            jax.ShapeDtypeStruct((8, WIDTH), F32),
        ],
        scratch_shapes=[
            pltpu.VMEM((TILES, S, TILE_W), F32),
            pltpu.VMEM((400, E), F32),
            pltpu.VMEM((3 * H, SPAN_F), F32),
            pltpu.VMEM((F, SPAN_F), BF16),
        ],
        cost_estimate=pl.CostEstimate(flops=8_000_000_000, bytes_accessed=14_000_000, transcendentals=0),
        name="full_grads",
    )(flag, k, v, *qs, *cs, *stats)


def mid_cot_body(sums, tail, w, att, stat, out):
    total = sums[...] + jnp.where(iota((S, WIDTH), 0) == S - 1, tail[0:1, :], 0.0)
    grad = dot_nt(total.astype(BF16), w[...]).astype(BF16)
    out[0:S, :] = grad
    weighed = grad.astype(F32) * att[...]
    for h in range(H):
        cols = slice(h * E, (h + 1) * E)
        delta = jnp.sum(jnp.transpose(weighed[:, cols]), axis=0, keepdims=True)
        rows = [*split3(stat[0:1, cols]), *split3(stat[1:2, cols]), *split3(delta)]
        rows = [row.astype(F32) for row in rows] + [jnp.zeros((7, E), F32)]
        out[S : S + 16, cols] = jnp.concatenate(rows, axis=0).astype(BF16)


def mid_cotangent(sums, tail, w, att, stat):
    return pl.pallas_call(
        mid_cot_body,
        out_shape=jax.ShapeDtypeStruct((S + 16, WIDTH), BF16),
        cost_estimate=pl.CostEstimate(flops=600_000_000, bytes_accessed=4_000_000, transcendentals=0),
        name="mid_cotangent",
    )(sums, tail, w, att, stat)


def mid_bwd_body(flag, p4, p3, p2, first, second, p0, *refs):
    ms = [ref[F:CQ, :] for ref in refs[0:3]] + [ref[...] for ref in refs[3:5]]
    gs = refs[5:10]
    dq, dk, dv, back, fore = refs[10:]
    pays = pair_slabs(flag, p4, p3, p2, first, second, p0)

    @pl.when(pl.program_id(0) == 0)
    def _():
        mine = p0[2 * S : 2 * S + 16, :].astype(F32)[0:1]
        column = to_column(mine, S)
        causal = iota((S, S), 1) >= iota((S, S), 0)
        for n, pay in enumerate(pays):
            ok = to_column(pay[2 * S : 2 * S + 16].astype(F32)[0:1], S) == mine
            if n == REACH:
                ok = ok & causal
            back[n * S : (n + 1) * S, :] = jnp.where(ok, 0.0, NEG)
        for n, pay in enumerate(ms):
            ok = column == pay[S : S + 16].astype(F32)[0:1]
            if n == 0:
                ok = ok & causal
            fore[:, n * S : (n + 1) * S] = jnp.where(ok, 0.0, NEG)

    def stats(ref):
        rows = ref[S : S + 16, :].astype(F32)
        return [rows[j : j + 1] + rows[j + 1 : j + 2] + rows[j + 2 : j + 3] for j in (0, 3, 6)]

    k = p0[0:S, :]
    v = p0[S : 2 * S, :]
    keys = jnp.concatenate([pay[0:S] for pay in pays], axis=0)
    values = jnp.concatenate([pay[S : 2 * S] for pay in pays], axis=0)
    peak, inv, delta = stats(gs[0])
    scores = dot_nt(keys, ms[0][0:S]) * LOG2 + back[...]
    probs = jnp.exp2(scores - peak) * inv
    grads = (probs * (dot_nt(values, gs[0][0:S, :]) - delta)).astype(BF16)
    dq[...] = (dot_tn(grads, keys) * SCALE).astype(BF16)
    queries = jnp.concatenate([one[0:S] for one in ms], axis=0)
    cots = jnp.concatenate([ref[0:S, :] for ref in gs], axis=0)
    every = [stats(ref) for ref in gs]
    peak, inv, delta = (jnp.concatenate([one[j] for one in every], axis=1) for j in range(3))
    scores = dot_nt(k, queries) * LOG2 + fore[...]
    probs = jnp.exp2(scores - peak) * inv
    grads = (probs * (dot_nt(v, cots) - delta)).astype(BF16)
    dk[...] = (dot_nn(grads, queries) * SCALE).astype(BF16)
    dv[...] = dot_nn(probs.astype(BF16), cots).astype(BF16)


def mid_backward(flag, pays, ms, gs):
    return pl.pallas_call(
        mid_bwd_body,
        grid=(H,),
        in_specs=[FLAG] + PAY_SPECS + [head_spec(CQ)] * 3 + [head_spec(S + 16)] * 7,
        out_specs=[head_spec(S)] * 3,
        out_shape=[jax.ShapeDtypeStruct((S, WIDTH), BF16)] * 3,
        scratch_shapes=[pltpu.VMEM((SPAN_M, S), F32), pltpu.VMEM((S, SPAN_M), F32)],
        cost_estimate=pl.CostEstimate(flops=3_000_000_000, bytes_accessed=6_000_000, transcendentals=0),
        name="mid_backward",
    )(flag, *pays, *ms, *gs)


def shift(value, steps):
    count = lax.axis_size("ctx")
    first, last = max(0, -steps), min(count, count - steps)
    return lax.ppermute(value, "ctx", [(n, n + steps) for n in range(first, last)])


def swap(value, axis, bit):
    count = lax.axis_size(axis)
    return lax.ppermute(value, axis, [(n, n ^ bit) for n in range(count)])


def together(*values):
    return lax.optimization_barrier(values)


def block(value, index, rows):
    return lax.dynamic_slice_in_dim(value, index * rows, rows, 0)


X_GROUPS = [[first + 16 * n for n in range(4)] for first in range(16)]
YZ_GROUPS = [[16 * first + n for n in range(16)] for first in range(4)]


def exchange(value, axis, groups):
    return lax.all_to_all(value, axis, 0, 0, axis_index_groups=groups, tiled=True)


def shards(q_mid, k_mid, v_mid, doc_ids, q_full, k_full, v_base, w_link, cotangent):
    place = lax.axis_index("ctx")
    upper = place % 2 == 1
    flag = (place % 2).astype(jnp.int32).reshape(1)
    q_m, q_f, k_f = q_mid[0], q_full[0], k_full[0]
    ids = jnp.broadcast_to(jnp.tile((doc_ids + 1).astype(BF16), (1, 2)), (16, 2 * S))
    own_kv, own_cq, swap_a = pack(flag, q_m, k_mid[0], v_mid[0], ids, q_f, cotangent[0])

    kv2 = shift(own_kv, 2)
    got_a = swap(swap_a, "ctx", 1)
    qf2 = shift(q_f, -2)
    late_cq, qf2, kv2, got_a = together(own_cq, qf2, kv2, got_a)
    swap_b = jnp.concatenate([jnp.where(upper, kv2, qf2[:KV]), qf2[KV:]], axis=0)
    got_b = swap(swap_b, "ctx", 1)
    kv4 = shift(kv2, 2)
    kv2, kv4 = together(kv2, kv4)
    kv3 = swap(jnp.where(upper, kv4, kv2), "ctx", 1)
    cq2 = shift(late_cq, -2)
    cq2, kv3_late = together(cq2, kv3)
    cq1 = swap(jnp.where(upper, late_cq, cq2), "ctx", 1)

    pays = (kv4, kv3, kv2, got_a, got_b, own_kv)
    mid_ext, attended, mid_stat = mid_forward(flag, q_m, pays)
    values, s0, s2 = full_stats(k_f, v_base[0], mid_ext, w_link, q_f, qf2, late_cq, cq2)
    up2, up1_far = shift(s2, 2), shift(s2, 1)
    down2, down1_far = shift(s0, -2), shift(s0, -1)
    s1 = next_stats(flag, k_f, values, got_b, got_a, late_cq, cq1)
    up1, down1 = shift(s1, 1), shift(s1, -1)

    qm2, s1 = together(cq2[F:], s1)
    qm4 = shift(qm2, -2)
    qm3 = swap(jnp.where(upper, qm2, qm4), "ctx", 1)
    qs, cs = (q_f, got_b, got_a, qf2), (late_cq, cq1, cq2)
    dk_f, dv_f, dq0, dq1, dq2, sums, sum_ext, tail = full_grads(
        flag, k_f, values, qs, cs, (s0, s1, s2, up1, up1_far, up2, down1, down1_far, down2)
    )

    next_tail = shift(tail, -1)
    near = swap(dq1, "ctx", 1)
    parts = [jnp.concatenate([sum_ext, mid_ext[:, n * 256 : (n + 1) * 256]], axis=1) for n in range(4)]
    parts = exchange(jnp.concatenate(parts, axis=0), "ctx", X_GROUPS)
    sums, parts = together(sums, parts)
    cot_m = mid_cotangent(sums, next_tail, w_link, attended, mid_stat)
    g2 = shift(cot_m, -2)
    term = dot_tn(parts[:, WIDTH:], parts[:, :WIDTH]).astype(BF16)
    term, g2, near = together(term, g2, near)
    g1 = swap(jnp.where(upper, cot_m, g2), "ctx", 1)
    g4 = shift(g2, -2)
    total = jnp.sum(exchange(term, "ctx", YZ_GROUPS).astype(F32).reshape(16, 16, WIDTH), axis=0)
    total, g4 = together(total, g4)
    g3 = swap(jnp.where(upper, g2, g4), "ctx", 1)
    every = exchange(jnp.concatenate([total] * 4, axis=0), "dp", None)
    factor = float(lax.axis_size("dp") * lax.axis_size("ctx") * F) ** (-0.5)
    grad_link = jnp.sum(every.reshape(4, 16, WIDTH), axis=0) * factor
    pays = (kv4, kv3_late, kv2, got_a, got_b, own_kv)
    dq_m, dk_m, dv_m = mid_backward(flag, pays, (late_cq, cq1, cq2, qm3, qm4), (cot_m, g1, g2, g3, g4))

    near = near.astype(F32)
    passed = jnp.where(upper, dq2.astype(F32), dq2.astype(F32) + near)
    far = shift(passed.astype(BF16), 2).astype(F32)
    dq_f = (dq0 + far + jnp.where(upper, near, 0.0)).astype(BF16)
    return (dq_m[None], dk_m[None], dv_m[None], dq_f[None], dk_f[None], dv_f[None], grad_link)


def solution(mesh):
    rows = P("dp", "ctx", None)
    return jax.shard_map(
        shards,
        mesh=mesh,
        in_specs=(rows, rows, rows, P("dp", "ctx"), rows, rows, rows, P(), rows),
        out_specs=(rows,) * 6 + (P("ctx", None),),
        check_vma=False,
    )
```

```python
import math

import jax
import jax.numpy as jnp
from jax import lax
from jax.experimental import pallas as pl
from jax.experimental.pallas import tpu as pltpu
from jax.sharding import PartitionSpec as P

H = 8
E = 128
S = 128
F = 384
REACH = 4
FREACH = 2
WIDTH = H * E
SPAN_M = (REACH + 1) * S
SPAN_F = (FREACH + 1) * F
WIN = FREACH * F
KV = 2 * S + 32
CQ = F + S + 16
TILES = F // S
TILE_W = WIN + S
STEP = 2
SCALE = E ** (-0.5)
LOG2 = SCALE * math.log2(math.e)
NEG = -1e30
F32 = jnp.float32
BF16 = jnp.bfloat16


def dot_nn(a, b):
    return lax.dot_general(a, b, (((1,), (0,)), ((), ())), preferred_element_type=F32)


def dot_nt(a, b):
    return lax.dot_general(a, b, (((1,), (1,)), ((), ())), preferred_element_type=F32)


def dot_tn(a, b):
    return lax.dot_general(a, b, (((0,), (0,)), ((), ())), preferred_element_type=F32)


def iota(shape, axis):
    return lax.broadcasted_iota(jnp.int32, shape, axis)


def to_column(row, size):
    return jnp.transpose(jnp.broadcast_to(row, (size, size)))


def split3(x):
    hi = x.astype(BF16)
    rest = x - hi.astype(F32)
    mid = rest.astype(BF16)
    return hi, mid, (rest - mid.astype(F32)).astype(BF16)


def head_spec(rows):
    return pl.BlockSpec((rows, STEP * E), lambda h: (0, h))


def by_head(body, in_specs, out_specs):
    split = [spec.block_shape is not None and spec.block_shape[-1] in (STEP * E, pl.Element(STEP * E)) for spec in in_specs + out_specs]

    def run(*refs):
        for sub in range(STEP):
            views = [ref.at[:, pl.ds(sub * E, E)] if cut else ref for ref, cut in zip(refs, split)]
            body(sub, pl.program_id(0) * STEP + sub, *views, *refs[len(split) :])

    return run


def call(body, name, flops, bytes_accessed, in_specs, out_specs, out_shape, scratch_shapes):
    return pl.pallas_call(
        by_head(body, in_specs, out_specs),
        grid=(H // STEP,),
        in_specs=in_specs,
        out_specs=out_specs,
        out_shape=out_shape,
        scratch_shapes=scratch_shapes,
        cost_estimate=pl.CostEstimate(flops=flops, bytes_accessed=bytes_accessed, transcendentals=0),
        name=name,
    )


def on_first(sub):
    return pl.when(pl.program_id(0) == 0) if sub == 0 else lambda build: None


def on_last(sub):
    return pl.when(pl.program_id(0) == H // STEP - 1) if sub == STEP - 1 else lambda build: None


def whole_spec(shape):
    return pl.BlockSpec(shape, lambda h: (0,) * len(shape))


def pack_body(flag, q, k, v, ids, qf, cot, kv, cq, first):
    kv[0:S, :] = k[...]
    kv[S : 2 * S, :] = v[...]
    kv[2 * S : 2 * S + 16, :] = ids[...]
    kv[2 * S + 16 : KV, :] = q[S - 16 : S, :]
    cq[0:F, :] = cot[...]
    cq[F : F + S, :] = q[...]
    cq[F + S : CQ, :] = ids[...]
    first[...] = qf[...]

    @pl.when(flag[0] == 0)
    def _():
        first[0:KV, :] = kv[...]


def pack(flag, q, k, v, ids, qf, cot):
    def wide(rows):
        return pl.BlockSpec((rows, 2 * E), lambda h: (0, h))

    return pl.pallas_call(
        pack_body,
        grid=(H // 2,),
        in_specs=[FLAG] + [wide(S)] * 3 + [whole_spec((16, 2 * E)), wide(F), wide(F)],
        out_specs=[wide(KV), wide(CQ), wide(F)],
        out_shape=[
            jax.ShapeDtypeStruct((KV, WIDTH), BF16),
            jax.ShapeDtypeStruct((CQ, WIDTH), BF16),
            jax.ShapeDtypeStruct((F, WIDTH), BF16),
        ],
        name="pack",
    )(flag, q, k, v, ids, qf, cot)


def pick(flag, upper, lower, rows):
    return jnp.where(flag[0] == 1, upper[0:rows, :], lower[0:rows, :])


def pair_slabs(flag, p4, p3, p2, first, second, p0):
    near = pick(flag, first, second, KV)
    return [p4[...], p3[...], p2[...], near, p0[...]]


def mid_fwd_body(sub, head, flag, q, p4, p3, p2, first, second, p0, out, att, stat, bias):
    pays = pair_slabs(flag, p4, p3, p2, first, second, p0)

    @on_first(sub)
    def _():
        def ids(n):
            return pays[n][2 * S : 2 * S + 16].astype(F32)[0:1]

        mine = to_column(ids(REACH), S)
        edge = to_column(ids(REACH - 1), S)[S - 16 : S]
        for n in range(REACH + 1):
            cols = slice(n * S, (n + 1) * S)
            ok = mine == ids(n)
            ok_edge = edge == ids(n)
            if n == REACH:
                ok = ok & (iota((S, S), 0) >= iota((S, S), 1))
                ok_edge = ok_edge & (iota((16, S), 1) < 0)
            if n == REACH - 1:
                ok_edge = ok_edge & (iota((16, S), 0) + (S - 16) >= iota((16, S), 1))
            bias[0:S, cols] = jnp.where(ok, 0.0, NEG)
            bias[S : S + 16, cols] = jnp.where(ok_edge, 0.0, NEG)

    keys = jnp.concatenate([pay[0:S] for pay in pays], axis=0)
    values = jnp.concatenate([pay[S : 2 * S] for pay in pays], axis=0)
    queries = jnp.concatenate([q[...], pays[REACH - 1][2 * S + 16 : KV]], axis=0)
    scores = dot_nt(queries, keys) * LOG2 + bias[...]
    peak = jnp.max(scores, axis=1, keepdims=True)
    expo = jnp.exp2(scores - peak)
    inv = 1.0 / jnp.sum(expo, axis=1, keepdims=True)
    attended = dot_nn((expo * inv).astype(BF16), values)
    att[...] = attended[0:S]
    out[...] = attended.astype(BF16)
    stat[0:1, :] = jnp.transpose(jnp.broadcast_to(peak[0:S], (S, S)))[0:1]
    stat[1:2, :] = jnp.transpose(jnp.broadcast_to(inv[0:S], (S, S)))[0:1]
    stat[2:8, :] = jnp.zeros((6, S), F32)


def mid_forward(flag, q, pays):
    return call(
        mid_fwd_body,
        "mid_forward",
        700_000_000,
        4_000_000,
        in_specs=[FLAG, head_spec(S)] + PAY_SPECS,
        out_specs=[head_spec(S + 16), head_spec(S), head_spec(8)],
        out_shape=[
            jax.ShapeDtypeStruct((S + 16, WIDTH), BF16),
            jax.ShapeDtypeStruct((S, WIDTH), F32),
            jax.ShapeDtypeStruct((8, WIDTH), F32),
        ],
        scratch_shapes=[pltpu.VMEM((S + 16, SPAN_M), F32)],
    )(flag, q, *pays)


FLAG = pl.BlockSpec(memory_space=pltpu.SMEM)
PAY_SPECS = [head_spec(KV)] * 3 + [head_spec(F)] * 2 + [head_spec(KV)]


def full_mask(bias, docs):
    spread = (iota((S, F), 1) // 3 == iota((S, F), 0)).astype(BF16)
    spread_t = (iota((F, S), 0) // 3 == iota((F, S), 1)).astype(BF16)
    rows = jnp.concatenate(
        [dot_nn(jnp.broadcast_to(d, (16, S)), spread)[0:1] for d in docs], axis=1
    )
    column = dot_nn(spread_t, to_column(docs[0].astype(F32), S).astype(BF16))
    for t in range(TILES):
        lo = t * S
        mine = jnp.concatenate([column[lo : lo + S]] * (TILE_W // S), axis=1)
        gap = iota((S, TILE_W), 1) - iota((S, TILE_W), 0)
        ok = (mine == rows[:, lo : lo + TILE_W]) & (gap >= 0) & (gap < WIN)
        bias[t] = jnp.where(ok, 0.0, NEG)


DOCS = pl.BlockSpec((16, S), lambda h: ((F + S) // 16, 0))


def doc_row(ref):
    return ref[...][0:1]


def stats_body(sub, head, k, base, mid, w, q0, q2, c0, c2, d0, d2, values, s0, s2, bias, ext, part):
    @on_first(sub)
    def _():
        full_mask(bias, [doc_row(ref) for ref in (d0, d0, d2)])

    linked = dot_nn(mid[...], w[...])
    for n in range(2, 5):
        ext[pl.ds(n, S, stride=3), :] = linked[0:S]
    ext[0:2, :] = jnp.broadcast_to(linked[S + 15 : S + 16], (2, E))
    v = (base[...].astype(F32) + ext[0:F, :]).astype(BF16)
    values[...] = v
    for t in range(TILES):
        lo, first, last = t * S, F - t * S, (t + 1) * S
        queries = jnp.concatenate([q0[lo:F, :], q2[0:last, :]], axis=0)
        cots = jnp.concatenate([c0[lo:F, :], c2[0:last, :]], axis=0)
        mask = jnp.concatenate([bias[t, :, 0:first], bias[t, :, first + F : first + F + last]], axis=1)
        rows = partial_stats(k[lo : lo + S, :], v[lo : lo + S], queries, cots, mask)
        for j, empty in enumerate((NEG, 0.0, 0.0)):
            pieces = [jnp.full((1, lo), empty, F32)] if lo else []
            pieces += [rows[j]] + ([jnp.full((1, F - last), empty, F32)] if last < F else [])
            part[t, pl.ds(j * H + head, 1), :] = jnp.concatenate(pieces, axis=1)

    @on_last(sub)
    def _():
        for out, cols in ((s0, slice(0, F)), (s2, slice(F, 2 * F))):
            merge_into(out, part, cols)


def partial_stats(k, v, queries, cots, mask):
    scores = dot_nt(k, queries) * LOG2 + mask
    peak = jnp.max(scores, axis=0, keepdims=True)
    expo = jnp.exp2(scores - peak)
    dots = dot_nt(v, cots)
    return peak, jnp.sum(expo, axis=0, keepdims=True), jnp.sum(expo * dots, axis=0, keepdims=True)


def merge_into(out, part, cols):
    merged = merge([tuple(part[t, j * H : (j + 1) * H, cols] for j in range(3)) for t in range(TILES)])
    for j in range(3):
        out[j * H : (j + 1) * H, :] = merged[j]


def stats_next_body(sub, head, flag, k, v, q1a, q1b, c1, d0, d1, s1, bias, part):
    @on_first(sub)
    def _():
        full_mask(bias, [doc_row(ref) for ref in (d0, d1, d1)])

    queries = pick(flag, q1a, q1b, F)
    for t in range(TILES):
        lo = t * S
        mask = bias[t, :, F - lo : 2 * F - lo]
        rows = partial_stats(k[lo : lo + S, :], v[lo : lo + S, :], queries, c1[0:F, :], mask)
        for j in range(3):
            part[t, pl.ds(j * H + head, 1), :] = rows[j]

    @on_last(sub)
    def _():
        merge_into(s1, part, slice(0, F))


def merge(parts):
    peak = parts[0][0]
    for part in parts[1:]:
        peak = jnp.maximum(peak, part[0])
    total, dots = 0.0, 0.0
    for part in parts:
        factor = jnp.exp2(part[0] - peak)
        total = total + part[1] * factor
        dots = dots + part[2] * factor
    return peak, total, dots


def full_stats(k, base, mid, w, q0, q2, c0, c2):
    stat = jax.ShapeDtypeStruct((3 * H, F), F32)
    return call(
        stats_body,
        "full_stats",
        2_000_000_000,
        8_000_000,
        in_specs=[head_spec(F), head_spec(F), whole_spec((S + 16, WIDTH)), head_spec(WIDTH)]
        + [head_spec(F)] * 4
        + [DOCS] * 2,
        out_specs=[head_spec(F)] + [whole_spec((3 * H, F))] * 2,
        out_shape=[jax.ShapeDtypeStruct((F, WIDTH), BF16), stat, stat],
        scratch_shapes=[
            pltpu.VMEM((TILES, S, TILE_W), F32),
            pltpu.VMEM((400, E), F32),
            pltpu.VMEM((TILES, 3 * H, 2 * F), F32),
        ],
    )(k, base, mid, w, q0, q2, c0, c2, c0, c2)


def next_stats(flag, k, v, q1a, q1b, c0, c1):
    return call(
        stats_next_body,
        "next_stats",
        1_000_000_000,
        6_000_000,
        in_specs=[FLAG] + [head_spec(F)] * 5 + [DOCS] * 2,
        out_specs=[whole_spec((3 * H, F))],
        out_shape=[jax.ShapeDtypeStruct((3 * H, F), F32)],
        scratch_shapes=[
            pltpu.VMEM((TILES, S, TILE_W), F32),
            pltpu.VMEM((TILES, 3 * H, F), F32),
        ],
    )(flag, k, v, q1a, q1b, c1, c0, c1)[0]


def grads_body(
    sub, head, flag, k, v, q0, q1a, q1b, q2, c0, c1, c2, d0, d1, d2, s0, s1, s2, up1, up1_far, up2, down1, down1_far, down2,
    dk, dv, dq0, dq1, dq2, sums, link, tail, bias, ext, glob, kept,
):
    @on_first(sub)
    def _():
        full_mask(bias, [doc_row(ref) for ref in (d0, d1, d2)])

        def triple(ref):
            peak, total, dots = (ref[j * H : (j + 1) * H, :] for j in range(3))
            return jnp.where(total > 0.0, peak, NEG), total, dots

        for n, group in enumerate(((s0, up1, up2), (s1, up1_far, down1_far), (s2, down1, down2))):
            cols = slice(n * F, (n + 1) * F)
            peak, total, dots = merge([triple(ref) for ref in group])
            inv = jnp.where(total > 0.0, 1.0 / total, 0.0)
            glob[0:H, cols] = peak
            glob[H : 2 * H, cols] = inv
            glob[2 * H : 3 * H, cols] = dots * inv
        kept[...] = jnp.zeros((F, SPAN_F), BF16)
        ext[F:400, :] = jnp.zeros((400 - F, E), F32)

    queries = jnp.concatenate([q0[...], pick(flag, q1a, q1b, F), q2[...]], axis=0)
    cots = jnp.concatenate([c0[0:F, :], c1[0:F, :], c2[0:F, :]], axis=0)
    for t in range(TILES):
        lo = t * S
        cols = slice(lo, lo + TILE_W)
        scores = dot_nt(k[lo : lo + S, :], queries[cols]) * LOG2 + bias[t]
        probs = jnp.exp2(scores - glob[pl.ds(head, 1), cols]) * glob[pl.ds(H + head, 1), cols]
        dots = dot_nt(v[lo : lo + S, :], cots[cols])
        grads = (probs * (dots - glob[pl.ds(2 * H + head, 1), cols])).astype(BF16)
        kept[lo : lo + S, cols] = grads
        dk[lo : lo + S, :] = (dot_nn(grads, queries[cols]) * SCALE).astype(BF16)
        grad_v = dot_nn(probs.astype(BF16), cots[cols]).astype(BF16)
        dv[lo : lo + S, :] = grad_v
        ext[lo : lo + S, :] = grad_v.astype(F32)
    for n, out in enumerate((dq0, dq1, dq2)):
        part = dot_tn(kept[:, n * F : (n + 1) * F], k[...]) * SCALE
        out[...] = part.astype(out.dtype)
    total = ext[pl.ds(2, S, stride=3), :] + ext[pl.ds(3, S, stride=3), :] + ext[pl.ds(4, S, stride=3), :]
    sums[...] = total
    first = ext[0:1, :] + ext[1:2, :]
    tail[...] = jnp.broadcast_to(first, (8, E))
    link[0:S, :] = total.astype(BF16)
    link[S : S + 16, :] = jnp.where(iota((16, E), 0) == 15, first, 0.0).astype(BF16)


def full_grads(flag, k, v, qs, cs, stats):
    return call(
        grads_body,
        "full_grads",
        8_000_000_000,
        14_000_000,
        in_specs=[FLAG, head_spec(F), head_spec(F)]
        + [head_spec(F)] * 7
        + [DOCS] * 3
        + [whole_spec(s.shape) for s in stats],
        out_specs=[head_spec(F)] * 5 + [head_spec(S), head_spec(S + 16), head_spec(8)],
        out_shape=[
            jax.ShapeDtypeStruct((F, WIDTH), BF16),
            jax.ShapeDtypeStruct((F, WIDTH), BF16),
            jax.ShapeDtypeStruct((F, WIDTH), F32),
            jax.ShapeDtypeStruct((F, WIDTH), BF16),
            jax.ShapeDtypeStruct((F, WIDTH), BF16),
            jax.ShapeDtypeStruct((S, WIDTH), F32),
            jax.ShapeDtypeStruct((S + 16, WIDTH), BF16),
            jax.ShapeDtypeStruct((8, WIDTH), F32),
        ],
        scratch_shapes=[
            pltpu.VMEM((TILES, S, TILE_W), F32),
            pltpu.VMEM((400, E), F32),
            pltpu.VMEM((3 * H, SPAN_F), F32),
            pltpu.VMEM((F, SPAN_F), BF16),
        ],
    )(flag, k, v, *qs, *cs, *cs, *stats)


def mid_cot_body(sub, head, w, att, stat, sums, tail, out, whole):
    @on_first(sub)
    def _():
        total = sums[...] + jnp.where(iota((S, WIDTH), 0) == S - 1, tail[0:1, :], 0.0)
        whole[...] = total.astype(BF16)

    grad = dot_nt(whole[...], w[...]).astype(BF16)
    out[0:S, :] = grad
    delta = jnp.sum(jnp.transpose(grad.astype(F32) * att[...]), axis=0, keepdims=True)
    rows = [*split3(stat[0:1, :]), *split3(stat[1:2, :]), *split3(delta)]
    rows = [row.astype(F32) for row in rows] + [jnp.zeros((7, E), F32)]
    out[S : S + 16, :] = jnp.concatenate(rows, axis=0).astype(BF16)


def mid_cotangent(sums, tail, w, att, stat):
    body = mid_cot_body

    def run(w_ref, *refs):
        for sub in range(STEP):
            cols = pl.ds(sub * E, E)
            att_ref, stat_ref, sums_ref, tail_ref, out_ref, whole = refs
            body(
                sub, None, w_ref.at[cols, :], att_ref.at[:, cols], stat_ref.at[:, cols],
                sums_ref, tail_ref, out_ref.at[:, cols], whole,
            )

    return pl.pallas_call(
        run,
        grid=(H // STEP,),
        in_specs=[
            pl.BlockSpec((STEP * E, WIDTH), lambda h: (h, 0)),
            head_spec(S),
            head_spec(8),
            whole_spec((S, WIDTH)),
            whole_spec((8, WIDTH)),
        ],
        out_specs=head_spec(S + 16),
        out_shape=jax.ShapeDtypeStruct((S + 16, WIDTH), BF16),
        scratch_shapes=[pltpu.VMEM((S, WIDTH), BF16)],
        cost_estimate=pl.CostEstimate(flops=600_000_000, bytes_accessed=4_000_000, transcendentals=0),
        name="mid_cotangent",
    )(w, att, stat, sums, tail)


def mid_bwd_body(sub, head, flag, p4, p3, p2, first, second, p0, *refs):
    ms = [ref[...] for ref in refs[0:5]]
    gs = refs[5:10]
    dq, dk, dv, back, fore = refs[10:]
    pays = pair_slabs(flag, p4, p3, p2, first, second, p0)

    @on_first(sub)
    def _():
        mine = p0[2 * S : 2 * S + 16, :].astype(F32)[0:1]
        column = to_column(mine, S)
        causal = iota((S, S), 1) >= iota((S, S), 0)
        for n, pay in enumerate(pays):
            ok = to_column(pay[2 * S : 2 * S + 16].astype(F32)[0:1], S) == mine
            if n == REACH:
                ok = ok & causal
            back[n * S : (n + 1) * S, :] = jnp.where(ok, 0.0, NEG)
        for n, pay in enumerate(ms):
            ok = column == pay[S : S + 16].astype(F32)[0:1]
            if n == 0:
                ok = ok & causal
            fore[:, n * S : (n + 1) * S] = jnp.where(ok, 0.0, NEG)

    def stats(ref):
        rows = ref[S : S + 16, :].astype(F32)
        return [rows[j : j + 1] + rows[j + 1 : j + 2] + rows[j + 2 : j + 3] for j in (0, 3, 6)]

    k = p0[0:S, :]
    v = p0[S : 2 * S, :]
    keys = jnp.concatenate([pay[0:S] for pay in pays], axis=0)
    values = jnp.concatenate([pay[S : 2 * S] for pay in pays], axis=0)
    peak, inv, delta = stats(gs[0])
    scores = dot_nt(keys, ms[0][0:S]) * LOG2 + back[...]
    probs = jnp.exp2(scores - peak) * inv
    grads = (probs * (dot_nt(values, gs[0][0:S, :]) - delta)).astype(BF16)
    dq[...] = (dot_tn(grads, keys) * SCALE).astype(BF16)
    queries = jnp.concatenate([one[0:S] for one in ms], axis=0)
    cots = jnp.concatenate([ref[0:S, :] for ref in gs], axis=0)
    every = [stats(ref) for ref in gs]
    peak, inv, delta = (jnp.concatenate([one[j] for one in every], axis=1) for j in range(3))
    scores = dot_nt(k, queries) * LOG2 + fore[...]
    probs = jnp.exp2(scores - peak) * inv
    grads = (probs * (dot_nt(v, cots) - delta)).astype(BF16)
    dk[...] = (dot_nn(grads, queries) * SCALE).astype(BF16)
    dv[...] = dot_nn(probs.astype(BF16), cots).astype(BF16)


QUERY_ROWS = pl.BlockSpec((pl.Element(S + 16), pl.Element(STEP * E)), lambda h: (F, h * STEP * E))


def mid_backward(flag, pays, ms, gs):
    return call(
        mid_bwd_body,
        "mid_backward",
        3_000_000_000,
        6_000_000,
        in_specs=[FLAG] + PAY_SPECS + [QUERY_ROWS] * 3 + [head_spec(S + 16)] * 7,
        out_specs=[head_spec(S)] * 3,
        out_shape=[jax.ShapeDtypeStruct((S, WIDTH), BF16)] * 3,
        scratch_shapes=[pltpu.VMEM((SPAN_M, S), F32), pltpu.VMEM((S, SPAN_M), F32)],
    )(flag, *pays, *ms, *gs)


def shift(value, steps):
    count = lax.axis_size("ctx")
    first, last = max(0, -steps), min(count, count - steps)
    return lax.ppermute(value, "ctx", [(n, n + steps) for n in range(first, last)])


def swap(value, axis, bit):
    count = lax.axis_size(axis)
    return lax.ppermute(value, axis, [(n, n ^ bit) for n in range(count)])


def together(*values):
    return lax.optimization_barrier(values)


def block(value, index, rows):
    return lax.dynamic_slice_in_dim(value, index * rows, rows, 0)


X_GROUPS = [[first + 16 * n for n in range(4)] for first in range(16)]
YZ_GROUPS = [[16 * first + n for n in range(16)] for first in range(4)]


def exchange(value, axis, groups):
    return lax.all_to_all(value, axis, 0, 0, axis_index_groups=groups, tiled=True)


def shards(q_mid, k_mid, v_mid, doc_ids, q_full, k_full, v_base, w_link, cotangent):
    place = lax.axis_index("ctx")
    upper = place % 2 == 1
    flag = (place % 2).astype(jnp.int32).reshape(1)
    q_m, q_f, k_f = q_mid[0], q_full[0], k_full[0]
    ids = jnp.broadcast_to(jnp.tile((doc_ids + 1).astype(BF16), (1, 2)), (16, 2 * S))
    own_kv, own_cq, swap_a = pack(flag, q_m, k_mid[0], v_mid[0], ids, q_f, cotangent[0])

    kv2 = shift(own_kv, 2)
    got_a = swap(swap_a, "ctx", 1)
    qf2 = shift(q_f, -2)
    late_cq, qf2, kv2, got_a = together(own_cq, qf2, kv2, got_a)
    swap_b = jnp.concatenate([jnp.where(upper, kv2, qf2[:KV]), qf2[KV:]], axis=0)
    got_b = swap(swap_b, "ctx", 1)
    kv4 = shift(kv2, 2)
    kv2, kv4 = together(kv2, kv4)
    kv3 = swap(jnp.where(upper, kv4, kv2), "ctx", 1)
    cq2 = shift(late_cq, -2)
    cq2, got_b_late, kv3_late = together(cq2, got_b, kv3)
    cq1 = swap(jnp.where(upper, late_cq, cq2), "ctx", 1)

    pays = (kv4, kv3, kv2, got_a, got_b, own_kv)
    mid_ext, attended, mid_stat = mid_forward(flag, q_m, pays)
    qm2 = cq2[F:]
    qm4, mid_ext = together(shift(qm2, -2), mid_ext)
    values, s0, s2 = full_stats(k_f, v_base[0], mid_ext, w_link, q_f, qf2, late_cq, cq2)
    up2, up1_far = shift(s2, 2), shift(s2, 1)
    down2, down1_far = shift(s0, -2), shift(s0, -1)
    s1 = next_stats(flag, k_f, values, got_b_late, got_a, late_cq, cq1)
    up1, down1 = shift(s1, 1), shift(s1, -1)

    qm3 = swap(jnp.where(upper, qm2, qm4), "ctx", 1)
    values, qm3 = together(values, qm3)
    qs, cs = (q_f, got_b_late, got_a, qf2), (late_cq, cq1, cq2)
    dk_f, dv_f, dq0, dq1, dq2, sums, sum_ext, tail = full_grads(
        flag, k_f, values, qs, cs, (s0, s1, s2, up1, up1_far, up2, down1, down1_far, down2)
    )

    sums, next_tail, sum_ext, dq1, dq2 = together(sums, shift(tail, -1), sum_ext, dq1, dq2)
    cot_m = mid_cotangent(sums, next_tail, w_link, attended, mid_stat)
    cot_m, sum_ext, dq1, dq2 = together(cot_m, sum_ext, dq1, dq2)
    g2 = shift(cot_m, -2)
    near, far = shift(dq1, 1), shift(dq2, 2)
    parts = [jnp.concatenate([sum_ext, mid_ext[:, n * 256 : (n + 1) * 256]], axis=1) for n in range(4)]
    parts = exchange(jnp.concatenate(parts, axis=0), "ctx", X_GROUPS)
    term = dot_tn(parts[:, WIDTH:], parts[:, :WIDTH]).astype(BF16)
    term, g2 = together(term, g2)
    g1 = swap(jnp.where(upper, cot_m, g2), "ctx", 1)
    g4 = shift(g2, -2)
    total = jnp.sum(exchange(term, "ctx", YZ_GROUPS).astype(F32).reshape(16, 16, WIDTH), axis=0)
    g2_late, g4 = together(g2, g4)
    g3 = swap(jnp.where(upper, g2_late, g4), "ctx", 1)
    every = exchange(jnp.concatenate([total] * 4, axis=0), "dp", None)
    factor = float(lax.axis_size("dp") * lax.axis_size("ctx") * F) ** (-0.5)
    grad_link = jnp.sum(every.reshape(4, 16, WIDTH), axis=0) * factor
    pays = (kv4, kv3_late, kv2, got_a, got_b, own_kv)
    dq_m, dk_m, dv_m = mid_backward(flag, pays, (late_cq, cq1, cq2, qm3, qm4), (cot_m, g1, g2, g3, g4))

    dq_f = (dq0 + far.astype(F32) + near.astype(F32)).astype(BF16)
    return (dq_m[None], dk_m[None], dv_m[None], dq_f[None], dk_f[None], dv_f[None], grad_link)


def solution(mesh):
    rows = P("dp", "ctx", None)
    return jax.shard_map(
        shards,
        mesh=mesh,
        in_specs=(rows, rows, rows, P("dp", "ctx"), rows, rows, rows, P(), rows),
        out_specs=(rows,) * 6 + (P("ctx", None),),
        check_vma=False,
    )
```

```python
import math

import jax
import jax.numpy as jnp
from jax import lax
from jax.experimental import pallas as pl
from jax.experimental.pallas import tpu as pltpu
from jax.sharding import PartitionSpec as P

H = 8
E = 128
S = 128
F = 384
REACH = 4
FREACH = 2
WIDTH = H * E
SPAN_M = (REACH + 1) * S
SPAN_F = (FREACH + 1) * F
WIN = FREACH * F
KV = 2 * S + 32
CQ = F + S + 16
TILES = F // S
TILE_W = WIN + S
STEP = 4
SCALE = E ** (-0.5)
LOG2 = SCALE * math.log2(math.e)
NEG = -1e30
F32 = jnp.float32
BF16 = jnp.bfloat16


def dot_nn(a, b):
    return lax.dot_general(a, b, (((1,), (0,)), ((), ())), preferred_element_type=F32)


def dot_nt(a, b):
    return lax.dot_general(a, b, (((1,), (1,)), ((), ())), preferred_element_type=F32)


def dot_tn(a, b):
    return lax.dot_general(a, b, (((0,), (0,)), ((), ())), preferred_element_type=F32)


def iota(shape, axis):
    return lax.broadcasted_iota(jnp.int32, shape, axis)


def to_column(row, size):
    return jnp.transpose(jnp.broadcast_to(row, (size, size)))


def split3(x):
    hi = x.astype(BF16)
    rest = x - hi.astype(F32)
    mid = rest.astype(BF16)
    return hi, mid, (rest - mid.astype(F32)).astype(BF16)


def head_spec(rows):
    return pl.BlockSpec((rows, STEP * E), lambda h: (0, h))


def by_head(body, in_specs, out_specs):
    split = [spec.block_shape is not None and spec.block_shape[-1] in (STEP * E, pl.Element(STEP * E)) for spec in in_specs + out_specs]

    def run(*refs):
        for sub in range(STEP):
            views = [ref.at[:, pl.ds(sub * E, E)] if cut else ref for ref, cut in zip(refs, split)]
            body(sub, pl.program_id(0) * STEP + sub, *views, *refs[len(split) :])

    return run


def call(body, name, flops, bytes_accessed, in_specs, out_specs, out_shape, scratch_shapes):
    return pl.pallas_call(
        by_head(body, in_specs, out_specs),
        grid=(H // STEP,),
        in_specs=in_specs,
        out_specs=out_specs,
        out_shape=out_shape,
        scratch_shapes=scratch_shapes,
        cost_estimate=pl.CostEstimate(flops=flops, bytes_accessed=bytes_accessed, transcendentals=0),
        name=name,
    )


def on_first(sub):
    return pl.when(pl.program_id(0) == 0) if sub == 0 else lambda build: None


def on_last(sub):
    return pl.when(pl.program_id(0) == H // STEP - 1) if sub == STEP - 1 else lambda build: None


def whole_spec(shape):
    return pl.BlockSpec(shape, lambda h: (0,) * len(shape))


def pack_body(flag, q, k, v, ids, qf, cot, kv, cq, first):
    kv[0:S, :] = k[...]
    kv[S : 2 * S, :] = v[...]
    kv[2 * S : 2 * S + 16, :] = ids[...]
    kv[2 * S + 16 : KV, :] = q[S - 16 : S, :]
    cq[0:F, :] = cot[...]
    cq[F : F + S, :] = q[...]
    cq[F + S : CQ, :] = ids[...]
    first[...] = qf[...]

    @pl.when(flag[0] == 0)
    def _():
        first[0:KV, :] = kv[...]


def pack(flag, q, k, v, ids, qf, cot):
    def wide(rows):
        return pl.BlockSpec((rows, 2 * E), lambda h: (0, h))

    return pl.pallas_call(
        pack_body,
        grid=(H // 2,),
        in_specs=[FLAG] + [wide(S)] * 3 + [whole_spec((16, 2 * E)), wide(F), wide(F)],
        out_specs=[wide(KV), wide(CQ), wide(F)],
        out_shape=[
            jax.ShapeDtypeStruct((KV, WIDTH), BF16),
            jax.ShapeDtypeStruct((CQ, WIDTH), BF16),
            jax.ShapeDtypeStruct((F, WIDTH), BF16),
        ],
        name="pack",
    )(flag, q, k, v, ids, qf, cot)


def pick(flag, upper, lower, rows):
    return jnp.where(flag[0] == 1, upper[0:rows, :], lower[0:rows, :])


def pair_slabs(flag, p4, p3, p2, first, second, p0):
    near = pick(flag, first, second, KV)
    return [p4[...], p3[...], p2[...], near, p0[...]]


def mid_fwd_body(sub, head, flag, q, p4, p3, p2, first, second, p0, out, att, stat, bias):
    pays = pair_slabs(flag, p4, p3, p2, first, second, p0)

    @on_first(sub)
    def _():
        def ids(n):
            return pays[n][2 * S : 2 * S + 16].astype(F32)[0:1]

        mine = to_column(ids(REACH), S)
        edge = to_column(ids(REACH - 1), S)[S - 16 : S]
        for n in range(REACH + 1):
            cols = slice(n * S, (n + 1) * S)
            ok = mine == ids(n)
            ok_edge = edge == ids(n)
            if n == REACH:
                ok = ok & (iota((S, S), 0) >= iota((S, S), 1))
                ok_edge = ok_edge & (iota((16, S), 1) < 0)
            if n == REACH - 1:
                ok_edge = ok_edge & (iota((16, S), 0) + (S - 16) >= iota((16, S), 1))
            bias[0:S, cols] = jnp.where(ok, 0.0, NEG)
            bias[S : S + 16, cols] = jnp.where(ok_edge, 0.0, NEG)

    keys = jnp.concatenate([pay[0:S] for pay in pays], axis=0)
    values = jnp.concatenate([pay[S : 2 * S] for pay in pays], axis=0)
    queries = jnp.concatenate([q[...], pays[REACH - 1][2 * S + 16 : KV]], axis=0)
    scores = dot_nt(queries, keys) * LOG2 + bias[...]
    peak = jnp.max(scores, axis=1, keepdims=True)
    expo = jnp.exp2(scores - peak)
    inv = 1.0 / jnp.sum(expo, axis=1, keepdims=True)
    attended = dot_nn((expo * inv).astype(BF16), values)
    att[...] = attended[0:S]
    out[...] = attended.astype(BF16)
    stat[0:1, :] = jnp.transpose(jnp.broadcast_to(peak[0:S], (S, S)))[0:1]
    stat[1:2, :] = jnp.transpose(jnp.broadcast_to(inv[0:S], (S, S)))[0:1]
    stat[2:8, :] = jnp.zeros((6, S), F32)


def mid_forward(flag, q, pays):
    return call(
        mid_fwd_body,
        "mid_forward",
        700_000_000,
        4_000_000,
        in_specs=[FLAG, head_spec(S)] + PAY_SPECS,
        out_specs=[head_spec(S + 16), head_spec(S), head_spec(8)],
        out_shape=[
            jax.ShapeDtypeStruct((S + 16, WIDTH), BF16),
            jax.ShapeDtypeStruct((S, WIDTH), F32),
            jax.ShapeDtypeStruct((8, WIDTH), F32),
        ],
        scratch_shapes=[pltpu.VMEM((S + 16, SPAN_M), F32)],
    )(flag, q, *pays)


FLAG = pl.BlockSpec(memory_space=pltpu.SMEM)
PAY_SPECS = [head_spec(KV)] * 3 + [head_spec(F)] * 2 + [head_spec(KV)]


def full_mask(bias, docs):
    spread = (iota((S, F), 1) // 3 == iota((S, F), 0)).astype(BF16)
    spread_t = (iota((F, S), 0) // 3 == iota((F, S), 1)).astype(BF16)
    rows = jnp.concatenate(
        [dot_nn(jnp.broadcast_to(d, (16, S)), spread)[0:1] for d in docs], axis=1
    )
    column = dot_nn(spread_t, to_column(docs[0].astype(F32), S).astype(BF16))
    for t in range(TILES):
        lo = t * S
        mine = jnp.concatenate([column[lo : lo + S]] * (TILE_W // S), axis=1)
        gap = iota((S, TILE_W), 1) - iota((S, TILE_W), 0)
        ok = (mine == rows[:, lo : lo + TILE_W]) & (gap >= 0) & (gap < WIN)
        bias[t] = jnp.where(ok, 0.0, NEG)


DOCS = pl.BlockSpec((16, S), lambda h: ((F + S) // 16, 0))


def doc_row(ref):
    return ref[...][0:1]


def stats_body(sub, head, k, base, mid, w, q0, q2, c0, c2, d0, d2, values, s0, s2, bias, ext, part):
    @on_first(sub)
    def _():
        full_mask(bias, [doc_row(ref) for ref in (d0, d0, d2)])

    linked = dot_nn(mid[...], w[...])
    for n in range(2, 5):
        ext[pl.ds(n, S, stride=3), :] = linked[0:S]
    ext[0:2, :] = jnp.broadcast_to(linked[S + 15 : S + 16], (2, E))
    v = (base[...].astype(F32) + ext[0:F, :]).astype(BF16)
    values[...] = v
    for t in range(TILES):
        lo, first, last = t * S, F - t * S, (t + 1) * S
        queries = jnp.concatenate([q0[lo:F, :], q2[0:last, :]], axis=0)
        cots = jnp.concatenate([c0[lo:F, :], c2[0:last, :]], axis=0)
        mask = jnp.concatenate([bias[t, :, 0:first], bias[t, :, first + F : first + F + last]], axis=1)
        rows = partial_stats(k[lo : lo + S, :], v[lo : lo + S], queries, cots, mask)
        for j, empty in enumerate((NEG, 0.0, 0.0)):
            pieces = [jnp.full((1, lo), empty, F32)] if lo else []
            pieces += [rows[j]] + ([jnp.full((1, F - last), empty, F32)] if last < F else [])
            part[t, pl.ds(j * H + head, 1), :] = jnp.concatenate(pieces, axis=1)

    @on_last(sub)
    def _():
        for out, cols in ((s0, slice(0, F)), (s2, slice(F, 2 * F))):
            merge_into(out, part, cols)


def partial_stats(k, v, queries, cots, mask):
    scores = dot_nt(k, queries) * LOG2 + mask
    peak = jnp.max(scores, axis=0, keepdims=True)
    expo = jnp.exp2(scores - peak)
    dots = dot_nt(v, cots)
    return peak, jnp.sum(expo, axis=0, keepdims=True), jnp.sum(expo * dots, axis=0, keepdims=True)


def merge_into(out, part, cols):
    merged = merge([tuple(part[t, j * H : (j + 1) * H, cols] for j in range(3)) for t in range(TILES)])
    for j in range(3):
        out[j * H : (j + 1) * H, :] = merged[j]


def stats_next_body(sub, head, flag, k, v, q1a, q1b, c1, d0, d1, s1, bias, part):
    @on_first(sub)
    def _():
        full_mask(bias, [doc_row(ref) for ref in (d0, d1, d1)])

    queries = pick(flag, q1a, q1b, F)
    for t in range(TILES):
        lo = t * S
        mask = bias[t, :, F - lo : 2 * F - lo]
        rows = partial_stats(k[lo : lo + S, :], v[lo : lo + S, :], queries, c1[0:F, :], mask)
        for j in range(3):
            part[t, pl.ds(j * H + head, 1), :] = rows[j]

    @on_last(sub)
    def _():
        merge_into(s1, part, slice(0, F))


def merge(parts):
    peak = parts[0][0]
    for part in parts[1:]:
        peak = jnp.maximum(peak, part[0])
    total, dots = 0.0, 0.0
    for part in parts:
        factor = jnp.exp2(part[0] - peak)
        total = total + part[1] * factor
        dots = dots + part[2] * factor
    return peak, total, dots


def full_stats(k, base, mid, w, q0, q2, c0, c2):
    stat = jax.ShapeDtypeStruct((3 * H, F), F32)
    return call(
        stats_body,
        "full_stats",
        2_000_000_000,
        8_000_000,
        in_specs=[head_spec(F), head_spec(F), whole_spec((S + 16, WIDTH)), head_spec(WIDTH)]
        + [head_spec(F)] * 4
        + [DOCS] * 2,
        out_specs=[head_spec(F)] + [whole_spec((3 * H, F))] * 2,
        out_shape=[jax.ShapeDtypeStruct((F, WIDTH), BF16), stat, stat],
        scratch_shapes=[
            pltpu.VMEM((TILES, S, TILE_W), F32),
            pltpu.VMEM((400, E), F32),
            pltpu.VMEM((TILES, 3 * H, 2 * F), F32),
        ],
    )(k, base, mid, w, q0, q2, c0, c2, c0, c2)


def next_stats(flag, k, v, q1a, q1b, c0, c1):
    return call(
        stats_next_body,
        "next_stats",
        1_000_000_000,
        6_000_000,
        in_specs=[FLAG] + [head_spec(F)] * 5 + [DOCS] * 2,
        out_specs=[whole_spec((3 * H, F))],
        out_shape=[jax.ShapeDtypeStruct((3 * H, F), F32)],
        scratch_shapes=[
            pltpu.VMEM((TILES, S, TILE_W), F32),
            pltpu.VMEM((TILES, 3 * H, F), F32),
        ],
    )(flag, k, v, q1a, q1b, c1, c0, c1)[0]


def grads_body(
    sub, head, flag, k, v, q0, q1a, q1b, q2, c0, c1, c2, d0, d1, d2, s0, s1, s2, up1, up2, down1, down2,
    dk, dv, dq0, dq1, dq2, sums, link, tail, bias, ext, glob, kept,
):
    @on_first(sub)
    def _():
        full_mask(bias, [doc_row(ref) for ref in (d0, d1, d2)])

        def triple(ref, base=0):
            peak, total, dots = (ref[base + j * H : base + (j + 1) * H, :] for j in range(3))
            return jnp.where(total > 0.0, peak, NEG), total, dots

        groups = (
            (triple(s0), triple(up1), triple(up2)),
            (triple(s1), triple(up1, 3 * H), triple(down1)),
            (triple(s2), triple(down1, 3 * H), triple(down2)),
        )
        for n, group in enumerate(groups):
            cols = slice(n * F, (n + 1) * F)
            peak, total, dots = merge(group)
            inv = jnp.where(total > 0.0, 1.0 / total, 0.0)
            glob[0:H, cols] = peak
            glob[H : 2 * H, cols] = inv
            glob[2 * H : 3 * H, cols] = dots * inv
        kept[...] = jnp.zeros((F, SPAN_F), BF16)
        ext[F:400, :] = jnp.zeros((400 - F, E), F32)

    queries = jnp.concatenate([q0[...], pick(flag, q1a, q1b, F), q2[...]], axis=0)
    cots = jnp.concatenate([c0[0:F, :], c1[0:F, :], c2[0:F, :]], axis=0)
    for t in range(TILES):
        lo = t * S
        cols = slice(lo, lo + TILE_W)
        scores = dot_nt(k[lo : lo + S, :], queries[cols]) * LOG2 + bias[t]
        probs = jnp.exp2(scores - glob[pl.ds(head, 1), cols]) * glob[pl.ds(H + head, 1), cols]
        dots = dot_nt(v[lo : lo + S, :], cots[cols])
        grads = (probs * (dots - glob[pl.ds(2 * H + head, 1), cols])).astype(BF16)
        kept[lo : lo + S, cols] = grads
        dk[lo : lo + S, :] = (dot_nn(grads, queries[cols]) * SCALE).astype(BF16)
        grad_v = dot_nn(probs.astype(BF16), cots[cols]).astype(BF16)
        dv[lo : lo + S, :] = grad_v
        ext[lo : lo + S, :] = grad_v.astype(F32)
    for n, out in enumerate((dq0, dq1, dq2)):
        part = dot_tn(kept[:, n * F : (n + 1) * F], k[...]) * SCALE
        out[...] = part.astype(out.dtype)
    total = ext[pl.ds(2, S, stride=3), :] + ext[pl.ds(3, S, stride=3), :] + ext[pl.ds(4, S, stride=3), :]
    sums[...] = total
    first = ext[0:1, :] + ext[1:2, :]
    tail[...] = jnp.broadcast_to(first, (8, E))
    narrow = total.astype(BF16)
    last = jnp.where(iota((16, E), 0) == 15, first, 0.0).astype(BF16)
    for x in range(4):
        link[x * (S + 16) : x * (S + 16) + S, :] = narrow
        link[x * (S + 16) + S : (x + 1) * (S + 16), :] = last


def full_grads(flag, k, v, qs, cs, stats):
    return call(
        grads_body,
        "full_grads",
        8_000_000_000,
        14_000_000,
        in_specs=[FLAG, head_spec(F), head_spec(F)]
        + [head_spec(F)] * 7
        + [DOCS] * 3
        + [whole_spec(s.shape) for s in stats],
        out_specs=[head_spec(F)] * 5 + [head_spec(S), head_spec(4 * (S + 16)), head_spec(8)],
        out_shape=[
            jax.ShapeDtypeStruct((F, WIDTH), BF16),
            jax.ShapeDtypeStruct((F, WIDTH), BF16),
            jax.ShapeDtypeStruct((F, WIDTH), F32),
            jax.ShapeDtypeStruct((F, WIDTH), BF16),
            jax.ShapeDtypeStruct((F, WIDTH), BF16),
            jax.ShapeDtypeStruct((S, WIDTH), F32),
            jax.ShapeDtypeStruct((4 * (S + 16), WIDTH), BF16),
            jax.ShapeDtypeStruct((8, WIDTH), F32),
        ],
        scratch_shapes=[
            pltpu.VMEM((TILES, S, TILE_W), F32),
            pltpu.VMEM((400, E), F32),
            pltpu.VMEM((3 * H, SPAN_F), F32),
            pltpu.VMEM((F, SPAN_F), BF16),
        ],
    )(flag, k, v, *qs, *cs, *cs, *stats)


def mid_cot_body(sub, head, w, att, stat, sums, tail, out, whole):
    @on_first(sub)
    def _():
        total = sums[...] + jnp.where(iota((S, WIDTH), 0) == S - 1, tail[0:1, :], 0.0)
        whole[...] = total.astype(BF16)

    grad = dot_nt(whole[...], w[...]).astype(BF16)
    out[0:S, :] = grad
    delta = jnp.sum(jnp.transpose(grad.astype(F32) * att[...]), axis=0, keepdims=True)
    rows = [*split3(stat[0:1, :]), *split3(stat[1:2, :]), *split3(delta)]
    rows = [row.astype(F32) for row in rows] + [jnp.zeros((7, E), F32)]
    out[S : S + 16, :] = jnp.concatenate(rows, axis=0).astype(BF16)


def mid_cotangent(sums, tail, w, att, stat):
    body = mid_cot_body

    def run(w_ref, *refs):
        for sub in range(STEP):
            cols = pl.ds(sub * E, E)
            att_ref, stat_ref, sums_ref, tail_ref, out_ref, whole = refs
            body(
                sub, None, w_ref.at[cols, :], att_ref.at[:, cols], stat_ref.at[:, cols],
                sums_ref, tail_ref, out_ref.at[:, cols], whole,
            )

    return pl.pallas_call(
        run,
        grid=(H // STEP,),
        in_specs=[
            pl.BlockSpec((STEP * E, WIDTH), lambda h: (h, 0)),
            head_spec(S),
            head_spec(8),
            whole_spec((S, WIDTH)),
            whole_spec((8, WIDTH)),
        ],
        out_specs=head_spec(S + 16),
        out_shape=jax.ShapeDtypeStruct((S + 16, WIDTH), BF16),
        scratch_shapes=[pltpu.VMEM((S, WIDTH), BF16)],
        compiler_params=pltpu.CompilerParams(vmem_limit_bytes=16 * 1024 * 1024),
        cost_estimate=pl.CostEstimate(flops=600_000_000, bytes_accessed=4_000_000, transcendentals=0),
        name="mid_cotangent",
    )(w, att, stat, sums, tail)


def mid_bwd_body(sub, head, flag, p4, p3, p2, first, second, p0, *refs):
    ms = [ref[...] for ref in refs[0:5]]
    gs = refs[5:10]
    dq, dk, dv, back, fore = refs[10:]
    pays = pair_slabs(flag, p4, p3, p2, first, second, p0)

    @on_first(sub)
    def _():
        mine = p0[2 * S : 2 * S + 16, :].astype(F32)[0:1]
        column = to_column(mine, S)
        causal = iota((S, S), 1) >= iota((S, S), 0)
        for n, pay in enumerate(pays):
            ok = to_column(pay[2 * S : 2 * S + 16].astype(F32)[0:1], S) == mine
            if n == REACH:
                ok = ok & causal
            back[n * S : (n + 1) * S, :] = jnp.where(ok, 0.0, NEG)
        for n, pay in enumerate(ms):
            ok = column == pay[S : S + 16].astype(F32)[0:1]
            if n == 0:
                ok = ok & causal
            fore[:, n * S : (n + 1) * S] = jnp.where(ok, 0.0, NEG)

    def stats(ref):
        rows = ref[S : S + 16, :].astype(F32)
        return [rows[j : j + 1] + rows[j + 1 : j + 2] + rows[j + 2 : j + 3] for j in (0, 3, 6)]

    k = p0[0:S, :]
    v = p0[S : 2 * S, :]
    keys = jnp.concatenate([pay[0:S] for pay in pays], axis=0)
    values = jnp.concatenate([pay[S : 2 * S] for pay in pays], axis=0)
    peak, inv, delta = stats(gs[0])
    scores = dot_nt(keys, ms[0][0:S]) * LOG2 + back[...]
    probs = jnp.exp2(scores - peak) * inv
    grads = (probs * (dot_nt(values, gs[0][0:S, :]) - delta)).astype(BF16)
    dq[...] = (dot_tn(grads, keys) * SCALE).astype(BF16)
    queries = jnp.concatenate([one[0:S] for one in ms], axis=0)
    cots = jnp.concatenate([ref[0:S, :] for ref in gs], axis=0)
    every = [stats(ref) for ref in gs]
    peak, inv, delta = (jnp.concatenate([one[j] for one in every], axis=1) for j in range(3))
    scores = dot_nt(k, queries) * LOG2 + fore[...]
    probs = jnp.exp2(scores - peak) * inv
    grads = (probs * (dot_nt(v, cots) - delta)).astype(BF16)
    dk[...] = (dot_nn(grads, queries) * SCALE).astype(BF16)
    dv[...] = dot_nn(probs.astype(BF16), cots).astype(BF16)


QUERY_ROWS = pl.BlockSpec((pl.Element(S + 16), pl.Element(STEP * E)), lambda h: (F, h * STEP * E))


def mid_backward(flag, pays, ms, gs):
    return call(
        mid_bwd_body,
        "mid_backward",
        3_000_000_000,
        6_000_000,
        in_specs=[FLAG] + PAY_SPECS + [QUERY_ROWS] * 3 + [head_spec(S + 16)] * 7,
        out_specs=[head_spec(S)] * 3,
        out_shape=[jax.ShapeDtypeStruct((S, WIDTH), BF16)] * 3,
        scratch_shapes=[pltpu.VMEM((SPAN_M, S), F32), pltpu.VMEM((S, SPAN_M), F32)],
    )(flag, *pays, *ms, *gs)


def shift(value, steps):
    count = lax.axis_size("ctx")
    first, last = max(0, -steps), min(count, count - steps)
    return lax.ppermute(value, "ctx", [(n, n + steps) for n in range(first, last)])


def swap(value, axis, bit):
    count = lax.axis_size(axis)
    return lax.ppermute(value, axis, [(n, n ^ bit) for n in range(count)])


def together(*values):
    return lax.optimization_barrier(values)


def block(value, index, rows):
    return lax.dynamic_slice_in_dim(value, index * rows, rows, 0)


X_GROUPS = [[first + 16 * n for n in range(4)] for first in range(16)]
YZ_GROUPS = [[16 * first + n for n in range(16)] for first in range(4)]


def exchange(value, axis, groups):
    return lax.all_to_all(value, axis, 0, 0, axis_index_groups=groups, tiled=True)


def shards(q_mid, k_mid, v_mid, doc_ids, q_full, k_full, v_base, w_link, cotangent):
    place = lax.axis_index("ctx")
    upper = place % 2 == 1
    flag = (place % 2).astype(jnp.int32).reshape(1)
    q_m, q_f, k_f = q_mid[0], q_full[0], k_full[0]
    ids = jnp.broadcast_to(jnp.tile((doc_ids + 1).astype(BF16), (1, 2)), (16, 2 * S))
    own_kv, own_cq, swap_a = pack(flag, q_m, k_mid[0], v_mid[0], ids, q_f, cotangent[0])

    kv2 = shift(own_kv, 2)
    got_a = swap(swap_a, "ctx", 1)
    qf2 = shift(q_f, -2)
    late_cq, qf2, kv2, got_a = together(own_cq, qf2, kv2, got_a)
    swap_b = jnp.concatenate([jnp.where(upper, kv2, qf2[:KV]), qf2[KV:]], axis=0)
    got_b = swap(swap_b, "ctx", 1)
    kv4 = shift(kv2, 2)
    kv2, kv4 = together(kv2, kv4)
    kv3 = swap(jnp.where(upper, kv4, kv2), "ctx", 1)
    cq2 = shift(late_cq, -2)
    cq2, got_b_late, kv3_late = together(cq2, got_b, kv3)
    cq1 = swap(jnp.where(upper, late_cq, cq2), "ctx", 1)

    pays = (kv4, kv3, kv2, got_a, got_b, own_kv)
    mid_ext, attended, mid_stat = mid_forward(flag, q_m, pays)
    parts = jnp.concatenate([mid_ext[:, n * 256 : (n + 1) * 256] for n in range(4)], axis=0)
    left = exchange(parts, "ctx", X_GROUPS)
    qm2 = cq2[F:]
    qm4, mid_ext = together(shift(qm2, -2), mid_ext)
    values, s0, s2 = full_stats(k_f, v_base[0], mid_ext, w_link, q_f, qf2, late_cq, cq2)
    up2, down2 = shift(s2, 2), shift(s0, -2)
    left, cq1, up2, down2 = together(left, cq1, up2, down2)
    s1 = next_stats(flag, k_f, values, got_b_late, got_a, late_cq, cq1)
    up1 = shift(jnp.concatenate([s1, s2], axis=0), 1)
    down1 = shift(jnp.concatenate([s0, s1], axis=0), -1)

    qm3 = swap(jnp.where(upper, qm2, qm4), "ctx", 1)
    values, qm3 = together(values, qm3)
    qs, cs = (q_f, got_b_late, got_a, qf2), (late_cq, cq1, cq2)
    dk_f, dv_f, dq0, dq1, dq2, sums, sum_ext, tail = full_grads(
        flag, k_f, values, qs, cs, (s0, s1, s2, up1, up2, down1, down2)
    )

    next_tail = shift(tail, -1)
    near = swap(dq1, "ctx", 1)
    cot_m = mid_cotangent(sums, next_tail, w_link, attended, mid_stat)
    g2 = shift(cot_m, -2)
    right = exchange(sum_ext, "ctx", X_GROUPS)
    term = dot_tn(left, right).astype(BF16)
    g1 = swap(jnp.where(upper, cot_m, g2), "ctx", 1)
    g4 = shift(g2, -2)
    total = jnp.sum(exchange(term, "ctx", YZ_GROUPS).astype(F32).reshape(16, 16, WIDTH), axis=0)
    near, total = together(near, total)
    passed = jnp.where(upper, dq2.astype(F32), dq2.astype(F32) + near.astype(F32)).astype(BF16)
    far = shift(passed, 2)
    g2_late, g4 = together(g2, g4)
    g3 = swap(jnp.where(upper, g2_late, g4), "ctx", 1)
    every = exchange(jnp.concatenate([total] * 4, axis=0), "dp", None)
    factor = float(lax.axis_size("dp") * lax.axis_size("ctx") * F) ** (-0.5)
    grad_link = jnp.sum(every.reshape(4, 16, WIDTH), axis=0) * factor
    pays = (kv4, kv3_late, kv2, got_a, got_b, own_kv)
    dq_m, dk_m, dv_m = mid_backward(flag, pays, (late_cq, cq1, cq2, qm3, qm4), (cot_m, g1, g2, g3, g4))

    dq_f = (dq0 + far.astype(F32) + jnp.where(upper, near.astype(F32), 0.0)).astype(BF16)
    return (dq_m[None], dk_m[None], dv_m[None], dq_f[None], dk_f[None], dv_f[None], grad_link)


def solution(mesh):
    rows = P("dp", "ctx", None)
    return jax.shard_map(
        shards,
        mesh=mesh,
        in_specs=(rows, rows, rows, P("dp", "ctx"), rows, rows, rows, P(), rows),
        out_specs=(rows,) * 6 + (P("ctx", None),),
        check_vma=False,
    )
```

```python
import math

import jax
import jax.numpy as jnp
from jax import lax
from jax.experimental import pallas as pl
from jax.experimental.pallas import tpu as pltpu
from jax.sharding import PartitionSpec as P

H = 8
E = 128
S = 128
F = 384
REACH = 4
FREACH = 2
WIDTH = H * E
SPAN_M = (REACH + 1) * S
SPAN_F = (FREACH + 1) * F
WIN = FREACH * F
KV = 2 * S + 32
CQ = F + S + 16
TILES = F // S
TILE_W = WIN + S
STEP = 4
SCALE = E ** (-0.5)
LOG2 = SCALE * math.log2(math.e)
NEG = -1e30
F32 = jnp.float32
BF16 = jnp.bfloat16


def dot_nn(a, b):
    return lax.dot_general(a, b, (((1,), (0,)), ((), ())), preferred_element_type=F32)


def dot_nt(a, b):
    return lax.dot_general(a, b, (((1,), (1,)), ((), ())), preferred_element_type=F32)


def dot_tn(a, b):
    return lax.dot_general(a, b, (((0,), (0,)), ((), ())), preferred_element_type=F32)


def iota(shape, axis):
    return lax.broadcasted_iota(jnp.int32, shape, axis)


def to_column(row, size):
    return jnp.transpose(jnp.broadcast_to(row, (size, size)))


def split3(x):
    hi = x.astype(BF16)
    rest = x - hi.astype(F32)
    mid = rest.astype(BF16)
    return hi, mid, (rest - mid.astype(F32)).astype(BF16)


def head_spec(rows):
    return pl.BlockSpec((rows, STEP * E), lambda h: (0, h))


def by_head(body, in_specs, out_specs):
    split = [spec.block_shape is not None and spec.block_shape[-1] in (STEP * E, pl.Element(STEP * E)) for spec in in_specs + out_specs]

    def run(*refs):
        for sub in range(STEP):
            views = [ref.at[:, pl.ds(sub * E, E)] if cut else ref for ref, cut in zip(refs, split)]
            body(sub, pl.program_id(0) * STEP + sub, *views, *refs[len(split) :])

    return run


def call(body, name, flops, bytes_accessed, in_specs, out_specs, out_shape, scratch_shapes):
    return pl.pallas_call(
        by_head(body, in_specs, out_specs),
        grid=(H // STEP,),
        in_specs=in_specs,
        out_specs=out_specs,
        out_shape=out_shape,
        scratch_shapes=scratch_shapes,
        cost_estimate=pl.CostEstimate(flops=flops, bytes_accessed=bytes_accessed, transcendentals=0),
        name=name,
    )


def on_first(sub):
    return pl.when(pl.program_id(0) == 0) if sub == 0 else lambda build: None


def on_last(sub):
    return pl.when(pl.program_id(0) == H // STEP - 1) if sub == STEP - 1 else lambda build: None


def whole_spec(shape):
    return pl.BlockSpec(shape, lambda h: (0,) * len(shape))


def pack_body(flag, q, k, v, ids, qf, cot, kv, cq, first):
    kv[0:S, :] = k[...]
    kv[S : 2 * S, :] = v[...]
    kv[2 * S : 2 * S + 16, :] = ids[...]
    kv[2 * S + 16 : KV, :] = q[S - 16 : S, :]
    cq[0:F, :] = cot[...]
    cq[F : F + S, :] = q[...]
    cq[F + S : CQ, :] = ids[...]
    first[...] = qf[...]

    @pl.when(flag[0] == 0)
    def _():
        first[0:KV, :] = kv[...]


def pack(flag, q, k, v, ids, qf, cot):
    def wide(rows):
        return pl.BlockSpec((rows, 2 * E), lambda h: (0, h))

    return pl.pallas_call(
        pack_body,
        grid=(H // 2,),
        in_specs=[FLAG] + [wide(S)] * 3 + [whole_spec((16, 2 * E)), wide(F), wide(F)],
        out_specs=[wide(KV), wide(CQ), wide(F)],
        out_shape=[
            jax.ShapeDtypeStruct((KV, WIDTH), BF16),
            jax.ShapeDtypeStruct((CQ, WIDTH), BF16),
            jax.ShapeDtypeStruct((F, WIDTH), BF16),
        ],
        name="pack",
    )(flag, q, k, v, ids, qf, cot)


def pick(flag, upper, lower, rows):
    return jnp.where(flag[0] == 1, upper[0:rows, :], lower[0:rows, :])


def pair_slabs(flag, p4, p2, a, b, c, p0):
    return [p4[...], pick(flag, b, c, KV), p2[...], pick(flag, a, b, KV), p0[...]]


def mid_fwd_body(sub, head, flag, q, p4, p2, a, b, c, p0, out, att, stat, bias):
    pays = pair_slabs(flag, p4, p2, a, b, c, p0)

    @on_first(sub)
    def _():
        def ids(n):
            return pays[n][2 * S : 2 * S + 16].astype(F32)[0:1]

        mine = to_column(ids(REACH), S)
        edge = to_column(ids(REACH - 1), S)[S - 16 : S]
        for n in range(REACH + 1):
            cols = slice(n * S, (n + 1) * S)
            ok = mine == ids(n)
            ok_edge = edge == ids(n)
            if n == REACH:
                ok = ok & (iota((S, S), 0) >= iota((S, S), 1))
                ok_edge = ok_edge & (iota((16, S), 1) < 0)
            if n == REACH - 1:
                ok_edge = ok_edge & (iota((16, S), 0) + (S - 16) >= iota((16, S), 1))
            bias[0:S, cols] = jnp.where(ok, 0.0, NEG)
            bias[S : S + 16, cols] = jnp.where(ok_edge, 0.0, NEG)

    keys = jnp.concatenate([pay[0:S] for pay in pays], axis=0)
    values = jnp.concatenate([pay[S : 2 * S] for pay in pays], axis=0)
    queries = jnp.concatenate([q[...], pays[REACH - 1][2 * S + 16 : KV]], axis=0)
    scores = dot_nt(queries, keys) * LOG2 + bias[...]
    peak = jnp.max(scores, axis=1, keepdims=True)
    expo = jnp.exp2(scores - peak)
    inv = 1.0 / jnp.sum(expo, axis=1, keepdims=True)
    attended = dot_nn((expo * inv).astype(BF16), values)
    att[...] = attended[0:S]
    out[...] = attended.astype(BF16)
    stat[0:1, :] = jnp.transpose(jnp.broadcast_to(peak[0:S], (S, S)))[0:1]
    stat[1:2, :] = jnp.transpose(jnp.broadcast_to(inv[0:S], (S, S)))[0:1]
    stat[2:8, :] = jnp.zeros((6, S), F32)


def mid_forward(flag, q, pays):
    return call(
        mid_fwd_body,
        "mid_forward",
        700_000_000,
        4_000_000,
        in_specs=[FLAG, head_spec(S)] + PAY_SPECS,
        out_specs=[head_spec(S + 16), head_spec(S), head_spec(8)],
        out_shape=[
            jax.ShapeDtypeStruct((S + 16, WIDTH), BF16),
            jax.ShapeDtypeStruct((S, WIDTH), F32),
            jax.ShapeDtypeStruct((8, WIDTH), F32),
        ],
        scratch_shapes=[pltpu.VMEM((S + 16, SPAN_M), F32)],
    )(flag, q, *pays)


FLAG = pl.BlockSpec(memory_space=pltpu.SMEM)
PAY_SPECS = [head_spec(KV)] * 6


def full_mask(bias, docs):
    spread = (iota((S, F), 1) // 3 == iota((S, F), 0)).astype(BF16)
    spread_t = (iota((F, S), 0) // 3 == iota((F, S), 1)).astype(BF16)
    rows = jnp.concatenate(
        [dot_nn(jnp.broadcast_to(d, (16, S)), spread)[0:1] for d in docs], axis=1
    )
    column = dot_nn(spread_t, to_column(docs[0].astype(F32), S).astype(BF16))
    for t in range(TILES):
        lo = t * S
        mine = jnp.concatenate([column[lo : lo + S]] * (TILE_W // S), axis=1)
        gap = iota((S, TILE_W), 1) - iota((S, TILE_W), 0)
        ok = (mine == rows[:, lo : lo + TILE_W]) & (gap >= 0) & (gap < WIN)
        bias[t] = jnp.where(ok, 0.0, NEG)


DOCS = pl.BlockSpec((16, S), lambda h: ((F + S) // 16, 0))


def doc_row(ref):
    return ref[...][0:1]


def stats_body(sub, head, k, base, mid, w, q0, q2, c0, c2, d0, d2, values, s0, s2, bias, ext, part):
    @on_first(sub)
    def _():
        full_mask(bias, [doc_row(ref) for ref in (d0, d0, d2)])

    linked = dot_nn(mid[...], w[...])
    for n in range(2, 5):
        ext[pl.ds(n, S, stride=3), :] = linked[0:S]
    ext[0:2, :] = jnp.broadcast_to(linked[S + 15 : S + 16], (2, E))
    v = (base[...].astype(F32) + ext[0:F, :]).astype(BF16)
    values[...] = v
    for t in range(TILES):
        lo, first, last = t * S, F - t * S, (t + 1) * S
        queries = jnp.concatenate([q0[lo:F, :], q2[0:last, :]], axis=0)
        cots = jnp.concatenate([c0[lo:F, :], c2[0:last, :]], axis=0)
        mask = jnp.concatenate([bias[t, :, 0:first], bias[t, :, first + F : first + F + last]], axis=1)
        rows = partial_stats(k[lo : lo + S, :], v[lo : lo + S], queries, cots, mask)
        for j, empty in enumerate((NEG, 0.0, 0.0)):
            pieces = [jnp.full((1, lo), empty, F32)] if lo else []
            pieces += [rows[j]] + ([jnp.full((1, F - last), empty, F32)] if last < F else [])
            part[t, pl.ds(j * H + head, 1), :] = jnp.concatenate(pieces, axis=1)

    @on_last(sub)
    def _():
        for out, cols in ((s0, slice(0, F)), (s2, slice(F, 2 * F))):
            merge_into(out, part, cols)


def partial_stats(k, v, queries, cots, mask):
    scores = dot_nt(k, queries) * LOG2 + mask
    peak = jnp.max(scores, axis=0, keepdims=True)
    expo = jnp.exp2(scores - peak)
    dots = dot_nt(v, cots)
    return peak, jnp.sum(expo, axis=0, keepdims=True), jnp.sum(expo * dots, axis=0, keepdims=True)


def merge_into(out, part, cols):
    merged = merge([tuple(part[t, j * H : (j + 1) * H, cols] for j in range(3)) for t in range(TILES)])
    for j in range(3):
        out[j * H : (j + 1) * H, :] = merged[j]


def stats_next_body(sub, head, flag, k, v, q1a, q1b, c1, d0, d1, s1, bias, part):
    @on_first(sub)
    def _():
        full_mask(bias, [doc_row(ref) for ref in (d0, d1, d1)])

    queries = pick(flag, q1a, q1b, F)
    for t in range(TILES):
        lo = t * S
        mask = bias[t, :, F - lo : 2 * F - lo]
        rows = partial_stats(k[lo : lo + S, :], v[lo : lo + S, :], queries, c1[0:F, :], mask)
        for j in range(3):
            part[t, pl.ds(j * H + head, 1), :] = rows[j]

    @on_last(sub)
    def _():
        merge_into(s1, part, slice(0, F))


def merge(parts):
    peak = parts[0][0]
    for part in parts[1:]:
        peak = jnp.maximum(peak, part[0])
    total, dots = 0.0, 0.0
    for part in parts:
        factor = jnp.exp2(part[0] - peak)
        total = total + part[1] * factor
        dots = dots + part[2] * factor
    return peak, total, dots


def full_stats(k, base, mid, w, q0, q2, c0, c2):
    stat = jax.ShapeDtypeStruct((3 * H, F), F32)
    return call(
        stats_body,
        "full_stats",
        2_000_000_000,
        8_000_000,
        in_specs=[head_spec(F), head_spec(F), whole_spec((S + 16, WIDTH)), head_spec(WIDTH)]
        + [head_spec(F)] * 4
        + [DOCS] * 2,
        out_specs=[head_spec(F)] + [whole_spec((3 * H, F))] * 2,
        out_shape=[jax.ShapeDtypeStruct((F, WIDTH), BF16), stat, stat],
        scratch_shapes=[
            pltpu.VMEM((TILES, S, TILE_W), F32),
            pltpu.VMEM((400, E), F32),
            pltpu.VMEM((TILES, 3 * H, 2 * F), F32),
        ],
    )(k, base, mid, w, q0, q2, c0, c2, c0, c2)


def next_stats(flag, k, v, q1a, q1b, c0, c1):
    return call(
        stats_next_body,
        "next_stats",
        1_000_000_000,
        6_000_000,
        in_specs=[FLAG] + [head_spec(F)] * 5 + [DOCS] * 2,
        out_specs=[whole_spec((3 * H, F))],
        out_shape=[jax.ShapeDtypeStruct((3 * H, F), F32)],
        scratch_shapes=[
            pltpu.VMEM((TILES, S, TILE_W), F32),
            pltpu.VMEM((TILES, 3 * H, F), F32),
        ],
    )(flag, k, v, q1a, q1b, c1, c0, c1)[0]


def grads_body(
    sub, head, flag, k, v, q0, q1a, q1b, q2, c0, c1, c2, d0, d1, d2, s0, s1, s2, up1, up2, down1, down2,
    dk, dv, dq0, dq1, dq2, sums, link, tail, bias, ext, glob, kept,
):
    @on_first(sub)
    def _():
        full_mask(bias, [doc_row(ref) for ref in (d0, d1, d2)])

        def triple(ref, base=0):
            peak, total, dots = (ref[base + j * H : base + (j + 1) * H, :] for j in range(3))
            return jnp.where(total > 0.0, peak, NEG), total, dots

        groups = (
            (triple(s0), triple(up1), triple(up2)),
            (triple(s1), triple(up1, 3 * H), triple(down1)),
            (triple(s2), triple(down1, 3 * H), triple(down2)),
        )
        for n, group in enumerate(groups):
            cols = slice(n * F, (n + 1) * F)
            peak, total, dots = merge(group)
            inv = jnp.where(total > 0.0, 1.0 / total, 0.0)
            glob[0:H, cols] = peak
            glob[H : 2 * H, cols] = inv
            glob[2 * H : 3 * H, cols] = dots * inv
        kept[...] = jnp.zeros((F, SPAN_F), BF16)
        ext[F:400, :] = jnp.zeros((400 - F, E), F32)

    queries = jnp.concatenate([q0[...], pick(flag, q1a, q1b, F), q2[...]], axis=0)
    cots = jnp.concatenate([c0[0:F, :], c1[0:F, :], c2[0:F, :]], axis=0)
    for t in range(TILES):
        lo = t * S
        cols = slice(lo, lo + TILE_W)
        scores = dot_nt(k[lo : lo + S, :], queries[cols]) * LOG2 + bias[t]
        probs = jnp.exp2(scores - glob[pl.ds(head, 1), cols]) * glob[pl.ds(H + head, 1), cols]
        dots = dot_nt(v[lo : lo + S, :], cots[cols])
        grads = (probs * (dots - glob[pl.ds(2 * H + head, 1), cols])).astype(BF16)
        kept[lo : lo + S, cols] = grads
        dk[lo : lo + S, :] = (dot_nn(grads, queries[cols]) * SCALE).astype(BF16)
        grad_v = dot_nn(probs.astype(BF16), cots[cols]).astype(BF16)
        dv[lo : lo + S, :] = grad_v
        ext[lo : lo + S, :] = grad_v.astype(F32)
    for n, out in enumerate((dq0, dq1, dq2)):
        part = dot_tn(kept[:, n * F : (n + 1) * F], k[...]) * SCALE
        out[...] = part.astype(out.dtype)
    total = ext[pl.ds(2, S, stride=3), :] + ext[pl.ds(3, S, stride=3), :] + ext[pl.ds(4, S, stride=3), :]
    sums[...] = total
    first = ext[0:1, :] + ext[1:2, :]
    tail[...] = jnp.broadcast_to(first, (8, E))
    narrow = total.astype(BF16)
    last = jnp.where(iota((16, E), 0) == 15, first, 0.0).astype(BF16)
    for x in range(4):
        link[x * (S + 16) : x * (S + 16) + S, :] = narrow
        link[x * (S + 16) + S : (x + 1) * (S + 16), :] = last


def full_grads(flag, k, v, qs, cs, stats):
    return call(
        grads_body,
        "full_grads",
        8_000_000_000,
        14_000_000,
        in_specs=[FLAG, head_spec(F), head_spec(F)]
        + [head_spec(F)] * 7
        + [DOCS] * 3
        + [whole_spec(s.shape) for s in stats],
        out_specs=[head_spec(F)] * 5 + [head_spec(S), head_spec(4 * (S + 16)), head_spec(8)],
        out_shape=[
            jax.ShapeDtypeStruct((F, WIDTH), BF16),
            jax.ShapeDtypeStruct((F, WIDTH), BF16),
            jax.ShapeDtypeStruct((F, WIDTH), F32),
            jax.ShapeDtypeStruct((F, WIDTH), BF16),
            jax.ShapeDtypeStruct((F, WIDTH), BF16),
            jax.ShapeDtypeStruct((S, WIDTH), F32),
            jax.ShapeDtypeStruct((4 * (S + 16), WIDTH), BF16),
            jax.ShapeDtypeStruct((8, WIDTH), F32),
        ],
        scratch_shapes=[
            pltpu.VMEM((TILES, S, TILE_W), F32),
            pltpu.VMEM((400, E), F32),
            pltpu.VMEM((3 * H, SPAN_F), F32),
            pltpu.VMEM((F, SPAN_F), BF16),
        ],
    )(flag, k, v, *qs, *cs, *cs, *stats)


def mid_cot_body(sub, head, w, att, stat, sums, tail, out, whole):
    @on_first(sub)
    def _():
        total = sums[...] + jnp.where(iota((S, WIDTH), 0) == S - 1, tail[0:1, :], 0.0)
        whole[...] = total.astype(BF16)

    grad = dot_nt(whole[...], w[...]).astype(BF16)
    out[0:S, :] = grad
    delta = jnp.sum(jnp.transpose(grad.astype(F32) * att[...]), axis=0, keepdims=True)
    rows = [*split3(stat[0:1, :]), *split3(stat[1:2, :]), *split3(delta)]
    rows = [row.astype(F32) for row in rows] + [jnp.zeros((7, E), F32)]
    out[S : S + 16, :] = jnp.concatenate(rows, axis=0).astype(BF16)


def mid_cotangent(sums, tail, w, att, stat):
    body = mid_cot_body

    def run(w_ref, *refs):
        for sub in range(STEP):
            cols = pl.ds(sub * E, E)
            att_ref, stat_ref, sums_ref, tail_ref, out_ref, whole = refs
            body(
                sub, None, w_ref.at[cols, :], att_ref.at[:, cols], stat_ref.at[:, cols],
                sums_ref, tail_ref, out_ref.at[:, cols], whole,
            )

    return pl.pallas_call(
        run,
        grid=(H // STEP,),
        in_specs=[
            pl.BlockSpec((STEP * E, WIDTH), lambda h: (h, 0)),
            head_spec(S),
            head_spec(8),
            whole_spec((S, WIDTH)),
            whole_spec((8, WIDTH)),
        ],
        out_specs=head_spec(S + 16),
        out_shape=jax.ShapeDtypeStruct((S + 16, WIDTH), BF16),
        scratch_shapes=[pltpu.VMEM((S, WIDTH), BF16)],
        compiler_params=pltpu.CompilerParams(vmem_limit_bytes=16 * 1024 * 1024),
        cost_estimate=pl.CostEstimate(flops=600_000_000, bytes_accessed=4_000_000, transcendentals=0),
        name="mid_cotangent",
    )(w, att, stat, sums, tail)


def mid_bwd_body(sub, head, flag, p4, p2, a, b, c, p0, *refs):
    ms = [ref[...] for ref in refs[0:5]]
    gs = refs[5:10]
    dq, dk, dv, back, fore = refs[10:]
    pays = pair_slabs(flag, p4, p2, a, b, c, p0)

    @on_first(sub)
    def _():
        mine = p0[2 * S : 2 * S + 16, :].astype(F32)[0:1]
        column = to_column(mine, S)
        causal = iota((S, S), 1) >= iota((S, S), 0)
        for n, pay in enumerate(pays):
            ok = to_column(pay[2 * S : 2 * S + 16].astype(F32)[0:1], S) == mine
            if n == REACH:
                ok = ok & causal
            back[n * S : (n + 1) * S, :] = jnp.where(ok, 0.0, NEG)
        for n, pay in enumerate(ms):
            ok = column == pay[S : S + 16].astype(F32)[0:1]
            if n == 0:
                ok = ok & causal
            fore[:, n * S : (n + 1) * S] = jnp.where(ok, 0.0, NEG)

    def stats(ref):
        rows = ref[S : S + 16, :].astype(F32)
        return [rows[j : j + 1] + rows[j + 1 : j + 2] + rows[j + 2 : j + 3] for j in (0, 3, 6)]

    k = p0[0:S, :]
    v = p0[S : 2 * S, :]
    keys = jnp.concatenate([pay[0:S] for pay in pays], axis=0)
    values = jnp.concatenate([pay[S : 2 * S] for pay in pays], axis=0)
    peak, inv, delta = stats(gs[0])
    scores = dot_nt(keys, ms[0][0:S]) * LOG2 + back[...]
    probs = jnp.exp2(scores - peak) * inv
    grads = (probs * (dot_nt(values, gs[0][0:S, :]) - delta)).astype(BF16)
    dq[...] = (dot_tn(grads, keys) * SCALE).astype(BF16)
    queries = jnp.concatenate([one[0:S] for one in ms], axis=0)
    cots = jnp.concatenate([ref[0:S, :] for ref in gs], axis=0)
    every = [stats(ref) for ref in gs]
    peak, inv, delta = (jnp.concatenate([one[j] for one in every], axis=1) for j in range(3))
    scores = dot_nt(k, queries) * LOG2 + fore[...]
    probs = jnp.exp2(scores - peak) * inv
    grads = (probs * (dot_nt(v, cots) - delta)).astype(BF16)
    dk[...] = (dot_nn(grads, queries) * SCALE).astype(BF16)
    dv[...] = dot_nn(probs.astype(BF16), cots).astype(BF16)


QUERY_ROWS = pl.BlockSpec((pl.Element(S + 16), pl.Element(STEP * E)), lambda h: (F, h * STEP * E))


def mid_backward(flag, pays, ms, gs):
    return call(
        mid_bwd_body,
        "mid_backward",
        3_000_000_000,
        6_000_000,
        in_specs=[FLAG] + PAY_SPECS + [QUERY_ROWS] * 3 + [head_spec(S + 16)] * 7,
        out_specs=[head_spec(S)] * 3,
        out_shape=[jax.ShapeDtypeStruct((S, WIDTH), BF16)] * 3,
        scratch_shapes=[pltpu.VMEM((SPAN_M, S), F32), pltpu.VMEM((S, SPAN_M), F32)],
    )(flag, *pays, *ms, *gs)


def shift(value, steps):
    count = lax.axis_size("ctx")
    first, last = max(0, -steps), min(count, count - steps)
    return lax.ppermute(value, "ctx", [(n, n + steps) for n in range(first, last)])


def swap(value, axis, bit):
    count = lax.axis_size(axis)
    return lax.ppermute(value, axis, [(n, n ^ bit) for n in range(count)])


def together(*values):
    return lax.optimization_barrier(values)


def block(value, index, rows):
    return lax.dynamic_slice_in_dim(value, index * rows, rows, 0)


X_GROUPS = [[first + 16 * n for n in range(4)] for first in range(16)]
YZ_GROUPS = [[16 * first + n for n in range(16)] for first in range(4)]


def exchange(value, axis, groups):
    return lax.all_to_all(value, axis, 0, 0, axis_index_groups=groups, tiled=True)


def shards(q_mid, k_mid, v_mid, doc_ids, q_full, k_full, v_base, w_link, cotangent):
    place = lax.axis_index("ctx")
    upper = place % 2 == 1
    flag = (place % 2).astype(jnp.int32).reshape(1)
    q_m, q_f, k_f = q_mid[0], q_full[0], k_full[0]
    ids = jnp.broadcast_to(jnp.tile((doc_ids + 1).astype(BF16), (1, 2)), (16, 2 * S))
    own_kv, own_cq, swap_a = pack(flag, q_m, k_mid[0], v_mid[0], ids, q_f, cotangent[0])

    kv2 = shift(own_kv, 2)
    got_a = swap(swap_a, "ctx", 1)
    qf2 = shift(q_f, -2)
    got_b = swap(kv2, "ctx", 1)
    late_cq, qf2, kv2, got_a = together(own_cq, qf2, kv2, got_a)
    kv4, got_b = together(shift(kv2, 2), got_b)
    got_c = swap(jnp.concatenate([jnp.where(upper, kv4, qf2[:KV]), qf2[KV:]], axis=0), "ctx", 1)
    cq2 = shift(late_cq, -2)
    cq2, got_c_late = together(cq2, got_c)
    cq1 = swap(jnp.where(upper, late_cq, cq2), "ctx", 1)

    pays = (kv4, kv2, got_a, got_b, got_c, own_kv)
    mid_ext, attended, mid_stat = mid_forward(flag, q_m, pays)
    parts = jnp.concatenate([mid_ext[:, n * 256 : (n + 1) * 256] for n in range(4)], axis=0)
    left = exchange(parts, "ctx", X_GROUPS)
    qm2 = cq2[F:]
    qm4, mid_ext = together(shift(qm2, -2), mid_ext)
    values, s0, s2 = full_stats(k_f, v_base[0], mid_ext, w_link, q_f, qf2, late_cq, cq2)
    up2, down2 = shift(s2, 2), shift(s0, -2)
    left, cq1, up2, down2 = together(left, cq1, up2, down2)
    s1 = next_stats(flag, k_f, values, got_c_late, got_a, late_cq, cq1)
    up1 = shift(jnp.concatenate([s1, s2], axis=0), 1)
    down1 = shift(jnp.concatenate([s0, s1], axis=0), -1)

    qm3 = swap(jnp.where(upper, qm2, qm4), "ctx", 1)
    values, qm3 = together(values, qm3)
    qs, cs = (q_f, got_c_late, got_a, qf2), (late_cq, cq1, cq2)
    dk_f, dv_f, dq0, dq1, dq2, sums, sum_ext, tail = full_grads(
        flag, k_f, values, qs, cs, (s0, s1, s2, up1, up2, down1, down2)
    )

    next_tail = shift(tail, -1)
    cot_m = mid_cotangent(sums, next_tail, w_link, attended, mid_stat)
    cot_m, dq1 = together(cot_m, dq1)
    near = swap(dq1, "ctx", 1)
    g2, sum_ext = together(shift(cot_m, -2), sum_ext)
    right = exchange(sum_ext, "ctx", X_GROUPS)
    term = dot_tn(left, right).astype(BF16)
    g1 = swap(jnp.where(upper, cot_m, g2), "ctx", 1)
    term, g4 = together(term, shift(g2, -2))
    total = jnp.sum(exchange(term, "ctx", YZ_GROUPS).astype(F32).reshape(16, 16, WIDTH), axis=0)
    near, total = together(near, total)
    passed = jnp.where(upper, dq2.astype(F32), dq2.astype(F32) + near.astype(F32)).astype(BF16)
    far = shift(passed, 2)
    g2_late, g4 = together(g2, g4)
    g3 = swap(jnp.where(upper, g2_late, g4), "ctx", 1)
    every = exchange(jnp.concatenate([total] * 4, axis=0), "dp", None)
    factor = float(lax.axis_size("dp") * lax.axis_size("ctx") * F) ** (-0.5)
    grad_link = jnp.sum(every.reshape(4, 16, WIDTH), axis=0) * factor
    dq_m, dk_m, dv_m = mid_backward(flag, pays, (late_cq, cq1, cq2, qm3, qm4), (cot_m, g1, g2, g3, g4))

    dq_f = (dq0 + far.astype(F32) + jnp.where(upper, near.astype(F32), 0.0)).astype(BF16)
    return (dq_m[None], dk_m[None], dv_m[None], dq_f[None], dk_f[None], dv_f[None], grad_link)


def solution(mesh):
    rows = P("dp", "ctx", None)
    return jax.shard_map(
        shards,
        mesh=mesh,
        in_specs=(rows, rows, rows, P("dp", "ctx"), rows, rows, rows, P(), rows),
        out_specs=(rows,) * 6 + (P("ctx", None),),
        check_vma=False,
    )
```

```python
import math

import jax
import jax.numpy as jnp
from jax import lax
from jax.experimental import pallas as pl
from jax.experimental.pallas import tpu as pltpu
from jax.sharding import PartitionSpec as P

H = 8
E = 128
S = 128
F = 384
REACH = 4
FREACH = 2
WIDTH = H * E
SPAN_M = (REACH + 1) * S
SPAN_F = (FREACH + 1) * F
WIN = FREACH * F
KV = 2 * S + 32
CQ = F + S + 16
TILES = F // S
TILE_W = WIN + S
STEP = 4
SCALE = E ** (-0.5)
LOG2 = SCALE * math.log2(math.e)
NEG = -1e30
F32 = jnp.float32
BF16 = jnp.bfloat16


def dot_nn(a, b):
    return lax.dot_general(a, b, (((1,), (0,)), ((), ())), preferred_element_type=F32)


def dot_nt(a, b):
    return lax.dot_general(a, b, (((1,), (1,)), ((), ())), preferred_element_type=F32)


def dot_tn(a, b):
    return lax.dot_general(a, b, (((0,), (0,)), ((), ())), preferred_element_type=F32)


def iota(shape, axis):
    return lax.broadcasted_iota(jnp.int32, shape, axis)


def to_column(row, size):
    return jnp.transpose(jnp.broadcast_to(row, (size, size)))


def split3(x):
    hi = x.astype(BF16)
    rest = x - hi.astype(F32)
    mid = rest.astype(BF16)
    return hi, mid, (rest - mid.astype(F32)).astype(BF16)


def head_spec(rows):
    return pl.BlockSpec((rows, STEP * E), lambda h: (0, h))


def by_head(body, in_specs, out_specs):
    split = [spec.block_shape is not None and spec.block_shape[-1] in (STEP * E, pl.Element(STEP * E)) for spec in in_specs + out_specs]

    def run(*refs):
        for sub in range(STEP):
            views = [ref.at[:, pl.ds(sub * E, E)] if cut else ref for ref, cut in zip(refs, split)]
            body(sub, pl.program_id(0) * STEP + sub, *views, *refs[len(split) :])

    return run


def call(body, name, flops, bytes_accessed, in_specs, out_specs, out_shape, scratch_shapes):
    return pl.pallas_call(
        by_head(body, in_specs, out_specs),
        grid=(H // STEP,),
        in_specs=in_specs,
        out_specs=out_specs,
        out_shape=out_shape,
        scratch_shapes=scratch_shapes,
        cost_estimate=pl.CostEstimate(flops=flops, bytes_accessed=bytes_accessed, transcendentals=0),
        name=name,
    )


def on_first(sub):
    return pl.when(pl.program_id(0) == 0) if sub == 0 else lambda build: None


def on_last(sub):
    return pl.when(pl.program_id(0) == H // STEP - 1) if sub == STEP - 1 else lambda build: None


def whole_spec(shape):
    return pl.BlockSpec(shape, lambda h: (0,) * len(shape))


def pack_body(flag, q, k, v, ids, qf, cot, kv, cq, first):
    kv[0:S, :] = k[...]
    kv[S : 2 * S, :] = v[...]
    kv[2 * S : 2 * S + 16, :] = ids[...]
    kv[2 * S + 16 : KV, :] = q[S - 16 : S, :]
    cq[0:F, :] = cot[...]
    cq[F : F + S, :] = q[...]
    cq[F + S : CQ, :] = ids[...]
    first[...] = qf[...]

    @pl.when(flag[0] == 0)
    def _():
        first[0:KV, :] = kv[...]


def pack(flag, q, k, v, ids, qf, cot):
    def wide(rows):
        return pl.BlockSpec((rows, 2 * E), lambda h: (0, h))

    return pl.pallas_call(
        pack_body,
        grid=(H // 2,),
        in_specs=[FLAG] + [wide(S)] * 3 + [whole_spec((16, 2 * E)), wide(F), wide(F)],
        out_specs=[wide(KV), wide(CQ), wide(F)],
        out_shape=[
            jax.ShapeDtypeStruct((KV, WIDTH), BF16),
            jax.ShapeDtypeStruct((CQ, WIDTH), BF16),
            jax.ShapeDtypeStruct((F, WIDTH), BF16),
        ],
        name="pack",
    )(flag, q, k, v, ids, qf, cot)


def pick(flag, upper, lower, rows):
    return jnp.where(flag[0] == 1, upper[0:rows, :], lower[0:rows, :])


def pair_slabs(flag, p4, p2, a, b, c, p0):
    return [p4[...], pick(flag, b, c, KV), p2[...], pick(flag, a, b, KV), p0[...]]


def mid_fwd_body(sub, head, flag, q, p4, p2, a, b, c, p0, out, att, stat, bias):
    pays = pair_slabs(flag, p4, p2, a, b, c, p0)

    @on_first(sub)
    def _():
        def ids(n):
            return pays[n][2 * S : 2 * S + 16].astype(F32)[0:1]

        mine = to_column(ids(REACH), S)
        edge = to_column(ids(REACH - 1), S)[S - 16 : S]
        for n in range(REACH + 1):
            cols = slice(n * S, (n + 1) * S)
            ok = mine == ids(n)
            ok_edge = edge == ids(n)
            if n == REACH:
                ok = ok & (iota((S, S), 0) >= iota((S, S), 1))
                ok_edge = ok_edge & (iota((16, S), 1) < 0)
            if n == REACH - 1:
                ok_edge = ok_edge & (iota((16, S), 0) + (S - 16) >= iota((16, S), 1))
            bias[0:S, cols] = jnp.where(ok, 0.0, NEG)
            bias[S : S + 16, cols] = jnp.where(ok_edge, 0.0, NEG)

    keys = jnp.concatenate([pay[0:S] for pay in pays], axis=0)
    values = jnp.concatenate([pay[S : 2 * S] for pay in pays], axis=0)
    queries = jnp.concatenate([q[...], pays[REACH - 1][2 * S + 16 : KV]], axis=0)
    scores = dot_nt(queries, keys) * LOG2 + bias[...]
    peak = jnp.max(scores, axis=1, keepdims=True)
    expo = jnp.exp2(scores - peak)
    inv = 1.0 / jnp.sum(expo, axis=1, keepdims=True)
    attended = dot_nn((expo * inv).astype(BF16), values)
    att[...] = attended[0:S]
    out[...] = attended.astype(BF16)
    stat[0:1, :] = jnp.transpose(jnp.broadcast_to(peak[0:S], (S, S)))[0:1]
    stat[1:2, :] = jnp.transpose(jnp.broadcast_to(inv[0:S], (S, S)))[0:1]
    stat[2:8, :] = jnp.zeros((6, S), F32)


def mid_forward(flag, q, pays):
    return call(
        mid_fwd_body,
        "mid_forward",
        700_000_000,
        4_000_000,
        in_specs=[FLAG, head_spec(S)] + PAY_SPECS,
        out_specs=[head_spec(S + 16), head_spec(S), head_spec(8)],
        out_shape=[
            jax.ShapeDtypeStruct((S + 16, WIDTH), BF16),
            jax.ShapeDtypeStruct((S, WIDTH), F32),
            jax.ShapeDtypeStruct((8, WIDTH), F32),
        ],
        scratch_shapes=[pltpu.VMEM((S + 16, SPAN_M), F32)],
    )(flag, q, *pays)


FLAG = pl.BlockSpec(memory_space=pltpu.SMEM)
PAY_SPECS = [head_spec(KV)] * 6


def full_mask(bias, docs):
    spread = (iota((S, F), 1) // 3 == iota((S, F), 0)).astype(BF16)
    spread_t = (iota((F, S), 0) // 3 == iota((F, S), 1)).astype(BF16)
    rows = jnp.concatenate(
        [dot_nn(jnp.broadcast_to(d, (16, S)), spread)[0:1] for d in docs], axis=1
    )
    column = dot_nn(spread_t, to_column(docs[0].astype(F32), S).astype(BF16))
    for t in range(TILES):
        lo = t * S
        mine = jnp.concatenate([column[lo : lo + S]] * (TILE_W // S), axis=1)
        gap = iota((S, TILE_W), 1) - iota((S, TILE_W), 0)
        ok = (mine == rows[:, lo : lo + TILE_W]) & (gap >= 0) & (gap < WIN)
        bias[t] = jnp.where(ok, 0.0, NEG)


DOCS = pl.BlockSpec((16, S), lambda h: ((F + S) // 16, 0))


def doc_row(ref):
    return ref[...][0:1]


def stats_body(sub, head, k, base, mid, w, q0, q2, c0, c2, d0, d2, values, s0, s2, bias, ext, part):
    @on_first(sub)
    def _():
        full_mask(bias, [doc_row(ref) for ref in (d0, d0, d2)])

    linked = dot_nn(mid[...], w[...])
    for n in range(2, 5):
        ext[pl.ds(n, S, stride=3), :] = linked[0:S]
    ext[0:2, :] = jnp.broadcast_to(linked[S + 15 : S + 16], (2, E))
    v = (base[...].astype(F32) + ext[0:F, :]).astype(BF16)
    values[...] = v
    for t in range(TILES):
        lo, first, last = t * S, F - t * S, (t + 1) * S
        queries = jnp.concatenate([q0[lo:F, :], q2[0:last, :]], axis=0)
        cots = jnp.concatenate([c0[lo:F, :], c2[0:last, :]], axis=0)
        mask = jnp.concatenate([bias[t, :, 0:first], bias[t, :, first + F : first + F + last]], axis=1)
        rows = partial_stats(k[lo : lo + S, :], v[lo : lo + S], queries, cots, mask)
        for j, empty in enumerate((NEG, 0.0, 0.0)):
            pieces = [jnp.full((1, lo), empty, F32)] if lo else []
            pieces += [rows[j]] + ([jnp.full((1, F - last), empty, F32)] if last < F else [])
            part[t, pl.ds(j * H + head, 1), :] = jnp.concatenate(pieces, axis=1)

    @on_last(sub)
    def _():
        for out, cols in ((s0, slice(0, F)), (s2, slice(F, 2 * F))):
            merge_into(out, part, cols)


def partial_stats(k, v, queries, cots, mask):
    scores = dot_nt(k, queries) * LOG2 + mask
    peak = jnp.max(scores, axis=0, keepdims=True)
    expo = jnp.exp2(scores - peak)
    dots = dot_nt(v, cots)
    return peak, jnp.sum(expo, axis=0, keepdims=True), jnp.sum(expo * dots, axis=0, keepdims=True)


def merge_into(out, part, cols):
    merged = merge([tuple(part[t, j * H : (j + 1) * H, cols] for j in range(3)) for t in range(TILES)])
    for j in range(3):
        out[j * H : (j + 1) * H, :] = merged[j]


def stats_next_body(sub, head, flag, k, v, q1a, q1b, c1, d0, d1, s1, bias, part):
    @on_first(sub)
    def _():
        full_mask(bias, [doc_row(ref) for ref in (d0, d1, d1)])

    queries = pick(flag, q1a, q1b, F)
    for t in range(TILES):
        lo = t * S
        mask = bias[t, :, F - lo : 2 * F - lo]
        rows = partial_stats(k[lo : lo + S, :], v[lo : lo + S, :], queries, c1[0:F, :], mask)
        for j in range(3):
            part[t, pl.ds(j * H + head, 1), :] = rows[j]

    @on_last(sub)
    def _():
        merge_into(s1, part, slice(0, F))


def merge(parts):
    peak = parts[0][0]
    for part in parts[1:]:
        peak = jnp.maximum(peak, part[0])
    total, dots = 0.0, 0.0
    for part in parts:
        factor = jnp.exp2(part[0] - peak)
        total = total + part[1] * factor
        dots = dots + part[2] * factor
    return peak, total, dots


def full_stats(k, base, mid, w, q0, q2, c0, c2):
    stat = jax.ShapeDtypeStruct((3 * H, F), F32)
    return call(
        stats_body,
        "full_stats",
        2_000_000_000,
        8_000_000,
        in_specs=[head_spec(F), head_spec(F), whole_spec((S + 16, WIDTH)), head_spec(WIDTH)]
        + [head_spec(F)] * 4
        + [DOCS] * 2,
        out_specs=[head_spec(F)] + [whole_spec((3 * H, F))] * 2,
        out_shape=[jax.ShapeDtypeStruct((F, WIDTH), BF16), stat, stat],
        scratch_shapes=[
            pltpu.VMEM((TILES, S, TILE_W), F32),
            pltpu.VMEM((400, E), F32),
            pltpu.VMEM((TILES, 3 * H, 2 * F), F32),
        ],
    )(k, base, mid, w, q0, q2, c0, c2, c0, c2)


def next_stats(flag, k, v, q1a, q1b, c0, c1):
    return call(
        stats_next_body,
        "next_stats",
        1_000_000_000,
        6_000_000,
        in_specs=[FLAG] + [head_spec(F)] * 5 + [DOCS] * 2,
        out_specs=[whole_spec((3 * H, F))],
        out_shape=[jax.ShapeDtypeStruct((3 * H, F), F32)],
        scratch_shapes=[
            pltpu.VMEM((TILES, S, TILE_W), F32),
            pltpu.VMEM((TILES, 3 * H, F), F32),
        ],
    )(flag, k, v, q1a, q1b, c1, c0, c1)[0]


def grads_body(
    sub, head, flag, k, v, q0, q1a, q1b, q2, c0, c1, c2, d0, d1, d2, s0, s1, s2, up1, up2, down1, down2,
    dk, dv, dq0, dq1, dq2, sums, link, tail, bias, ext, glob, kept,
):
    @on_first(sub)
    def _():
        full_mask(bias, [doc_row(ref) for ref in (d0, d1, d2)])

        def triple(ref, base=0):
            peak, total, dots = (ref[base + j * H : base + (j + 1) * H, :] for j in range(3))
            return jnp.where(total > 0.0, peak, NEG), total, dots

        groups = (
            (triple(s0), triple(up1), triple(up2)),
            (triple(s1), triple(up1, 3 * H), triple(down1)),
            (triple(s2), triple(down1, 3 * H), triple(down2)),
        )
        for n, group in enumerate(groups):
            cols = slice(n * F, (n + 1) * F)
            peak, total, dots = merge(group)
            inv = jnp.where(total > 0.0, 1.0 / total, 0.0)
            glob[0:H, cols] = peak
            glob[H : 2 * H, cols] = inv
            glob[2 * H : 3 * H, cols] = dots * inv
        kept[...] = jnp.zeros((F, SPAN_F), BF16)
        ext[F:400, :] = jnp.zeros((400 - F, E), F32)

    queries = jnp.concatenate([q0[...], pick(flag, q1a, q1b, F), q2[...]], axis=0)
    cots = jnp.concatenate([c0[0:F, :], c1[0:F, :], c2[0:F, :]], axis=0)
    for t in range(TILES):
        lo = t * S
        cols = slice(lo, lo + TILE_W)
        scores = dot_nt(k[lo : lo + S, :], queries[cols]) * LOG2 + bias[t]
        probs = jnp.exp2(scores - glob[pl.ds(head, 1), cols]) * glob[pl.ds(H + head, 1), cols]
        dots = dot_nt(v[lo : lo + S, :], cots[cols])
        grads = (probs * (dots - glob[pl.ds(2 * H + head, 1), cols])).astype(BF16)
        kept[lo : lo + S, cols] = grads
        dk[lo : lo + S, :] = (dot_nn(grads, queries[cols]) * SCALE).astype(BF16)
        grad_v = dot_nn(probs.astype(BF16), cots[cols]).astype(BF16)
        dv[lo : lo + S, :] = grad_v
        ext[lo : lo + S, :] = grad_v.astype(F32)
    for n, out in enumerate((dq0, dq1, dq2)):
        part = dot_tn(kept[:, n * F : (n + 1) * F], k[...]) * SCALE
        out[...] = part.astype(out.dtype)
    total = ext[pl.ds(2, S, stride=3), :] + ext[pl.ds(3, S, stride=3), :] + ext[pl.ds(4, S, stride=3), :]
    sums[...] = total
    first = ext[0:1, :] + ext[1:2, :]
    tail[...] = jnp.broadcast_to(first, (8, E))
    narrow = total.astype(BF16)
    last = jnp.where(iota((16, E), 0) == 15, first, 0.0).astype(BF16)
    for x in range(4):
        link[x * (S + 16) : x * (S + 16) + S, :] = narrow
        link[x * (S + 16) + S : (x + 1) * (S + 16), :] = last


def full_grads(flag, k, v, qs, cs, stats):
    return call(
        grads_body,
        "full_grads",
        8_000_000_000,
        14_000_000,
        in_specs=[FLAG, head_spec(F), head_spec(F)]
        + [head_spec(F)] * 7
        + [DOCS] * 3
        + [whole_spec(s.shape) for s in stats],
        out_specs=[head_spec(F)] * 5 + [head_spec(S), head_spec(4 * (S + 16)), head_spec(8)],
        out_shape=[
            jax.ShapeDtypeStruct((F, WIDTH), BF16),
            jax.ShapeDtypeStruct((F, WIDTH), BF16),
            jax.ShapeDtypeStruct((F, WIDTH), F32),
            jax.ShapeDtypeStruct((F, WIDTH), BF16),
            jax.ShapeDtypeStruct((F, WIDTH), BF16),
            jax.ShapeDtypeStruct((S, WIDTH), F32),
            jax.ShapeDtypeStruct((4 * (S + 16), WIDTH), BF16),
            jax.ShapeDtypeStruct((8, WIDTH), F32),
        ],
        scratch_shapes=[
            pltpu.VMEM((TILES, S, TILE_W), F32),
            pltpu.VMEM((400, E), F32),
            pltpu.VMEM((3 * H, SPAN_F), F32),
            pltpu.VMEM((F, SPAN_F), BF16),
        ],
    )(flag, k, v, *qs, *cs, *cs, *stats)


def mid_cot_body(sub, head, w, att, stat, sums, tail, out, whole):
    @on_first(sub)
    def _():
        total = sums[...] + jnp.where(iota((S, WIDTH), 0) == S - 1, tail[0:1, :], 0.0)
        whole[...] = total.astype(BF16)

    grad = dot_nt(whole[...], w[...]).astype(BF16)
    out[0:S, :] = grad
    delta = jnp.sum(jnp.transpose(grad.astype(F32) * att[...]), axis=0, keepdims=True)
    rows = [*split3(stat[0:1, :]), *split3(stat[1:2, :]), *split3(delta)]
    rows = [row.astype(F32) for row in rows] + [jnp.zeros((7, E), F32)]
    out[S : S + 16, :] = jnp.concatenate(rows, axis=0).astype(BF16)


def mid_cotangent(sums, tail, w, att, stat):
    body = mid_cot_body

    def run(w_ref, *refs):
        for sub in range(STEP):
            cols = pl.ds(sub * E, E)
            att_ref, stat_ref, sums_ref, tail_ref, out_ref, whole = refs
            body(
                sub, None, w_ref.at[cols, :], att_ref.at[:, cols], stat_ref.at[:, cols],
                sums_ref, tail_ref, out_ref.at[:, cols], whole,
            )

    return pl.pallas_call(
        run,
        grid=(H // STEP,),
        in_specs=[
            pl.BlockSpec((STEP * E, WIDTH), lambda h: (h, 0)),
            head_spec(S),
            head_spec(8),
            whole_spec((S, WIDTH)),
            whole_spec((8, WIDTH)),
        ],
        out_specs=head_spec(S + 16),
        out_shape=jax.ShapeDtypeStruct((S + 16, WIDTH), BF16),
        scratch_shapes=[pltpu.VMEM((S, WIDTH), BF16)],
        compiler_params=pltpu.CompilerParams(vmem_limit_bytes=16 * 1024 * 1024),
        cost_estimate=pl.CostEstimate(flops=600_000_000, bytes_accessed=4_000_000, transcendentals=0),
        name="mid_cotangent",
    )(w, att, stat, sums, tail)


def mid_bwd_body(sub, head, flag, p4, p2, a, b, c, p0, *refs):
    ms = [ref[...] for ref in refs[0:5]]
    gs = refs[5:10]
    dq, dk, dv, back, fore = refs[10:]
    pays = pair_slabs(flag, p4, p2, a, b, c, p0)

    @on_first(sub)
    def _():
        mine = p0[2 * S : 2 * S + 16, :].astype(F32)[0:1]
        column = to_column(mine, S)
        causal = iota((S, S), 1) >= iota((S, S), 0)
        for n, pay in enumerate(pays):
            ok = to_column(pay[2 * S : 2 * S + 16].astype(F32)[0:1], S) == mine
            if n == REACH:
                ok = ok & causal
            back[n * S : (n + 1) * S, :] = jnp.where(ok, 0.0, NEG)
        for n, pay in enumerate(ms):
            ok = column == pay[S : S + 16].astype(F32)[0:1]
            if n == 0:
                ok = ok & causal
            fore[:, n * S : (n + 1) * S] = jnp.where(ok, 0.0, NEG)

    def stats(ref):
        rows = ref[S : S + 16, :].astype(F32)
        return [rows[j : j + 1] + rows[j + 1 : j + 2] + rows[j + 2 : j + 3] for j in (0, 3, 6)]

    k = p0[0:S, :]
    v = p0[S : 2 * S, :]
    keys = jnp.concatenate([pay[0:S] for pay in pays], axis=0)
    values = jnp.concatenate([pay[S : 2 * S] for pay in pays], axis=0)
    peak, inv, delta = stats(gs[0])
    scores = dot_nt(keys, ms[0][0:S]) * LOG2 + back[...]
    probs = jnp.exp2(scores - peak) * inv
    grads = (probs * (dot_nt(values, gs[0][0:S, :]) - delta)).astype(BF16)
    dq[...] = (dot_tn(grads, keys) * SCALE).astype(BF16)
    queries = jnp.concatenate([one[0:S] for one in ms], axis=0)
    cots = jnp.concatenate([ref[0:S, :] for ref in gs], axis=0)
    every = [stats(ref) for ref in gs]
    peak, inv, delta = (jnp.concatenate([one[j] for one in every], axis=1) for j in range(3))
    scores = dot_nt(k, queries) * LOG2 + fore[...]
    probs = jnp.exp2(scores - peak) * inv
    grads = (probs * (dot_nt(v, cots) - delta)).astype(BF16)
    dk[...] = (dot_nn(grads, queries) * SCALE).astype(BF16)
    dv[...] = dot_nn(probs.astype(BF16), cots).astype(BF16)


QUERY_ROWS = pl.BlockSpec((pl.Element(S + 16), pl.Element(STEP * E)), lambda h: (F, h * STEP * E))


def mid_backward(flag, pays, ms, gs):
    return call(
        mid_bwd_body,
        "mid_backward",
        3_000_000_000,
        6_000_000,
        in_specs=[FLAG] + PAY_SPECS + [QUERY_ROWS] * 3 + [head_spec(S + 16)] * 7,
        out_specs=[head_spec(S)] * 3,
        out_shape=[jax.ShapeDtypeStruct((S, WIDTH), BF16)] * 3,
        scratch_shapes=[pltpu.VMEM((SPAN_M, S), F32), pltpu.VMEM((S, SPAN_M), F32)],
    )(flag, *pays, *ms, *gs)


def shift(value, steps):
    count = lax.axis_size("ctx")
    first, last = max(0, -steps), min(count, count - steps)
    return lax.ppermute(value, "ctx", [(n, n + steps) for n in range(first, last)])


def swap(value, axis, bit):
    count = lax.axis_size(axis)
    return lax.ppermute(value, axis, [(n, n ^ bit) for n in range(count)])


def together(*values):
    return lax.optimization_barrier(values)


def block(value, index, rows):
    return lax.dynamic_slice_in_dim(value, index * rows, rows, 0)


X_GROUPS = [[first + 16 * n for n in range(4)] for first in range(16)]
YZ_GROUPS = [[16 * first + n for n in range(16)] for first in range(4)]


def exchange(value, axis, groups):
    return lax.all_to_all(value, axis, 0, 0, axis_index_groups=groups, tiled=True)


def shards(q_mid, k_mid, v_mid, doc_ids, q_full, k_full, v_base, w_link, cotangent):
    place = lax.axis_index("ctx")
    upper = place % 2 == 1
    flag = (place % 2).astype(jnp.int32).reshape(1)
    q_m, q_f, k_f = q_mid[0], q_full[0], k_full[0]
    ids = jnp.broadcast_to(jnp.tile((doc_ids + 1).astype(BF16), (1, 2)), (16, 2 * S))
    own_kv, own_cq, swap_a = pack(flag, q_m, k_mid[0], v_mid[0], ids, q_f, cotangent[0])

    kv2 = shift(own_kv, 2)
    got_a = swap(swap_a, "ctx", 1)
    qf2 = shift(q_f, -2)
    got_b = swap(kv2, "ctx", 1)
    late_cq, qf2, kv2, got_a = together(own_cq, qf2, kv2, got_a)
    kv4, got_b = together(shift(kv2, 2), got_b)
    got_c = swap(jnp.concatenate([jnp.where(upper, kv4, qf2[:KV]), qf2[KV:]], axis=0), "ctx", 1)
    cq2 = shift(late_cq, -2)
    cq2, got_c_late = together(cq2, got_c)
    cq1 = swap(jnp.where(upper, late_cq, cq2), "ctx", 1)

    pays = (kv4, kv2, got_a, got_b, got_c, own_kv)
    mid_ext, attended, mid_stat = mid_forward(flag, q_m, pays)
    qm2 = cq2[F:]
    qm4, mid_ext = together(shift(qm2, -2), mid_ext)
    values, s0, s2 = full_stats(k_f, v_base[0], mid_ext, w_link, q_f, qf2, late_cq, cq2)
    up2, down2 = shift(s2, 2), shift(s0, -2)
    cq1, up2, down2 = together(cq1, up2, down2)
    s1 = next_stats(flag, k_f, values, got_c_late, got_a, late_cq, cq1)
    up1 = shift(jnp.concatenate([s1, s2], axis=0), 1)
    down1 = shift(jnp.concatenate([s0, s1], axis=0), -1)

    qm3 = swap(jnp.where(upper, qm2, qm4), "ctx", 1)
    values, qm3 = together(values, qm3)
    qs, cs = (q_f, got_c_late, got_a, qf2), (late_cq, cq1, cq2)
    dk_f, dv_f, dq0, dq1, dq2, sums, sum_ext, tail = full_grads(
        flag, k_f, values, qs, cs, (s0, s1, s2, up1, up2, down1, down2)
    )

    next_tail = shift(tail, -1)
    cot_m = mid_cotangent(sums, next_tail, w_link, attended, mid_stat)
    cot_m, dq1, mid_ext = together(cot_m, dq1, mid_ext)
    parts = jnp.concatenate([mid_ext[:, n * 256 : (n + 1) * 256] for n in range(4)], axis=0)
    left = exchange(parts, "ctx", X_GROUPS)
    near = swap(dq1, "ctx", 1)
    g2, sum_ext = together(shift(cot_m, -2), sum_ext)
    right = exchange(sum_ext, "ctx", X_GROUPS)
    term = dot_tn(left, right).astype(BF16)
    g1 = swap(jnp.where(upper, cot_m, g2), "ctx", 1)
    term, g4, near = together(term, shift(g2, -2), near)
    total = jnp.sum(exchange(term, "ctx", YZ_GROUPS).astype(F32).reshape(16, 16, WIDTH), axis=0)
    g2_late, g4 = together(g2, g4)
    total, g3 = together(total, swap(jnp.where(upper, g2_late, g4), "ctx", 1))
    every = exchange(jnp.concatenate([total] * 4, axis=0), "dp", None)
    near, every = together(near, every)
    passed = jnp.where(upper, dq2.astype(F32), dq2.astype(F32) + near.astype(F32)).astype(BF16)
    far = shift(passed, 2)
    factor = float(lax.axis_size("dp") * lax.axis_size("ctx") * F) ** (-0.5)
    grad_link = jnp.sum(every.reshape(4, 16, WIDTH), axis=0) * factor
    dq_m, dk_m, dv_m = mid_backward(flag, pays, (late_cq, cq1, cq2, qm3, qm4), (cot_m, g1, g2, g3, g4))

    dq_f = (dq0 + far.astype(F32) + jnp.where(upper, near.astype(F32), 0.0)).astype(BF16)
    return (dq_m[None], dk_m[None], dv_m[None], dq_f[None], dk_f[None], dv_f[None], grad_link)


def solution(mesh):
    rows = P("dp", "ctx", None)
    return jax.shard_map(
        shards,
        mesh=mesh,
        in_specs=(rows, rows, rows, P("dp", "ctx"), rows, rows, rows, P(), rows),
        out_specs=(rows,) * 6 + (P("ctx", None),),
        check_vma=False,
    )
```

```python
import math

import jax
import jax.numpy as jnp
from jax import lax
from jax.experimental import pallas as pl
from jax.experimental.pallas import tpu as pltpu
from jax.sharding import PartitionSpec as P

H = 8
E = 128
S = 128
F = 384
REACH = 4
FREACH = 2
WIDTH = H * E
SPAN_M = (REACH + 1) * S
SPAN_F = (FREACH + 1) * F
WIN = FREACH * F
KV = 2 * S + 32
CQ = F + S + 16
TILES = F // S
TILE_W = WIN + S
STEP = 4
SCALE = E ** (-0.5)
LOG2 = SCALE * math.log2(math.e)
NEG = -1e30
F32 = jnp.float32
BF16 = jnp.bfloat16


def dot_nn(a, b):
    return lax.dot_general(a, b, (((1,), (0,)), ((), ())), preferred_element_type=F32)


def dot_nt(a, b):
    return lax.dot_general(a, b, (((1,), (1,)), ((), ())), preferred_element_type=F32)


def dot_tn(a, b):
    return lax.dot_general(a, b, (((0,), (0,)), ((), ())), preferred_element_type=F32)


def iota(shape, axis):
    return lax.broadcasted_iota(jnp.int32, shape, axis)


def to_column(row, size):
    return jnp.transpose(jnp.broadcast_to(row, (size, size)))


def split3(x):
    hi = x.astype(BF16)
    rest = x - hi.astype(F32)
    mid = rest.astype(BF16)
    return hi, mid, (rest - mid.astype(F32)).astype(BF16)


def head_spec(rows):
    return pl.BlockSpec((rows, STEP * E), lambda h: (0, h))


def by_head(body, in_specs, out_specs):
    split = [spec.block_shape is not None and spec.block_shape[-1] in (STEP * E, pl.Element(STEP * E)) for spec in in_specs + out_specs]

    def run(*refs):
        for sub in range(STEP):
            views = [ref.at[:, pl.ds(sub * E, E)] if cut else ref for ref, cut in zip(refs, split)]
            body(sub, pl.program_id(0) * STEP + sub, *views, *refs[len(split) :])

    return run


def call(body, name, flops, bytes_accessed, in_specs, out_specs, out_shape, scratch_shapes):
    return pl.pallas_call(
        by_head(body, in_specs, out_specs),
        grid=(H // STEP,),
        in_specs=in_specs,
        out_specs=out_specs,
        out_shape=out_shape,
        scratch_shapes=scratch_shapes,
        cost_estimate=pl.CostEstimate(flops=flops, bytes_accessed=bytes_accessed, transcendentals=0),
        name=name,
    )


def on_first(sub):
    return pl.when(pl.program_id(0) == 0) if sub == 0 else lambda build: None


def on_last(sub):
    return pl.when(pl.program_id(0) == H // STEP - 1) if sub == STEP - 1 else lambda build: None


def whole_spec(shape):
    return pl.BlockSpec(shape, lambda h: (0,) * len(shape))


def pack_body(flag, q, k, v, ids, qf, cot, kv, cq, first):
    kv[0:S, :] = k[...]
    kv[S : 2 * S, :] = v[...]
    kv[2 * S : 2 * S + 16, :] = ids[...]
    kv[2 * S + 16 : KV, :] = q[S - 16 : S, :]
    cq[0:F, :] = cot[...]
    cq[F : F + S, :] = q[...]
    cq[F + S : CQ, :] = ids[...]
    first[...] = qf[...]

    @pl.when(flag[0] == 0)
    def _():
        first[0:KV, :] = kv[...]


def pack(flag, q, k, v, ids, qf, cot):
    def wide(rows):
        return pl.BlockSpec((rows, 2 * E), lambda h: (0, h))

    return pl.pallas_call(
        pack_body,
        grid=(H // 2,),
        in_specs=[FLAG] + [wide(S)] * 3 + [whole_spec((16, 2 * E)), wide(F), wide(F)],
        out_specs=[wide(KV), wide(CQ), wide(F)],
        out_shape=[
            jax.ShapeDtypeStruct((KV, WIDTH), BF16),
            jax.ShapeDtypeStruct((CQ, WIDTH), BF16),
            jax.ShapeDtypeStruct((F, WIDTH), BF16),
        ],
        name="pack",
    )(flag, q, k, v, ids, qf, cot)


def pick(flag, upper, lower, rows):
    return jnp.where(flag[0] == 1, upper[0:rows, :], lower[0:rows, :])


def pair_slabs(flag, p4, p2, a, b, c, p0):
    return [p4[...], pick(flag, b, c, KV), p2[...], pick(flag, a, b, KV), p0[...]]


def mid_fwd_body(sub, head, flag, q, p4, p2, a, b, c, p0, out, att, stat, bias):
    pays = pair_slabs(flag, p4, p2, a, b, c, p0)

    @on_first(sub)
    def _():
        def ids(n):
            return pays[n][2 * S : 2 * S + 16].astype(F32)[0:1]

        mine = to_column(ids(REACH), S)
        edge = to_column(ids(REACH - 1), S)[S - 16 : S]
        for n in range(REACH + 1):
            cols = slice(n * S, (n + 1) * S)
            ok = mine == ids(n)
            ok_edge = edge == ids(n)
            if n == REACH:
                ok = ok & (iota((S, S), 0) >= iota((S, S), 1))
                ok_edge = ok_edge & (iota((16, S), 1) < 0)
            if n == REACH - 1:
                ok_edge = ok_edge & (iota((16, S), 0) + (S - 16) >= iota((16, S), 1))
            bias[0:S, cols] = jnp.where(ok, 0.0, NEG)
            bias[S : S + 16, cols] = jnp.where(ok_edge, 0.0, NEG)

    keys = jnp.concatenate([pay[0:S] for pay in pays], axis=0)
    values = jnp.concatenate([pay[S : 2 * S] for pay in pays], axis=0)
    queries = jnp.concatenate([q[...], pays[REACH - 1][2 * S + 16 : KV]], axis=0)
    scores = dot_nt(queries, keys) * LOG2 + bias[...]
    peak = jnp.max(scores, axis=1, keepdims=True)
    expo = jnp.exp2(scores - peak)
    inv = 1.0 / jnp.sum(expo, axis=1, keepdims=True)
    attended = dot_nn((expo * inv).astype(BF16), values)
    att[...] = attended[0:S]
    out[...] = attended.astype(BF16)
    stat[0:1, :] = jnp.transpose(jnp.broadcast_to(peak[0:S], (S, S)))[0:1]
    stat[1:2, :] = jnp.transpose(jnp.broadcast_to(inv[0:S], (S, S)))[0:1]
    stat[2:8, :] = jnp.zeros((6, S), F32)


def mid_forward(flag, q, pays):
    return call(
        mid_fwd_body,
        "mid_forward",
        700_000_000,
        4_000_000,
        in_specs=[FLAG, head_spec(S)] + PAY_SPECS,
        out_specs=[head_spec(S + 16), head_spec(S), head_spec(8)],
        out_shape=[
            jax.ShapeDtypeStruct((S + 16, WIDTH), BF16),
            jax.ShapeDtypeStruct((S, WIDTH), F32),
            jax.ShapeDtypeStruct((8, WIDTH), F32),
        ],
        scratch_shapes=[pltpu.VMEM((S + 16, SPAN_M), F32)],
    )(flag, q, *pays)


FLAG = pl.BlockSpec(memory_space=pltpu.SMEM)
PAY_SPECS = [head_spec(KV)] * 6


def full_mask(bias, docs):
    spread = (iota((S, F), 1) // 3 == iota((S, F), 0)).astype(BF16)
    spread_t = (iota((F, S), 0) // 3 == iota((F, S), 1)).astype(BF16)
    rows = jnp.concatenate(
        [dot_nn(jnp.broadcast_to(d, (16, S)), spread)[0:1] for d in docs], axis=1
    )
    column = dot_nn(spread_t, to_column(docs[0].astype(F32), S).astype(BF16))
    for t in range(TILES):
        lo = t * S
        mine = jnp.concatenate([column[lo : lo + S]] * (TILE_W // S), axis=1)
        gap = iota((S, TILE_W), 1) - iota((S, TILE_W), 0)
        ok = (mine == rows[:, lo : lo + TILE_W]) & (gap >= 0) & (gap < WIN)
        bias[t] = jnp.where(ok, 0.0, NEG)


DOCS = pl.BlockSpec((16, S), lambda h: ((F + S) // 16, 0))


def doc_row(ref):
    return ref[...][0:1]


def stats_body(sub, head, k, base, mid, w, q0, q2, c0, c2, d0, d2, values, s0, s2, bias, ext, part):
    @on_first(sub)
    def _():
        full_mask(bias, [doc_row(ref) for ref in (d0, d0, d2)])

    linked = dot_nn(mid[...], w[...])
    for n in range(2, 5):
        ext[pl.ds(n, S, stride=3), :] = linked[0:S]
    ext[0:2, :] = jnp.broadcast_to(linked[S + 15 : S + 16], (2, E))
    v = (base[...].astype(F32) + ext[0:F, :]).astype(BF16)
    values[...] = v
    for t in range(TILES):
        lo, first, last = t * S, F - t * S, (t + 1) * S
        queries = jnp.concatenate([q0[lo:F, :], q2[0:last, :]], axis=0)
        cots = jnp.concatenate([c0[lo:F, :], c2[0:last, :]], axis=0)
        mask = jnp.concatenate([bias[t, :, 0:first], bias[t, :, first + F : first + F + last]], axis=1)
        rows = partial_stats(k[lo : lo + S, :], v[lo : lo + S], queries, cots, mask)
        for j, empty in enumerate((NEG, 0.0, 0.0)):
            pieces = [jnp.full((1, lo), empty, F32)] if lo else []
            pieces += [rows[j]] + ([jnp.full((1, F - last), empty, F32)] if last < F else [])
            part[t, pl.ds(j * H + head, 1), :] = jnp.concatenate(pieces, axis=1)

    @on_last(sub)
    def _():
        for out, cols in ((s0, slice(0, F)), (s2, slice(F, 2 * F))):
            merge_into(out, part, cols)


def partial_stats(k, v, queries, cots, mask):
    scores = dot_nt(k, queries) * LOG2 + mask
    peak = jnp.max(scores, axis=0, keepdims=True)
    expo = jnp.exp2(scores - peak)
    dots = dot_nt(v, cots)
    return peak, jnp.sum(expo, axis=0, keepdims=True), jnp.sum(expo * dots, axis=0, keepdims=True)


def merge_into(out, part, cols):
    merged = merge([tuple(part[t, j * H : (j + 1) * H, cols] for j in range(3)) for t in range(TILES)])
    for j in range(3):
        out[j * H : (j + 1) * H, :] = merged[j]


def stats_next_body(sub, head, flag, k, v, q1a, q1b, c1, d0, d1, s1, bias, part):
    @on_first(sub)
    def _():
        full_mask(bias, [doc_row(ref) for ref in (d0, d1, d1)])

    queries = pick(flag, q1a, q1b, F)
    for t in range(TILES):
        lo = t * S
        mask = bias[t, :, F - lo : 2 * F - lo]
        rows = partial_stats(k[lo : lo + S, :], v[lo : lo + S, :], queries, c1[0:F, :], mask)
        for j in range(3):
            part[t, pl.ds(j * H + head, 1), :] = rows[j]

    @on_last(sub)
    def _():
        merge_into(s1, part, slice(0, F))


def merge(parts):
    peak = parts[0][0]
    for part in parts[1:]:
        peak = jnp.maximum(peak, part[0])
    total, dots = 0.0, 0.0
    for part in parts:
        factor = jnp.exp2(part[0] - peak)
        total = total + part[1] * factor
        dots = dots + part[2] * factor
    return peak, total, dots


def full_stats(k, base, mid, w, q0, q2, c0, c2):
    stat = jax.ShapeDtypeStruct((3 * H, F), F32)
    return call(
        stats_body,
        "full_stats",
        2_000_000_000,
        8_000_000,
        in_specs=[head_spec(F), head_spec(F), whole_spec((S + 16, WIDTH)), head_spec(WIDTH)]
        + [head_spec(F)] * 4
        + [DOCS] * 2,
        out_specs=[head_spec(F)] + [whole_spec((3 * H, F))] * 2,
        out_shape=[jax.ShapeDtypeStruct((F, WIDTH), BF16), stat, stat],
        scratch_shapes=[
            pltpu.VMEM((TILES, S, TILE_W), F32),
            pltpu.VMEM((400, E), F32),
            pltpu.VMEM((TILES, 3 * H, 2 * F), F32),
        ],
    )(k, base, mid, w, q0, q2, c0, c2, c0, c2)


def next_stats(flag, k, v, q1a, q1b, c0, c1):
    return call(
        stats_next_body,
        "next_stats",
        1_000_000_000,
        6_000_000,
        in_specs=[FLAG] + [head_spec(F)] * 5 + [DOCS] * 2,
        out_specs=[whole_spec((3 * H, F))],
        out_shape=[jax.ShapeDtypeStruct((3 * H, F), F32)],
        scratch_shapes=[
            pltpu.VMEM((TILES, S, TILE_W), F32),
            pltpu.VMEM((TILES, 3 * H, F), F32),
        ],
    )(flag, k, v, q1a, q1b, c1, c0, c1)[0]


def grads_body(
    sub, head, flag, k, v, q0, q1a, q1b, q2, c0, c1, c2, d0, d1, d2, s0, s1, s2, up1, up2, down1, down2,
    dk, dv, dq0, dq1, dq2, sums, link, tail, bias, ext, glob, kept,
):
    @on_first(sub)
    def _():
        full_mask(bias, [doc_row(ref) for ref in (d0, d1, d2)])

        def triple(ref, base=0):
            peak, total, dots = (ref[base + j * H : base + (j + 1) * H, :] for j in range(3))
            return jnp.where(total > 0.0, peak, NEG), total, dots

        groups = (
            (triple(s0), triple(up1), triple(up2)),
            (triple(s1), triple(up1, 3 * H), triple(down1)),
            (triple(s2), triple(down1, 3 * H), triple(down2)),
        )
        for n, group in enumerate(groups):
            cols = slice(n * F, (n + 1) * F)
            peak, total, dots = merge(group)
            inv = jnp.where(total > 0.0, 1.0 / total, 0.0)
            glob[0:H, cols] = peak
            glob[H : 2 * H, cols] = inv
            glob[2 * H : 3 * H, cols] = dots * inv
        kept[...] = jnp.zeros((F, SPAN_F), BF16)
        ext[F:400, :] = jnp.zeros((400 - F, E), F32)

    queries = jnp.concatenate([q0[...], pick(flag, q1a, q1b, F), q2[...]], axis=0)
    cots = jnp.concatenate([c0[0:F, :], c1[0:F, :], c2[0:F, :]], axis=0)
    for t in range(TILES):
        lo = t * S
        cols = slice(lo, lo + TILE_W)
        scores = dot_nt(k[lo : lo + S, :], queries[cols]) * LOG2 + bias[t]
        probs = jnp.exp2(scores - glob[pl.ds(head, 1), cols]) * glob[pl.ds(H + head, 1), cols]
        dots = dot_nt(v[lo : lo + S, :], cots[cols])
        grads = (probs * (dots - glob[pl.ds(2 * H + head, 1), cols])).astype(BF16)
        kept[lo : lo + S, cols] = grads
        dk[lo : lo + S, :] = (dot_nn(grads, queries[cols]) * SCALE).astype(BF16)
        grad_v = dot_nn(probs.astype(BF16), cots[cols]).astype(BF16)
        dv[lo : lo + S, :] = grad_v
        ext[lo : lo + S, :] = grad_v.astype(F32)
    for n, out in enumerate((dq0, dq1, dq2)):
        part = dot_tn(kept[:, n * F : (n + 1) * F], k[...]) * SCALE
        out[...] = part.astype(out.dtype)
    total = ext[pl.ds(2, S, stride=3), :] + ext[pl.ds(3, S, stride=3), :] + ext[pl.ds(4, S, stride=3), :]
    sums[...] = total
    first = ext[0:1, :] + ext[1:2, :]
    tail[...] = jnp.broadcast_to(first, (8, E))
    narrow = total.astype(BF16)
    last = jnp.where(iota((16, E), 0) == 15, first, 0.0).astype(BF16)
    for x in range(4):
        link[x * (S + 16) : x * (S + 16) + S, :] = narrow
        link[x * (S + 16) + S : (x + 1) * (S + 16), :] = last


def full_grads(flag, k, v, qs, cs, stats):
    return call(
        grads_body,
        "full_grads",
        8_000_000_000,
        14_000_000,
        in_specs=[FLAG, head_spec(F), head_spec(F)]
        + [head_spec(F)] * 7
        + [DOCS] * 3
        + [whole_spec(s.shape) for s in stats],
        out_specs=[head_spec(F)] * 5 + [head_spec(S), head_spec(4 * (S + 16)), head_spec(8)],
        out_shape=[
            jax.ShapeDtypeStruct((F, WIDTH), BF16),
            jax.ShapeDtypeStruct((F, WIDTH), BF16),
            jax.ShapeDtypeStruct((F, WIDTH), F32),
            jax.ShapeDtypeStruct((F, WIDTH), BF16),
            jax.ShapeDtypeStruct((F, WIDTH), BF16),
            jax.ShapeDtypeStruct((S, WIDTH), F32),
            jax.ShapeDtypeStruct((4 * (S + 16), WIDTH), BF16),
            jax.ShapeDtypeStruct((8, WIDTH), F32),
        ],
        scratch_shapes=[
            pltpu.VMEM((TILES, S, TILE_W), F32),
            pltpu.VMEM((400, E), F32),
            pltpu.VMEM((3 * H, SPAN_F), F32),
            pltpu.VMEM((F, SPAN_F), BF16),
        ],
    )(flag, k, v, *qs, *cs, *cs, *stats)


def mid_cot_body(sub, head, w, att, stat, sums, tail, out, whole):
    @on_first(sub)
    def _():
        total = sums[...] + jnp.where(iota((S, WIDTH), 0) == S - 1, tail[0:1, :], 0.0)
        whole[...] = total.astype(BF16)

    grad = dot_nt(whole[...], w[...]).astype(BF16)
    out[0:S, :] = grad
    delta = jnp.sum(jnp.transpose(grad.astype(F32) * att[...]), axis=0, keepdims=True)
    rows = [*split3(stat[0:1, :]), *split3(stat[1:2, :]), *split3(delta)]
    rows = [row.astype(F32) for row in rows] + [jnp.zeros((7, E), F32)]
    out[S : S + 16, :] = jnp.concatenate(rows, axis=0).astype(BF16)


def mid_cotangent(sums, tail, w, att, stat):
    body = mid_cot_body

    def run(w_ref, *refs):
        for sub in range(STEP):
            cols = pl.ds(sub * E, E)
            att_ref, stat_ref, sums_ref, tail_ref, out_ref, whole = refs
            body(
                sub, None, w_ref.at[cols, :], att_ref.at[:, cols], stat_ref.at[:, cols],
                sums_ref, tail_ref, out_ref.at[:, cols], whole,
            )

    return pl.pallas_call(
        run,
        grid=(H // STEP,),
        in_specs=[
            pl.BlockSpec((STEP * E, WIDTH), lambda h: (h, 0)),
            head_spec(S),
            head_spec(8),
            whole_spec((S, WIDTH)),
            whole_spec((8, WIDTH)),
        ],
        out_specs=head_spec(S + 16),
        out_shape=jax.ShapeDtypeStruct((S + 16, WIDTH), BF16),
        scratch_shapes=[pltpu.VMEM((S, WIDTH), BF16)],
        compiler_params=pltpu.CompilerParams(vmem_limit_bytes=16 * 1024 * 1024),
        cost_estimate=pl.CostEstimate(flops=600_000_000, bytes_accessed=4_000_000, transcendentals=0),
        name="mid_cotangent",
    )(w, att, stat, sums, tail)


def mid_bwd_body(sub, head, flag, p4, p2, a, b, c, p0, *refs):
    ms = [ref[...] for ref in refs[0:5]]
    gs = refs[5:10]
    dq, dk, dv, back, fore = refs[10:]
    pays = pair_slabs(flag, p4, p2, a, b, c, p0)

    @on_first(sub)
    def _():
        mine = p0[2 * S : 2 * S + 16, :].astype(F32)[0:1]
        column = to_column(mine, S)
        causal = iota((S, S), 1) >= iota((S, S), 0)
        for n, pay in enumerate(pays):
            ok = to_column(pay[2 * S : 2 * S + 16].astype(F32)[0:1], S) == mine
            if n == REACH:
                ok = ok & causal
            back[n * S : (n + 1) * S, :] = jnp.where(ok, 0.0, NEG)
        for n, pay in enumerate(ms):
            ok = column == pay[S : S + 16].astype(F32)[0:1]
            if n == 0:
                ok = ok & causal
            fore[:, n * S : (n + 1) * S] = jnp.where(ok, 0.0, NEG)

    def stats(ref):
        rows = ref[S : S + 16, :].astype(F32)
        return [rows[j : j + 1] + rows[j + 1 : j + 2] + rows[j + 2 : j + 3] for j in (0, 3, 6)]

    k = p0[0:S, :]
    v = p0[S : 2 * S, :]
    keys = jnp.concatenate([pay[0:S] for pay in pays], axis=0)
    values = jnp.concatenate([pay[S : 2 * S] for pay in pays], axis=0)
    peak, inv, delta = stats(gs[0])
    scores = dot_nt(keys, ms[0][0:S]) * LOG2 + back[...]
    probs = jnp.exp2(scores - peak) * inv
    grads = (probs * (dot_nt(values, gs[0][0:S, :]) - delta)).astype(BF16)
    dq[...] = (dot_tn(grads, keys) * SCALE).astype(BF16)
    queries = jnp.concatenate([one[0:S] for one in ms], axis=0)
    cots = jnp.concatenate([ref[0:S, :] for ref in gs], axis=0)
    every = [stats(ref) for ref in gs]
    peak, inv, delta = (jnp.concatenate([one[j] for one in every], axis=1) for j in range(3))
    scores = dot_nt(k, queries) * LOG2 + fore[...]
    probs = jnp.exp2(scores - peak) * inv
    grads = (probs * (dot_nt(v, cots) - delta)).astype(BF16)
    dk[...] = (dot_nn(grads, queries) * SCALE).astype(BF16)
    dv[...] = dot_nn(probs.astype(BF16), cots).astype(BF16)


QUERY_ROWS = pl.BlockSpec((pl.Element(S + 16), pl.Element(STEP * E)), lambda h: (F, h * STEP * E))


def mid_backward(flag, pays, ms, gs):
    return call(
        mid_bwd_body,
        "mid_backward",
        3_000_000_000,
        6_000_000,
        in_specs=[FLAG] + PAY_SPECS + [QUERY_ROWS] * 3 + [head_spec(S + 16)] * 7,
        out_specs=[head_spec(S)] * 3,
        out_shape=[jax.ShapeDtypeStruct((S, WIDTH), BF16)] * 3,
        scratch_shapes=[pltpu.VMEM((SPAN_M, S), F32), pltpu.VMEM((S, SPAN_M), F32)],
    )(flag, *pays, *ms, *gs)


def shift(value, steps):
    count = lax.axis_size("ctx")
    first, last = max(0, -steps), min(count, count - steps)
    return lax.ppermute(value, "ctx", [(n, n + steps) for n in range(first, last)])


def swap(value, axis, bit):
    count = lax.axis_size(axis)
    return lax.ppermute(value, axis, [(n, n ^ bit) for n in range(count)])


def together(*values):
    return lax.optimization_barrier(values)


def block(value, index, rows):
    return lax.dynamic_slice_in_dim(value, index * rows, rows, 0)


X_GROUPS = [[first + 16 * n for n in range(4)] for first in range(16)]
YZ_GROUPS = [[16 * first + n for n in range(16)] for first in range(4)]


def exchange(value, axis, groups):
    return lax.all_to_all(value, axis, 0, 0, axis_index_groups=groups, tiled=True)


def shards(q_mid, k_mid, v_mid, doc_ids, q_full, k_full, v_base, w_link, cotangent):
    place = lax.axis_index("ctx")
    upper = place % 2 == 1
    flag = (place % 2).astype(jnp.int32).reshape(1)
    q_m, q_f, k_f = q_mid[0], q_full[0], k_full[0]
    ids = jnp.broadcast_to(jnp.tile((doc_ids + 1).astype(BF16), (1, 2)), (16, 2 * S))
    own_kv, own_cq, swap_a = pack(flag, q_m, k_mid[0], v_mid[0], ids, q_f, cotangent[0])

    kv2 = shift(own_kv, 2)
    got_a = swap(swap_a, "ctx", 1)
    qf2 = shift(q_f, -2)
    got_b = swap(kv2, "ctx", 1)
    late_cq, qf2, kv2, got_a = together(own_cq, qf2, kv2, got_a)
    kv4, got_b = together(shift(kv2, 2), got_b)
    got_c = swap(jnp.concatenate([jnp.where(upper, kv4, qf2[:KV]), qf2[KV:]], axis=0), "ctx", 1)
    cq2 = shift(late_cq, -2)
    cq2, got_c_late = together(cq2, got_c)
    cq1 = swap(jnp.where(upper, late_cq, cq2), "ctx", 1)

    pays = (kv4, kv2, got_a, got_b, got_c, own_kv)
    mid_ext, attended, mid_stat = mid_forward(flag, q_m, pays)
    parts = jnp.concatenate([mid_ext[:, n * 256 : (n + 1) * 256] for n in range(4)], axis=0)
    left = exchange(parts, "ctx", X_GROUPS)
    qm2 = cq2[F:]
    qm4, mid_ext = together(shift(qm2, -2), mid_ext)
    values, s0, s2 = full_stats(k_f, v_base[0], mid_ext, w_link, q_f, qf2, late_cq, cq2)
    up2, down2 = shift(s2, 2), shift(s0, -2)
    left, cq1, up2, down2 = together(left, cq1, up2, down2)
    s1 = next_stats(flag, k_f, values, got_c_late, got_a, late_cq, cq1)
    up1 = shift(jnp.concatenate([s1, s2], axis=0), 1)
    down1 = shift(jnp.concatenate([s0, s1], axis=0), -1)

    qm3 = swap(jnp.where(upper, qm2, qm4), "ctx", 1)
    values, qm3 = together(values, qm3)
    qs, cs = (q_f, got_c_late, got_a, qf2), (late_cq, cq1, cq2)
    dk_f, dv_f, dq0, dq1, dq2, sums, sum_ext, tail = full_grads(
        flag, k_f, values, qs, cs, (s0, s1, s2, up1, up2, down1, down2)
    )

    next_tail = shift(tail, -1)
    cot_m = mid_cotangent(sums, next_tail, w_link, attended, mid_stat)
    cot_m, dq1 = together(cot_m, dq1)
    near = swap(dq1, "ctx", 1)
    g2, sum_ext = together(shift(cot_m, -2), sum_ext)
    right = exchange(sum_ext, "ctx", X_GROUPS)
    term = dot_tn(left, right).astype(BF16)
    g1 = swap(jnp.where(upper, cot_m, g2), "ctx", 1)
    term, g4, near = together(term, shift(g2, -2), near)
    total = jnp.sum(exchange(term, "ctx", YZ_GROUPS).astype(F32).reshape(16, 16, WIDTH), axis=0)
    near, total = together(near, total)
    passed = jnp.where(upper, dq2.astype(F32), dq2.astype(F32) + near.astype(F32)).astype(BF16)
    far = shift(passed, 2)
    g2_late, g4 = together(g2, g4)
    g3 = swap(jnp.where(upper, g2_late, g4), "ctx", 1)
    dq_m, dk_m, dv_m = mid_backward(flag, pays, (late_cq, cq1, cq2, qm3, qm4), (cot_m, g1, g2, g3, g4))
    dq_m, total = together(dq_m, total)
    every = exchange(jnp.concatenate([total] * 4, axis=0), "dp", None)
    factor = float(lax.axis_size("dp") * lax.axis_size("ctx") * F) ** (-0.5)
    grad_link = jnp.sum(every.reshape(4, 16, WIDTH), axis=0) * factor

    dq_f = (dq0 + far.astype(F32) + jnp.where(upper, near.astype(F32), 0.0)).astype(BF16)
    return (dq_m[None], dk_m[None], dv_m[None], dq_f[None], dk_f[None], dv_f[None], grad_link)


def solution(mesh):
    rows = P("dp", "ctx", None)
    return jax.shard_map(
        shards,
        mesh=mesh,
        in_specs=(rows, rows, rows, P("dp", "ctx"), rows, rows, rows, P(), rows),
        out_specs=(rows,) * 6 + (P("ctx", None),),
        check_vma=False,
    )
```
